32 devices in a mesh: dp: 8 (over z, y), mp: 4 (over x, core).
Axes of the slice: x: 2, y: 2, z: 4, core: 2. Of those that a mesh axis runs over, the one named last changes fastest.
Arguments:
- patches: bfloat16 [32, 256, 768], P('dp'), may hold values from -20 to 20
- segment_ids: int32 [32, 256], P('dp'), may hold values from 0 to 1, never falling along the last dimension, each value on 1 to 196 neighbouring positions
- mask_slots: int32 [32, 64], P('dp'), may hold values from 0 to 255
- gain_attn: bfloat16 [768], replicated, may hold values from 0.099609375 to 1.8984375
- qkv_weight: bfloat16 [3, 768, 768], P(None, None, 'mp'), may hold values from -0.21875 to 0.21875
- out_weight: bfloat16 [768, 768], P('mp'), may hold values from -2 to 2
- gain_mlp: bfloat16 [768], replicated, may hold values from 0.099609375 to 1.8984375
- up_weight: bfloat16 [768, 3072], P(None, 'mp'), may hold values from -0.21875 to 0.21875
- down_weight: bfloat16 [3072, 768], P('mp'), may hold values from -0.109375 to 0.109375
- embed_weight: bfloat16 [768, 384], P(None, 'mp'), may hold values from -0.21875 to 0.21875
- mask_token: bfloat16 [384], replicated, may hold values from -4 to 4
- pred_gain_attn: bfloat16 [384], replicated, may hold values from 0.099609375 to 1.8984375
- pred_qkv: bfloat16 [3, 384, 384], P(None, None, 'mp'), may hold values from -0.3125 to 0.3125
- pred_out: bfloat16 [384, 384], P('mp'), may hold values from -3 to 3
- pred_gain_mlp: bfloat16 [384], replicated, may hold values from 0.099609375 to 1.8984375
- pred_up: bfloat16 [384, 1536], P(None, 'mp'), may hold values from -0.3125 to 0.3125
- pred_down: bfloat16 [1536, 384], P('mp'), may hold values from -0.15625 to 0.15625
- cotangent: bfloat16 [32, 256, 384], P('dp'), may hold values from -6 to 6
Outputs:
- predictions: bfloat16 [32, 256, 384], P('dp')
- patches_grad: bfloat16 [32, 256, 768], P('dp')
- variance: float32 [384], P('mp')
- grad_gain_attn: float32 [768], P('dp')
- grad_qkv: float32 [3, 768, 768], P(None, 'dp', 'mp')
- grad_out: float32 [768, 768], P('mp', 'dp')
- grad_gain_mlp: float32 [768], P('dp')
- grad_up: float32 [768, 3072], P('dp', 'mp')
- grad_down: float32 [3072, 768], P('mp', 'dp')
- grad_embed: float32 [768, 384], P('dp', 'mp')
- grad_mask_token: float32 [384], P('dp')
- grad_pred_gain_attn: float32 [384], P('dp')
- grad_pred_qkv: float32 [3, 384, 384], P(None, 'dp', 'mp')
- grad_pred_out: float32 [384, 384], P('mp', 'dp')
- grad_pred_gain_mlp: float32 [384], P('dp')
- grad_pred_up: float32 [384, 1536], P('dp', 'mp')
- grad_pred_down: float32 [1536, 384], P('mp', 'dp')
The draws below stay inside these ranges and needn't reach their ends.
Inputs may be any that keep to these rules, and one draw needn't show every extreme that they name: `segment_ids`: each row holds image 0 then image 1, each of 60 to 196 tokens. `mask_slots`: positions within the row that take the mask token; a position may repeat.
All inputs are finite; a program needn't handle non-finite values.
Results may differ from the reference program's by a relative error of at most 0.03.
Values may be sent and summed in bfloat16 or wider, within the bound.
No kernel may reach another device: no remote copies, remote signals or barrier semaphores. Data moves between devices by JAX's collectives and lax.ppermute only.
A program may use at most 128 MiB of HBM per device.

```python
import math
import jax
import jax.numpy as jnp
import numpy as np
from jax import lax

D = 768
HEADS = 12
F = 3072
PD = 384
P_HEADS = 12
PF = 1536
SEQ_LEN = 256
IMAGE_TOKENS = 196
MASK_SLOTS = 64
SEQ_DEV = 4
SEQS = 32


def draw_patches(key, part):
    key = jax.random.fold_in(key, 7)
    base_key, pick_key = jax.random.split(key)
    frac = jnp.arange(SEQS).astype(jnp.float32) / max(SEQS - 1, 1)
    chosen = jax.random.randint(pick_key, (), 0, SEQS // SEQ_DEV)
    owner = jnp.arange(SEQS).astype(jnp.int32) // SEQ_DEV
    heavy = jnp.where(owner == chosen, 4.0, 1.0)
    base = jnp.clip(jax.random.normal(base_key, (SEQS, SEQ_LEN, D), jnp.float32), -4.0, 4.0)
    scale = (0.6 + 0.6 * frac) * heavy
    return (base * scale[:, None, None]).astype(jnp.bfloat16)


def plant(values, stream_key, least, high):
    shape = values.shape
    spot = [jax.random.randint(jax.random.fold_in(stream_key, axis), (), 0, shape[axis]) for axis in range(len(shape))]
    values = values.at[tuple(spot)].set(least)
    longest = shape.index(max(shape))
    spot[longest] = (spot[longest] + 1) % shape[longest]
    return values.at[tuple(spot)].set(high)


def block_scale(key, shape, shards, low, high):
    factor_of, own = 1.0, jax.random.fold_in(key, 6)
    for axis_at, shards_of in shards:
        steps = jnp.exp(jax.random.uniform(jax.random.fold_in(own, axis_at), (shards_of,), jnp.float32, low / len(shards), high / len(shards)))
        factor_of = factor_of * jnp.repeat(steps, shape[axis_at] // shards_of).reshape([-1 if axis == axis_at else 1 for axis in range(len(shape))])
    return factor_of


def split_up(amount, total, bound, skew):
    weights = [(1 << 20) // math.isqrt(rank ** skew) + 1 for rank in range(2, amount + 1)]
    surplus, counts = total - bound - (amount - 1), [1] * (amount - 1)
    while surplus > 0:
        candidates = [i for i in range(amount - 1) if counts[i] < bound]
        mass, budget = sum([weights[i] for i in candidates]), surplus
        for i in candidates:
            more = min(bound - counts[i], max(1, budget * weights[i] // mass), surplus)
            counts[i] = counts[i] + more
            surplus = surplus - more
    return np.array([bound] + counts)


def ragged_sizes(own_key, number_of, total, bound, slope):
    if number_of == 2:
        one = jax.random.randint(own_key, (), max(1, total - bound), min(bound, total - 1) + 1)
        return jnp.stack([one, total - one])
    sizes = jnp.asarray(split_up(number_of, total, bound, slope), jnp.int32)
    pairs = (number_of - 1) // 2
    giver, taker = sizes[1:1 + 2 * pairs:2], sizes[2:2 + 2 * pairs:2]
    margin = jnp.minimum(giver - 1, bound - taker)
    shifted = jax.random.randint(jax.random.fold_in(own_key, 1), (pairs,), 0, 1 << 20) % (margin + 1)
    sizes = sizes.at[1:1 + 2 * pairs:2].set(giver - shifted).at[2:2 + 2 * pairs:2].set(taker + shifted)
    return sizes[jax.random.permutation(jax.random.fold_in(own_key, 2), number_of)]


def normal_values(rng, shape, deviation, bound, cuts=(), kind=jnp.bfloat16):
    result = jax.random.normal(rng, shape, jnp.float32) * deviation
    if len(cuts) > 0:
        result = block_scale(rng, shape, cuts, -0.22, 0.18) * result
    return jnp.clip(result, min=-bound, max=bound).astype(kind)


def setup_inputs(seed: int = 0) -> dict:
    arg_keys = jax.random.split(jax.random.key(seed), 19)
    return {
        "patches": draw_patches(jax.random.fold_in(arg_keys[18], 71), 0),
        "segment_ids": jax.vmap(lambda own: jnp.searchsorted(jnp.cumsum(ragged_sizes(own, 2, SEQ_LEN, IMAGE_TOKENS, 0)), jnp.arange(SEQ_LEN), side="right"))(jax.random.split(arg_keys[1], SEQS)).reshape((SEQS, SEQ_LEN)).astype(jnp.int32),
        "mask_slots": plant(jax.random.randint(arg_keys[2], (SEQS, MASK_SLOTS), 0, SEQ_LEN), jax.random.fold_in(arg_keys[2], 1), 0, SEQ_LEN - 1).astype(jnp.int32),
        "gain_attn": jnp.clip(1.0 + 0.18 * jax.random.normal(arg_keys[3], (D,), jnp.float32), 0.099609375, 1.8984375).astype(jnp.bfloat16),
        "qkv_weight": normal_values(arg_keys[4], (3, D, D), D ** -0.5, 0.21875, ((2, 4),)),
        "out_weight": normal_values(arg_keys[5], (D, D), (max(1, D // 96)) ** -0.5, 2.0, ((0, 4),)),
        "gain_mlp": jnp.clip(1.0 + 0.18 * jax.random.normal(arg_keys[6], (D,), jnp.float32), 0.099609375, 1.8984375).astype(jnp.bfloat16),
        "up_weight": normal_values(arg_keys[7], (D, F), D ** -0.5, 0.21875, ((1, 4),)),
        "down_weight": normal_values(arg_keys[8], (F, D), F ** -0.5, 0.109375, ((0, 4),)),
        "embed_weight": normal_values(arg_keys[9], (D, PD), D ** -0.5, 0.21875, ((1, 4),)),
        "mask_token": normal_values(arg_keys[10], (PD,), 1.0, 4.0),
        "pred_gain_attn": jnp.clip(1.0 + 0.18 * jax.random.normal(arg_keys[11], (PD,), jnp.float32), 0.099609375, 1.8984375).astype(jnp.bfloat16),
        "pred_qkv": normal_values(arg_keys[12], (3, PD, PD), PD ** -0.5, 0.3125, ((2, 4),)),
        "pred_out": normal_values(arg_keys[13], (PD, PD), (max(1, PD // 96)) ** -0.5, 3.0, ((0, 4),)),
        "pred_gain_mlp": jnp.clip(1.0 + 0.18 * jax.random.normal(arg_keys[14], (PD,), jnp.float32), 0.099609375, 1.8984375).astype(jnp.bfloat16),
        "pred_up": normal_values(arg_keys[15], (PD, PF), PD ** -0.5, 0.3125, ((1, 4),)),
        "pred_down": normal_values(arg_keys[16], (PF, PD), PF ** -0.5, 0.15625, ((0, 4),)),
        "cotangent": normal_values(arg_keys[17], (SEQS, SEQ_LEN, PD), 1.0, 6.0, ((0, 8),)),
    }


EPS = 1e-06

@jax.custom_vjp
def low(v):
    return lax.optimization_barrier(v.astype(jnp.bfloat16)).astype(jnp.float32)

@jax.custom_vjp
def low_back(v):
    return v

def low_keep(v):
    return (low(v), None)

def low_pass(kept, grad):
    return (grad,)

def back_keep(v):
    return (v, None)

def back_low(kept, grad):
    return (low(grad),)
low.defvjp(low_keep, low_pass)
low_back.defvjp(back_keep, back_low)

def layer_norm(value, gain):
    mean = lax.optimization_barrier(jnp.mean(value, -1, keepdims=True))
    centred = value - mean
    spread = lax.optimization_barrier(jnp.mean(centred * centred, -1, keepdims=True))
    return centred * lax.rsqrt(spread + EPS) * gain

def matmul(left, right):
    return jnp.einsum('...d,de->...e', left, right, precision=lax.Precision.HIGHEST)

def attention(normed, w_qkv, w_out, same, heads):
    shape = normed.shape[:2] + (heads, -1)
    query = low(low_back(matmul(normed, w_qkv[0]))).reshape(shape)
    keys = low(low_back(matmul(normed, w_qkv[1]))).reshape(shape)
    values = low(low_back(matmul(normed, w_qkv[2]))).reshape(shape)
    scale = query.shape[-1] ** (-0.5)
    scores = jnp.einsum('bqhd,bkhd->bhqk', query, keys, precision=lax.Precision.HIGHEST) * scale
    scores = low_back(scores)
    scores = jnp.where(same[:, None], scores, -1000000000.0)
    top = lax.optimization_barrier(jnp.max(scores, -1, keepdims=True))
    expd = jnp.exp(scores - top)
    probs = low(expd / lax.optimization_barrier(jnp.sum(expd, -1, keepdims=True)))
    mixed = jnp.einsum('bhqk,bkhd->bqhd', probs, values, precision=lax.Precision.HIGHEST)
    mixed = low(low_back(mixed.reshape(normed.shape[:2] + (-1,))))
    return low_back(matmul(mixed, w_out))

def block(value, gain_one, w_qkv, w_out, gain_two, w_up, w_down, same, heads):
    normed = low(layer_norm(value, gain_one))
    middle = value + attention(normed, w_qkv, w_out, same, heads)
    second = low(layer_norm(middle, gain_two))
    before = low_back(matmul(second, w_up))
    hidden = low(jax.nn.gelu(before, approximate=False))
    return middle + low_back(matmul(hidden, w_down))

def forward(params, value, segments, slots):
    same = segments[:, :, None] == segments[:, None, :]
    encoded = block(value, params[0], params[1], params[2], params[3], params[4], params[5], same, HEADS)
    embedded = low_back(matmul(low(encoded), params[6]))
    positions = jnp.arange(SEQ_LEN).astype(jnp.int32)
    masked = jnp.any(positions[None, :, None] == slots[:, None, :], -1)
    start = jnp.where(masked[..., None], params[7], embedded)
    return block(start, params[8], params[9], params[10], params[11], params[12], params[13], same, P_HEADS)

def reference(patches, segment_ids, mask_slots, gain_attn, qkv_weight, out_weight, gain_mlp, up_weight, down_weight, embed_weight, mask_token, pred_gain_attn, pred_qkv, pred_out, pred_gain_mlp, pred_up, pred_down, cotangent):
    params = tuple((item.astype(jnp.float32) for item in (gain_attn, qkv_weight, out_weight, gain_mlp, up_weight, down_weight, embed_weight, mask_token, pred_gain_attn, pred_qkv, pred_out, pred_gain_mlp, pred_up, pred_down)))
    group = math.gcd(SEQS, 16)
    blocks = SEQS // group

    def split(array):
        return array.reshape((blocks, group) + array.shape[1:])

    def step(carry, item):
        grads, first, squares = carry
        value, segments, slots, incoming = item
        pred, pullback = jax.vjp(lambda weights, inputs: forward(weights, inputs, segments, slots), params, value.astype(jnp.float32))
        d_params, d_value = pullback(incoming.astype(jnp.float32))
        grads = jax.tree.map(jnp.add, grads, d_params)
        first = first + lax.optimization_barrier(jnp.sum(pred, (0, 1)))
        squares = squares + lax.optimization_barrier(jnp.sum(pred * pred, (0, 1)))
        return ((grads, first, squares), (pred.astype(jnp.bfloat16), d_value.astype(jnp.bfloat16)))
    start = (jax.tree.map(jnp.zeros_like, params), jnp.zeros((PD,), jnp.float32), jnp.zeros((PD,), jnp.float32))
    (grads, first, squares), (preds, d_inputs) = lax.scan(step, start, (split(patches), split(segment_ids), split(mask_slots), split(cotangent)))
    count = SEQS * SEQ_LEN
    mean = first / count
    variance = squares / count - mean * mean
    return (preds.reshape(SEQS, SEQ_LEN, PD), d_inputs.reshape(SEQS, SEQ_LEN, D), variance, grads[0], grads[1], grads[2], grads[3], grads[4], grads[5], grads[6], grads[7], grads[8], grads[9], grads[10], grads[11], grads[12], grads[13])
```

```python
import jax
import jax.numpy as jnp
from jax import lax
from jax.sharding import PartitionSpec as P

HEAD_DIM = 64
P_HEAD_DIM = 32
EPS = 1e-06
BF = jnp.bfloat16
F32 = jnp.float32


def swap(value, axis, bit):
    size = lax.axis_size(axis)
    return lax.ppermute(value, axis, [(i, i ^ bit) for i in range(size)])


def pick(value, index, axis=0):
    return lax.dynamic_index_in_dim(value, index, axis, keepdims=False)


def mm(spec, left, right):
    return jnp.einsum(spec, left, right, preferred_element_type=F32)


def norm_parts(value):
    mean = jnp.mean(value, -1, keepdims=True)
    centred = value - mean
    inverse = lax.rsqrt(jnp.mean(centred * centred, -1, keepdims=True) + EPS)
    return centred * inverse, inverse


def norm_back(normed, inverse, gain, grad):
    scaled = grad * gain
    along = jnp.mean(scaled * normed, -1, keepdims=True)
    d_value = (scaled - jnp.mean(scaled, -1, keepdims=True) - normed * along) * inverse
    return d_value, jnp.sum(grad * normed, 0)


def gather_shards(own):
    across = swap(own, "mp", 2)
    return [own, swap(own, "mp", 1), across, swap(across, "mp", 1)]


def block_forward(value, gains, weights, same, head_dim):
    w_q, w_k, w_v, w_o, w_up, w_down = weights
    length = value.shape[0]
    n_one, r_one = norm_parts(value)
    a = (n_one * gains[0]).astype(BF)
    heads = w_q.shape[0] // head_dim
    q, k, u = (mm("td,hd->ht", a, w).astype(BF).reshape(heads, head_dim, length) for w in (w_q, w_k, w_v))
    s = mm("hdq,hdk->hqk", q, k) * head_dim ** (-0.5)
    s = jnp.where(same, s, -1e9)
    expd = jnp.exp(s - jnp.max(s, -1, keepdims=True))
    p = expd / jnp.sum(expd, -1, keepdims=True)
    pb = p.astype(BF)
    o = mm("hqk,hdk->hdq", pb, u).astype(BF).reshape(-1, length)
    middle = value + mm("ht,hd->td", o, w_o)
    n_two, r_two = norm_parts(middle)
    b = (n_two * gains[1]).astype(BF)
    pre = mm("td,hd->th", b, w_up)
    cdf = 0.5 * (1.0 + lax.erf(pre * 0.7071067811865476))
    hid = (pre * cdf).astype(BF)
    slope = cdf + pre * (0.3989422804014327 * jnp.exp(-0.5 * pre * pre))
    out = middle + mm("th,hd->td", hid, w_down)
    return out, (n_one, r_one, a, q, k, u, pb, o, n_two, r_two, b, hid, slope)


def block_backward(grad, kept, gains, weights, head_dim):
    w_q, w_k, w_v, w_o, w_up, w_down = weights
    n_one, r_one, a, q, k, u, pb, o, n_two, r_two, b, hid, slope = kept
    length = grad.shape[0]
    shards = 4
    grad_low = grad.astype(BF)
    d_hid = mm("td,hd->th", grad_low, w_down)
    d_pre = (d_hid * slope).astype(BF)

    def weight_grad(left, right):
        return mm("td,tsc->sdc", left, right.reshape(length, shards, -1)).astype(BF)

    def weight_grad_t(left, right):
        return mm("td,sct->sdc", left, right.reshape(shards, -1, length)).astype(BF)

    g_down = weight_grad(grad_low, hid)
    g_up = weight_grad(b, d_pre)
    d_b = mm("th,hd->td", d_pre, w_up)
    d_middle, d_gain_two = norm_back(n_two, r_two, gains[1], d_b)
    grad_mid = grad + d_middle
    mid_low = grad_mid.astype(BF)
    g_out = weight_grad_t(mid_low, o)
    d_o = mm("hd,td->ht", w_o, mid_low).astype(BF).reshape(q.shape)
    p = pb.astype(F32)
    d_p = mm("hdq,hdk->hqk", d_o, u)
    d_s = (p * (d_p - jnp.sum(d_p * p, -1, keepdims=True))).astype(BF)
    scale = head_dim ** (-0.5)
    d_q = (mm("hqk,hdk->hdq", d_s, k) * scale).astype(BF).reshape(-1, length)
    d_k = (mm("hqk,hdq->hdk", d_s, q) * scale).astype(BF).reshape(-1, length)
    d_u = mm("hqk,hdq->hdk", pb, d_o).astype(BF).reshape(-1, length)
    g_q, g_k, g_v = (weight_grad_t(a, d) for d in (d_q, d_k, d_u))
    d_a = mm("ht,hd->td", d_q, w_q) + mm("ht,hd->td", d_k, w_k) + mm("ht,hd->td", d_u, w_v)
    d_value, d_gain_one = norm_back(n_one, r_one, gains[0], d_a)
    g_attn = jnp.concatenate([g_q, g_k, g_v, g_out], -1)
    return grad_mid + d_value, (g_attn, g_up, g_down), (d_gain_one, d_gain_two)


def reduce_shards(grads):
    away = swap(jnp.stack([grads[1], grads[3]]), "mp", 1)
    pair = jnp.stack([grads[0], grads[2]]).astype(F32) + away.astype(F32)
    other = swap(pair[1].astype(BF), "mp", 2)
    total = (pair[0] + other.astype(F32)).astype(BF)
    size = lax.axis_size("dp")
    rows = total.shape[0] // size
    parts = lax.all_to_all(total, "dp", 0, 0, tiled=True).reshape(size, rows, -1)
    return jnp.sum(parts.astype(F32), 0)


def spread_rows(value, me):
    across = swap(value, "mp", 2)
    both = jnp.stack([value, across])
    other = swap(both, "mp", 1)
    rel = jnp.stack([both[0], other[0], both[1], other[1]])
    return rel[jnp.arange(4) ^ me]


def body(
    patches, segment_ids, mask_slots, gain_attn, qkv_weight, out_weight, gain_mlp, up_weight, down_weight,
    embed_weight, mask_token, pred_gain_attn, pred_qkv, pred_out, pred_gain_mlp, pred_up, pred_down, cotangent,
):
    me = lax.axis_index("mp")
    dp_size = lax.axis_size("dp")
    length, width = patches.shape[1:]
    channels = cotangent.shape[2]
    value = pick(patches, me).astype(F32)
    segments = pick(segment_ids, me)
    slots = pick(mask_slots, me)
    grad = pick(cotangent, me).astype(F32)
    same = (segments[:, None] == segments[None, :])[None]
    masked = jnp.any(jnp.arange(length, dtype=jnp.int32)[:, None] == slots[None, :], -1, keepdims=True)

    attn_own = jnp.concatenate([jnp.swapaxes(qkv_weight, 1, 2).reshape(-1, width), out_weight], 0)
    attn = gather_shards(attn_own)
    up = gather_shards(up_weight.T)
    down = gather_shards(down_weight)
    embed = gather_shards(embed_weight.T)
    p_attn_own = jnp.concatenate([jnp.swapaxes(pred_qkv, 1, 2).reshape(-1, channels), pred_out], 0)
    pred = gather_shards(jnp.concatenate([p_attn_own, pred_up.T, pred_down], 0))

    def attn_parts(packs, n):
        stacked = jnp.stack([p[: 4 * n].reshape(4, n, -1) for p in packs], 1)
        return tuple(stacked[i].reshape(4 * n, -1) for i in range(4))

    hd = qkv_weight.shape[2]
    p_hd = pred_qkv.shape[2]
    p_hid = pred_up.shape[1]
    enc_w = attn_parts(attn, hd) + (jnp.concatenate(up, 0), jnp.concatenate(down, 0))
    pred_w = attn_parts(pred, p_hd) + (
        jnp.concatenate([p[4 * p_hd : 4 * p_hd + p_hid] for p in pred], 0),
        jnp.concatenate([p[4 * p_hd + p_hid :] for p in pred], 0),
    )
    embed_all = jnp.stack(embed)[jnp.arange(4) ^ me].reshape(channels, width)
    enc_gains = (gain_attn.astype(F32), gain_mlp.astype(F32))
    pred_gains = (pred_gain_attn.astype(F32), pred_gain_mlp.astype(F32))

    encoded, enc_kept = block_forward(value, enc_gains, enc_w, same, HEAD_DIM)
    enc_low = encoded.astype(BF)
    e = mm("td,cd->tc", enc_low, embed_all)
    start = jnp.where(masked, mask_token.astype(F32), e)
    predicted, pred_kept = block_forward(start, pred_gains, pred_w, same, P_HEAD_DIM)
    d_start, pred_g, pred_dg = block_backward(grad, pred_kept, pred_gains, pred_w, P_HEAD_DIM)
    d_token = jnp.sum(jnp.where(masked, d_start, 0.0), 0)
    d_e = jnp.where(masked, 0.0, d_start).astype(BF)
    d_e_rel = d_e.reshape(length, 4, -1)[:, jnp.arange(4) ^ me]
    g_embed = mm("td,tsc->sdc", enc_low, d_e_rel).astype(BF)
    d_enc = mm("tc,cd->td", d_e, embed_all)
    d_value, enc_g, enc_dg = block_backward(d_enc, enc_kept, enc_gains, enc_w, HEAD_DIM)

    r_pred = reduce_shards(jnp.concatenate(pred_g, -1))
    r_embed = reduce_shards(g_embed)
    r_down = reduce_shards(enc_g[2])
    r_up = reduce_shards(enc_g[1])
    r_attn = reduce_shards(enc_g[0])

    small = jnp.concatenate(
        [enc_dg[0], enc_dg[1], pred_dg[0], pred_dg[1], d_token, jnp.sum(predicted, 0), jnp.sum(predicted * predicted, 0)]
    )
    small = small.reshape(-1, 128)
    for axis in ("mp", "dp"):
        bit = 1
        while bit < lax.axis_size(axis):
            small = small + swap(small, axis, bit)
            bit *= 2
    small = small.reshape(-1)
    d_index = lax.axis_index("dp")

    def dp_slice(lo, n):
        return lax.dynamic_slice_in_dim(small[lo : lo + n], d_index * (n // dp_size), n // dp_size)

    c0 = 2 * width
    count = dp_size * patches.shape[0] * length
    mean = small[c0 + 3 * channels : c0 + 4 * channels] / count
    square = small[c0 + 4 * channels : c0 + 5 * channels] / count
    var_all = square - mean * mean
    n_var = channels // 4
    variance = lax.dynamic_slice_in_dim(var_all, me * n_var, n_var)

    predictions = spread_rows(predicted.astype(BF), me)
    patches_grad = spread_rows(d_value.astype(BF), me)

    def qkv_of(block, n):
        return jnp.stack([block[:, i * n : (i + 1) * n] for i in range(3)])

    return (
        predictions,
        patches_grad,
        variance,
        dp_slice(0, width),
        qkv_of(r_attn, hd),
        r_attn[:, 3 * hd :].T,
        dp_slice(width, width),
        r_up,
        r_down.T,
        r_embed,
        dp_slice(c0 + 2 * channels, channels),
        dp_slice(c0, channels),
        qkv_of(r_pred, p_hd),
        r_pred[:, 3 * p_hd : 4 * p_hd].T,
        dp_slice(c0 + channels, channels),
        r_pred[:, 4 * p_hd : 4 * p_hd + p_hid],
        r_pred[:, 4 * p_hd + p_hid :].T,
    )


def solution(mesh):
    placed = (
        P("dp", None, None), P("dp", None), P("dp", None), P(), P(None, None, "mp"), P("mp", None), P(),
        P(None, "mp"), P("mp", None), P(None, "mp"), P(), P(), P(None, None, "mp"), P("mp", None), P(),
        P(None, "mp"), P("mp", None), P("dp", None, None),
    )
    return jax.shard_map(
        body,
        mesh=mesh,
        in_specs=placed,
        out_specs=(
            P("dp", None, None), P("dp", None, None), P("mp"), P("dp"), P(None, "dp", "mp"), P("mp", "dp"),
            P("dp"), P("dp", "mp"), P("mp", "dp"), P("dp", "mp"), P("dp"), P("dp"), P(None, "dp", "mp"),
            P("mp", "dp"), P("dp"), P("dp", "mp"), P("mp", "dp"),
        ),
        check_vma=False,
    )
```

```python
import jax
import jax.numpy as jnp
from jax import lax
from jax.sharding import PartitionSpec as P

HEAD_DIM = 64
P_HEAD_DIM = 32
EPS = 1e-06
BF = jnp.bfloat16
F32 = jnp.float32


def swap(value, axis, bit):
    size = lax.axis_size(axis)
    return lax.ppermute(value, axis, [(i, i ^ bit) for i in range(size)])


def pick(value, index, axis=0):
    return lax.dynamic_index_in_dim(value, index, axis, keepdims=False)


def mm(spec, left, right):
    return jnp.einsum(spec, left, right, preferred_element_type=F32)


def norm_parts(value):
    mean = jnp.mean(value, -1, keepdims=True)
    centred = value - mean
    inverse = lax.rsqrt(jnp.mean(centred * centred, -1, keepdims=True) + EPS)
    return centred * inverse, inverse


def norm_back(normed, inverse, gain, grad):
    scaled = grad * gain
    along = jnp.mean(scaled * normed, -1, keepdims=True)
    d_value = (scaled - jnp.mean(scaled, -1, keepdims=True) - normed * along) * inverse
    return d_value, jnp.sum(grad * normed, 0)


def after(value, token):
    return lax.optimization_barrier((value, token))[0]


def gather_halves(own, y):
    direct = swap(pick(own, y), "mp", 2)
    relay = swap(direct, "dp", 1)
    across = jnp.stack([direct, relay])
    return [own, swap(own, "mp", 1), across, swap(across, "mp", 1)], direct


def in_order(packs, y):
    return packs[:2] + [p[jnp.arange(2) ^ y] for p in packs[2:]]


def block_forward(value, gains, weights, same, head_dim):
    w_q, w_k, w_v, w_o, w_up, w_down = weights
    length = value.shape[0]
    n_one, r_one = norm_parts(value)
    a = (n_one * gains[0]).astype(BF)
    heads = w_q.shape[0] // head_dim
    q, k, u = (mm("td,hd->ht", a, w).astype(BF).reshape(heads, head_dim, length) for w in (w_q, w_k, w_v))
    s = mm("hdq,hdk->hqk", q, k) * head_dim ** (-0.5)
    s = jnp.where(same, s, -1e9)
    expd = jnp.exp(s - jnp.max(s, -1, keepdims=True))
    p = expd / jnp.sum(expd, -1, keepdims=True)
    pb = p.astype(BF)
    o = mm("hqk,hdk->hdq", pb, u).astype(BF).reshape(-1, length)
    middle = value + mm("ht,hd->td", o, w_o)
    n_two, r_two = norm_parts(middle)
    b = (n_two * gains[1]).astype(BF)
    pre = mm("td,dh->th", b, w_up)
    cdf = 0.5 * (1.0 + lax.erf(pre * 0.7071067811865476))
    hid = (pre * cdf).astype(BF)
    slope = cdf + pre * (0.3989422804014327 * jnp.exp(-0.5 * pre * pre))
    out = middle + mm("th,hd->td", hid, w_down)
    return out, (n_one, r_one, a, q, k, u, pb, o, n_two, r_two, b, hid, slope)


def block_backward(grad, kept, gains, weights, head_dim):
    w_q, w_k, w_v, w_o, w_up, w_down = weights
    n_one, r_one, a, q, k, u, pb, o, n_two, r_two, b, hid, slope = kept
    length = grad.shape[0]
    shards = 4
    grad_low = grad.astype(BF)
    d_hid = mm("td,hd->th", grad_low, w_down)
    d_pre = (d_hid * slope).astype(BF)

    def weight_grad(left, right):
        return mm("td,tsc->sdc", left, right.reshape(length, shards, -1)).astype(BF)

    def weight_grad_t(left, right):
        return mm("td,sct->sdc", left, right.reshape(shards, -1, length)).astype(BF)

    g_down = weight_grad(grad_low, hid)
    g_up = weight_grad(b, d_pre)
    d_b = mm("th,dh->td", d_pre, w_up)
    d_middle, d_gain_two = norm_back(n_two, r_two, gains[1], d_b)
    grad_mid = grad + d_middle
    mid_low = grad_mid.astype(BF)
    g_out = weight_grad_t(mid_low, o)
    d_o = mm("hd,td->ht", w_o, mid_low).astype(BF).reshape(q.shape)
    p = pb.astype(F32)
    d_p = mm("hdq,hdk->hqk", d_o, u)
    d_s = (p * (d_p - jnp.sum(d_p * p, -1, keepdims=True))).astype(BF)
    scale = head_dim ** (-0.5)
    d_q = (mm("hqk,hdk->hdq", d_s, k) * scale).astype(BF).reshape(-1, length)
    d_k = (mm("hqk,hdq->hdk", d_s, q) * scale).astype(BF).reshape(-1, length)
    d_u = mm("hqk,hdq->hdk", pb, d_o).astype(BF).reshape(-1, length)
    g_q, g_k, g_v = (weight_grad_t(a, d) for d in (d_q, d_k, d_u))
    d_a = mm("ht,hd->td", d_q, w_q) + mm("ht,hd->td", d_k, w_k) + mm("ht,hd->td", d_u, w_v)
    d_value, d_gain_one = norm_back(n_one, r_one, gains[0], d_a)
    g_attn = jnp.concatenate([g_q, g_k, g_v, g_out], -1)
    return grad_mid + d_value, (g_attn, g_up, g_down), (d_gain_one, d_gain_two)


def core_step(grads):
    away = swap(jnp.stack([grads[1], grads[3]]), "mp", 1)
    return (jnp.stack([grads[0], grads[2]]).astype(F32) + away.astype(F32)).astype(BF)


def by_side(value, y):
    size = lax.axis_size("dp")
    rows, cols = value.shape[-2:]
    value = value.reshape(value.shape[:-2] + (size // 2, 2, rows // size, cols))
    axis = value.ndim - 3
    return pick(value, y, axis), pick(value, 1 - y, axis)


def add(left, right):
    return (left.astype(F32) + right.astype(F32)).astype(BF)


def x_then_y(pair, y):
    total = add(pair[0], swap(pair[1], "mp", 2))
    here, there = by_side(total, y)
    return add(here, swap(there, "dp", 1))


def y_then_x(pair, y):
    here, there = by_side(pair, y)
    pair = add(here, swap(there, "dp", 1))
    return add(pair[0], swap(pair[1], "mp", 2))


def last_step(value):
    size = lax.axis_size("dp")
    groups = [[i for i in range(size) if i % 2 == side] for side in range(2)]
    parts = lax.all_to_all(value, "dp", 0, 0, axis_index_groups=groups, tiled=True)
    return jnp.sum(parts.astype(F32), 0)


def spread_rows(value, me):
    across = swap(value, "mp", 2)
    both = jnp.stack([value, across])
    other = swap(both, "mp", 1)
    rel = jnp.stack([both[0], other[0], both[1], other[1]])
    return rel[jnp.arange(4) ^ me]


def body(
    patches, segment_ids, mask_slots, gain_attn, qkv_weight, out_weight, gain_mlp, up_weight, down_weight,
    embed_weight, mask_token, pred_gain_attn, pred_qkv, pred_out, pred_gain_mlp, pred_up, pred_down, cotangent,
):
    me = lax.axis_index("mp")
    dp_size = lax.axis_size("dp")
    length, width = patches.shape[1:]
    channels = cotangent.shape[2]
    value = pick(patches, me).astype(F32)
    segments = pick(segment_ids, me)
    slots = pick(mask_slots, me)
    grad = pick(cotangent, me).astype(F32)
    same = (segments[:, None] == segments[None, :])[None]
    masked = jnp.any(jnp.arange(length, dtype=jnp.int32)[:, None] == slots[None, :], -1, keepdims=True)

    y = lax.axis_index("dp") % 2
    hd = qkv_weight.shape[2]
    p_hd = pred_qkv.shape[2]
    p_hid = pred_up.shape[1]
    attn_own = jnp.concatenate([jnp.swapaxes(qkv_weight, 1, 2).reshape(-1, width), out_weight], 0)
    attn, t_attn = gather_halves(attn_own.reshape(2, -1, width), y)
    up_own = jnp.swapaxes(up_weight.reshape(width, 2, -1), 0, 1)
    up, t_up = gather_halves(up_own, y)
    down, t_down = gather_halves(after(down_weight, t_attn).reshape(2, -1, width), y)
    p_attn_own = jnp.concatenate([jnp.swapaxes(pred_qkv, 1, 2).reshape(-1, channels), pred_out], 0)
    p_attn, _ = gather_halves(after(p_attn_own, t_up).reshape(2, -1, channels), y)
    embed, _ = gather_halves(after(embed_weight, t_up).T.reshape(2, -1, width), y)
    p_mlp_own = jnp.stack([pred_up.T.reshape(2, -1, channels), pred_down.reshape(2, -1, channels)], 1)
    p_mlp, _ = gather_halves(after(p_mlp_own, t_down), y)

    def attn_parts(packs, n):
        stacked = jnp.stack([p.reshape(4, n, -1) for p in in_order(packs, y)], 1)
        return tuple(stacked[i].reshape(4 * n, -1) for i in range(4))

    enc_w = attn_parts(attn, hd) + (
        jnp.concatenate([h for p in up for h in (p[0], p[1])], 1),
        jnp.concatenate(down, 0).reshape(-1, width),
    )
    pred_w = attn_parts(p_attn, p_hd) + (
        jnp.concatenate([p[:, 0] for p in p_mlp], 0).reshape(-1, channels).T,
        jnp.concatenate([p[:, 1] for p in p_mlp], 0).reshape(-1, channels),
    )
    embed = [p.reshape(-1, width) for p in in_order(embed, y)]
    embed_all = jnp.stack(embed)[jnp.arange(4) ^ me].reshape(channels, width)
    enc_gains = (gain_attn.astype(F32), gain_mlp.astype(F32))
    pred_gains = (pred_gain_attn.astype(F32), pred_gain_mlp.astype(F32))

    encoded, enc_kept = block_forward(value, enc_gains, enc_w, same, HEAD_DIM)
    enc_low = encoded.astype(BF)
    e = mm("td,cd->tc", enc_low, embed_all)
    start = jnp.where(masked, mask_token.astype(F32), e)
    predicted, pred_kept = block_forward(start, pred_gains, pred_w, same, P_HEAD_DIM)
    d_start, pred_g, pred_dg = block_backward(grad, pred_kept, pred_gains, pred_w, P_HEAD_DIM)
    d_token = jnp.sum(jnp.where(masked, d_start, 0.0), 0)
    d_e = jnp.where(masked, 0.0, d_start).astype(BF)
    d_e_rel = d_e.reshape(length, 4, -1)[:, jnp.arange(4) ^ me]
    g_embed = mm("td,tsc->sdc", enc_low, d_e_rel).astype(BF)
    d_enc = mm("tc,cd->td", d_e, embed_all)
    d_value, enc_g, enc_dg = block_backward(d_enc, enc_kept, enc_gains, enc_w, HEAD_DIM)

    def ordered(grads, parts):
        r, rows, cols = grads.shape
        last = grads[2:].reshape(2, rows, parts, cols // parts)
        return jnp.concatenate([grads[:2], last[:, :, jnp.arange(parts) ^ y].reshape(2, rows, cols)], 0)

    r_pred = last_step(x_then_y(core_step(jnp.concatenate([pred_g[0], ordered(pred_g[1], 2), ordered(pred_g[2], 2)], -1)), y))
    r_down = last_step(x_then_y(core_step(ordered(enc_g[2], 2)), y))
    r_up = last_step(y_then_x(core_step(ordered(enc_g[1], 2)), y))
    attn_pair = core_step(jnp.concatenate([enc_g[0], g_embed], -1))
    r_attn = last_step(
        jnp.concatenate([x_then_y(attn_pair[..., : 2 * hd], y), y_then_x(attn_pair[..., 2 * hd :], y)], -1)
    )
    r_embed = r_attn[:, 4 * hd :]

    small = jnp.concatenate(
        [enc_dg[0], enc_dg[1], pred_dg[0], pred_dg[1], d_token, jnp.sum(predicted, 0), jnp.sum(predicted * predicted, 0)]
    )
    small = small.reshape(-1, 128)
    for axis in ("mp", "dp"):
        bit = 1
        while bit < lax.axis_size(axis):
            small = small + swap(small, axis, bit)
            bit *= 2
    small = small.reshape(-1)
    d_index = lax.axis_index("dp")

    def dp_slice(lo, n):
        return lax.dynamic_slice_in_dim(small[lo : lo + n], d_index * (n // dp_size), n // dp_size)

    c0 = 2 * width
    count = dp_size * patches.shape[0] * length
    mean = small[c0 + 3 * channels : c0 + 4 * channels] / count
    square = small[c0 + 4 * channels : c0 + 5 * channels] / count
    var_all = square - mean * mean
    n_var = channels // 4
    variance = lax.dynamic_slice_in_dim(var_all, me * n_var, n_var)

    predictions = spread_rows(predicted.astype(BF), me)
    patches_grad = spread_rows(d_value.astype(BF), me)

    def qkv_of(block, n):
        return jnp.stack([block[:, i * n : (i + 1) * n] for i in range(3)])

    return (
        predictions,
        patches_grad,
        variance,
        dp_slice(0, width),
        qkv_of(r_attn, hd),
        r_attn[:, 3 * hd : 4 * hd].T,
        dp_slice(width, width),
        r_up,
        r_down.T,
        r_embed,
        dp_slice(c0 + 2 * channels, channels),
        dp_slice(c0, channels),
        qkv_of(r_pred, p_hd),
        r_pred[:, 3 * p_hd : 4 * p_hd].T,
        dp_slice(c0 + channels, channels),
        r_pred[:, 4 * p_hd : 4 * p_hd + p_hid],
        r_pred[:, 4 * p_hd + p_hid :].T,
    )


def solution(mesh):
    placed = (
        P("dp", None, None), P("dp", None), P("dp", None), P(), P(None, None, "mp"), P("mp", None), P(),
        P(None, "mp"), P("mp", None), P(None, "mp"), P(), P(), P(None, None, "mp"), P("mp", None), P(),
        P(None, "mp"), P("mp", None), P("dp", None, None),
    )
    return jax.shard_map(
        body,
        mesh=mesh,
        in_specs=placed,
        out_specs=(
            P("dp", None, None), P("dp", None, None), P("mp"), P("dp"), P(None, "dp", "mp"), P("mp", "dp"),
            P("dp"), P("dp", "mp"), P("mp", "dp"), P("dp", "mp"), P("dp"), P("dp"), P(None, "dp", "mp"),
            P("mp", "dp"), P("dp"), P("dp", "mp"), P("mp", "dp"),
        ),
        check_vma=False,
    )
```

```python
import math

import jax
import jax.numpy as jnp
from jax import lax
from jax.experimental import pallas as pl
from jax.experimental.pallas import tpu as pltpu
from jax.sharding import PartitionSpec as P

HEAD_DIM = 64
P_HEAD_DIM = 32
SHARDS = 4
EPS = 1e-06
BF = jnp.bfloat16
F32 = jnp.float32
VMEM_BYTES = 48 * 1024 * 1024


def contract(left, right, at_left, at_right):
    return lax.dot_general(left, right, (((at_left,), (at_right,)), ((), ())), preferred_element_type=F32)


def nn(left, right):
    return contract(left, right, 1, 0)


def nt(left, right):
    return contract(left, right, 1, 1)


def tn(left, right):
    return contract(left, right, 0, 0)


def norm(value):
    centred = value - jnp.mean(value, -1, keepdims=True)
    inverse = lax.rsqrt(jnp.mean(centred * centred, -1, keepdims=True) + EPS)
    return centred * inverse, inverse


def norm_back(normed, inverse, gain, grad):
    scaled = grad * gain
    along = jnp.mean(scaled * normed, -1, keepdims=True)
    d_value = (scaled - jnp.mean(scaled, -1, keepdims=True) - normed * along) * inverse
    return d_value, jnp.sum(grad * normed, 0, keepdims=True)


def gelu_parts(pre):
    cdf = 0.5 * (1.0 + lax.erf(pre * 0.7071067811865476))
    density = 0.3989422804014327 * jnp.exp(-0.5 * pre * pre)
    return pre * cdf, cdf + pre * density


def turned(source_rows, value):
    width = value.shape[1]
    one_hot = (lax.broadcasted_iota(jnp.int32, (width, width), 1) == source_rows).astype(BF)
    return nt(one_hot, value).astype(BF)


def head_rows(head, per, head_dim):
    shard = head // per
    first = shard * (3 * per * head_dim) + (head - shard * per) * head_dim
    return [pl.ds(pl.multiple_of(first + part * per * head_dim, head_dim), head_dim) for part in range(3)]


def attend(qkv_ref, probs_ref, mixed_ref, same, per, head_dim):
    factor = head_dim ** (-0.5) * math.log2(math.e)

    def one_head(head, carry):
        q_at, k_at, u_at = head_rows(head, per, head_dim)
        scores = jnp.where(same, tn(qkv_ref[k_at, :], qkv_ref[q_at, :]), -1e9)
        top = jnp.max(scores, 0, keepdims=True)
        expd = jnp.exp2((scores - top) * factor)
        probs = (expd * (1.0 / jnp.sum(expd, 0, keepdims=True))).astype(BF)
        probs_ref[head] = probs
        at = pl.ds(pl.multiple_of(head * head_dim, head_dim), head_dim)
        mixed_ref[at, :] = nn(qkv_ref[u_at, :], probs).astype(BF)
        return carry

    lax.fori_loop(0, SHARDS * per, one_head, 0, unroll=2)


def attend_back(qkv_ref, probs_ref, d_mixed_ref, d_qkv_ref, per, head_dim):
    scale = head_dim ** (-0.5)

    def one_head(head, carry):
        q_at, k_at, u_at = head_rows(head, per, head_dim)
        at = pl.ds(pl.multiple_of(head * head_dim, head_dim), head_dim)
        d_mixed = d_mixed_ref[at, :]
        low = probs_ref[head]
        probs = low.astype(F32)
        d_probs = tn(qkv_ref[u_at, :], d_mixed)
        along = jnp.sum(d_probs * probs, 0, keepdims=True)
        d_scores = (probs * (d_probs - along)).astype(BF)
        d_qkv_ref[q_at, :] = (nn(qkv_ref[k_at, :], d_scores) * scale).astype(BF)
        d_qkv_ref[k_at, :] = (nt(qkv_ref[q_at, :], d_scores) * scale).astype(BF)
        d_qkv_ref[u_at, :] = nt(d_mixed, low).astype(BF)
        return carry

    lax.fori_loop(0, SHARDS * per, one_head, 0, unroll=2)


def call(kernel, outs, args, scratch=(), flops=0):
    shapes = [jax.ShapeDtypeStruct(shape, kind) for shape, kind in outs]
    moved = sum(math.prod(a.shape) * a.dtype.itemsize for a in list(args) + shapes)
    return pl.pallas_call(
        kernel,
        out_shape=shapes,
        in_specs=[pl.BlockSpec(memory_space=pltpu.SMEM)] + [pl.BlockSpec(memory_space=pltpu.VMEM)] * (len(args) - 1),
        out_specs=[pl.BlockSpec(memory_space=pltpu.VMEM)] * len(shapes),
        scratch_shapes=[pltpu.VMEM(shape, kind) for shape, kind in scratch],
        compiler_params=pltpu.CompilerParams(vmem_limit_bytes=VMEM_BYTES),
        cost_estimate=pl.CostEstimate(flops=flops, bytes_accessed=moved, transcendentals=0),
    )(*args)


def pack_attn_kernel(pos, qkv, out, own, direct):
    cols = qkv.shape[2]
    for part in range(3):
        own[part * cols : (part + 1) * cols, :] = qkv[part].T
    own[3 * cols :, :] = out[...]
    half = direct.shape[0]
    direct[...] = own[pl.ds(pl.multiple_of(pos[1] * half, half), half), :]


def pack_mlp_kernel(pos, up, down, up_direct, down_direct):
    half = up_direct.shape[1]
    at = pl.ds(pl.multiple_of(pos[1] * half, half), half)
    up_direct[...] = up[:, at]
    down_direct[...] = down[at, :]


def pack_pred_kernel(pos, qkv, out, embed, up, down, attn, attn_direct, mlp, mlp_direct):
    cols, half_width = qkv.shape[2], attn.shape[2]
    attn[0, :cols, :] = qkv[0].T
    attn[0, cols : 2 * cols, :] = qkv[1].T
    attn[0, 2 * cols :, :] = embed[:half_width, :].T
    attn[1, :cols, :] = qkv[2].T
    attn[1, cols : 2 * cols, :] = out[...]
    attn[1, 2 * cols :, :] = embed[half_width:, :].T
    half = mlp.shape[2]
    turned_up = up[...].T
    for side in range(2):
        mlp[side, 0] = turned_up[side * half : (side + 1) * half, :]
        mlp[side, 1] = down[side * half : (side + 1) * half, :]
    attn_direct[...] = attn[pos[1]]
    mlp_direct[...] = mlp[pos[1]]


def enc_attn_kernel(pos, x, seg_row, seg_col, gain, own, core, d_x, e_x, d_c, e_c, middle, qkv, probs, mixed, far):
    side = pos[1]
    half = d_x.shape[0]
    per = own.shape[0] // 4 // HEAD_DIM
    rows = 3 * per * HEAD_DIM
    for at, (first, second) in enumerate(((d_x, e_x), (d_c, e_c))):
        far[at, pl.ds(pl.multiple_of(side * half, half), half), :] = first[...]
        far[at, pl.ds(pl.multiple_of((1 - side) * half, half), half), :] = second[...]
    value = x[...].astype(F32)
    normed, _ = norm(value)
    low = (normed * gain[...]).astype(BF)
    packs = (own, core, far.at[0], far.at[1])
    for shard, pack in enumerate(packs):
        qkv[shard * rows : (shard + 1) * rows, :] = nt(pack[:rows, :], low).astype(BF)
    attend(qkv, probs, mixed, seg_col[...] == seg_row[...], per, HEAD_DIM)
    total = value
    for shard, pack in enumerate(packs):
        total = total + tn(mixed[shard * rows // 3 : (shard + 1) * rows // 3, :], pack[rows:, :])
    middle[...] = total


def hidden_pieces(side, mats, width):
    half = width // 2
    own, core, d_x, e_x, d_c, e_c = mats
    first, second = side * half, (1 - side) * half
    return (
        (own, 0, width), (core, width, width),
        (d_x, 2 * width + first, half), (e_x, 2 * width + second, half),
        (d_c, 3 * width + first, half), (e_c, 3 * width + second, half),
    )


def columns(first, size):
    return pl.ds(first if isinstance(first, int) else pl.multiple_of(first, 128), size)


def enc_mlp_kernel(pos, middle, gain, *refs):
    ups, downs, (hidden, slope, out) = refs[:6], refs[6:12], refs[12:]
    width = ups[0].shape[1]
    value = middle[...]
    normed, _ = norm(value)
    low = (normed * gain[...]).astype(BF)
    total = value
    for (up, first, size), down in zip(hidden_pieces(pos[1], ups, width), downs):
        act, back = gelu_parts(nn(low, up[...]))
        act = act.astype(BF)
        hidden[:, columns(first, size)] = act
        slope[:, columns(first, size)] = back.astype(BF)
        total = total + nn(act, down[...])
    out[...] = total.astype(BF)


def pred_kernel(
    pos, enc, seg_row, seg_col, masked, token, gain_one, gain_two, cot, rows_at,
    a_own, a_core, a_dx, a_ex, a_dc, a_ec, m_own, m_core, m_dx, m_ex, m_dc, m_ec,
    pred_out, stats, g_mine, g_theirs, d_embedded, d_enc, d_gains,
    w_qkv, w_out, w_embed, w_up, w_down, qkv, probs, mixed, d_mixed, d_qkv,
):
    me, side = pos[0], pos[1]
    cols = w_out.shape[0] // SHARDS
    per = cols // P_HEAD_DIM
    half = m_dx.shape[1]
    hid = 2 * half
    width = w_out.shape[1]
    flip = side != 0
    near = ((a_own[0], a_own[1]), (a_core[0], a_core[1]))
    far = tuple((jnp.where(flip, e[...], d[...]), jnp.where(flip, d[...], e[...])) for d, e in ((a_dx, a_ex), (a_dc, a_ec)))
    for shard, (zero, one) in enumerate(near + far):
        w_qkv[shard * 3 * cols : shard * 3 * cols + 2 * cols, :] = zero[: 2 * cols]
        w_qkv[shard * 3 * cols + 2 * cols : (shard + 1) * 3 * cols, :] = one[:cols]
        w_out[shard * cols : (shard + 1) * cols, :] = one[cols : 2 * cols]
        at = pl.ds(pl.multiple_of((me ^ shard) * cols, 16), cols)
        w_embed[at, :width] = zero[2 * cols :]
        w_embed[at, width:] = one[2 * cols :]
    for shard, pack in enumerate((m_own, m_core)):
        for which in range(2):
            at = slice(shard * hid + which * half, shard * hid + (which + 1) * half)
            w_up[at, :] = pack[which, 0]
            w_down[at, :] = pack[which, 1]
    for shard, (d, e) in ((2, (m_dx, m_ex)), (3, (m_dc, m_ec))):
        for first, pack in ((side, d), (1 - side, e)):
            at = pl.ds(pl.multiple_of(shard * hid + first * half, 16), half)
            w_up[at, :] = pack[0]
            w_down[at, :] = pack[1]

    hidden_mask = masked[...] > 0.0
    start = jnp.where(hidden_mask, token[...], nt(enc[...], w_embed[...]))
    n_one, r_one = norm(start)
    a = (n_one * gain_one[...]).astype(BF)
    qkv[...] = nt(w_qkv[...], a).astype(BF)
    attend(qkv, probs, mixed, seg_col[...] == seg_row[...], per, P_HEAD_DIM)
    middle = start + tn(mixed[...], w_out[...])
    n_two, r_two = norm(middle)
    b = (n_two * gain_two[...]).astype(BF)
    act, slope = gelu_parts(nt(b, w_up[...]))
    act = act.astype(BF)
    predicted = middle + nn(act, w_down[...])
    pred_out[...] = predicted.astype(BF)
    stats[0:1, :] = jnp.sum(predicted, 0, keepdims=True)
    stats[1:2, :] = jnp.sum(predicted * predicted, 0, keepdims=True)

    homes = ((g_mine, 0), (g_theirs, 0), (g_mine, 1), (g_theirs, 1))
    grad_low = cot[...]
    d_pre = (nt(grad_low, w_down[...]) * slope).astype(BF)
    source = rows_at[...]
    grad_turned, b_turned = turned(source, grad_low), turned(source, b)
    for shard, (home, at) in enumerate(homes):
        cut = slice(shard * hid, (shard + 1) * hid)
        home[at, :, 4 * cols : 4 * cols + hid] = nn(b_turned, d_pre[:, cut]).astype(BF)
        home[at, :, 4 * cols + hid :] = nn(grad_turned, act[:, cut]).astype(BF)
    d_middle, d_gain_two = norm_back(n_two, r_two, gain_two[...], nn(d_pre, w_up[...]))
    grad_mid = grad_low.astype(F32) + d_middle
    mid_low = grad_mid.astype(BF)
    d_mixed[...] = nt(w_out[...], mid_low).astype(BF)
    attend_back(qkv, probs, d_mixed, d_qkv, per, P_HEAD_DIM)
    a_turned, mid_turned = turned(source, a), turned(source, mid_low)
    for shard, (home, at) in enumerate(homes):
        home[at, :, : 3 * cols] = nt(a_turned, d_qkv[shard * 3 * cols : (shard + 1) * 3 * cols, :]).astype(BF)
        home[at, :, 3 * cols : 4 * cols] = nt(mid_turned, mixed[shard * cols : (shard + 1) * cols, :]).astype(BF)
    d_value, d_gain_one = norm_back(n_one, r_one, gain_one[...], tn(d_qkv[...], w_qkv[...]))
    d_start = grad_mid + d_value
    d_gains[0:1, :] = d_gain_one
    d_gains[1:2, :] = d_gain_two
    d_gains[2:3, :] = jnp.sum(jnp.where(hidden_mask, d_start, 0.0), 0, keepdims=True)
    d_low = jnp.where(hidden_mask, 0.0, d_start).astype(BF)
    d_embedded[...] = d_low
    d_enc[...] = nn(d_low, w_embed[...])


def enc_down_kernel(pos, rows_at, grad, hidden, mine, theirs):
    width = hidden.shape[1] // SHARDS
    grad_turned = turned(rows_at[...], grad[...].astype(BF))
    for shard, (home, at) in ((1, (theirs, 0)), (3, (theirs, 1)), (0, (mine, 0)), (2, (mine, 1))):
        home[at] = nn(grad_turned, hidden[:, shard * width : (shard + 1) * width]).astype(BF)


def enc_up_kernel(pos, rows_at, grad, d_embedded, enc, middle, gain, slope, *refs):
    ups, downs, (mine, theirs, grad_mid, d_gain) = refs[:6], refs[6:12], refs[12:]
    me = pos[0]
    width = ups[0].shape[1]
    source = rows_at[...]
    value = middle[...]
    n_two, r_two = norm(value)
    b_turned = turned(source, (n_two * gain[...]).astype(BF))
    homes = ((mine, 0), (theirs, 0), (mine, 1), (theirs, 1))
    low = grad[...].astype(BF)
    d_b = jnp.zeros_like(value)
    pieces = hidden_pieces(pos[1], ups, width)
    for piece in (1, 4, 5, 0, 2, 3):
        up, first, size = pieces[piece]
        shard = (0, 1, 2, 2, 3, 3)[piece]
        d_pre = (nt(low, downs[piece][...]) * slope[:, columns(first, size)].astype(F32)).astype(BF)
        d_b = d_b + nt(d_pre, up[...])
        home, at = homes[shard]
        home[at, :, columns(first - shard * width, size)] = nn(b_turned, d_pre).astype(BF)
    channels = d_embedded.shape[1]
    cols = channels // SHARDS
    row = lax.broadcasted_iota(jnp.int32, (channels, SHARDS * 128), 0)
    column = lax.broadcasted_iota(jnp.int32, (channels, SHARDS * 128), 1)
    within = column & 127
    one_hot = ((((column >> 7) ^ me) * cols + within == row) & (within < cols)).astype(BF)
    spaced = nn(d_embedded[...], one_hot).astype(BF)
    g_embed = nn(turned(source, enc[...]), spaced).astype(BF)
    for shard, (home, at) in enumerate(homes):
        home[at, :, width:] = g_embed[:, shard * 128 : (shard + 1) * 128]
    d_middle, d_gain_two = norm_back(n_two, r_two, gain[...], d_b)
    grad_mid[...] = grad[...] + d_middle
    d_gain[...] = d_gain_two


def enc_attn_back_kernel(
    pos, rows_at, x, gain, grad, qkv, probs, mixed, own, core, d_x, e_x, d_c, e_c,
    mine, theirs, d_input, d_gain, far, d_mixed, d_qkv,
):
    side = pos[1]
    half = d_x.shape[0]
    per = own.shape[0] // 4 // HEAD_DIM
    cols = per * HEAD_DIM
    for at, (first, second) in enumerate(((d_x, e_x), (d_c, e_c))):
        far[at, pl.ds(pl.multiple_of(side * half, half), half), :] = first[...]
        far[at, pl.ds(pl.multiple_of((1 - side) * half, half), half), :] = second[...]
    packs = (own, core, far.at[0], far.at[1])
    low = grad[...].astype(BF)
    for shard, pack in enumerate(packs):
        d_mixed[shard * cols : (shard + 1) * cols, :] = nt(pack[3 * cols :, :], low).astype(BF)
    attend_back(qkv, probs, d_mixed, d_qkv, per, HEAD_DIM)
    value = x[...].astype(F32)
    normed, inverse = norm(value)
    source = rows_at[...]
    a_turned = turned(source, (normed * gain[...]).astype(BF))
    mid_turned = turned(source, low)
    homes = ((mine, 0), (theirs, 0), (mine, 1), (theirs, 1))
    d_a = jnp.zeros_like(value)
    for shard in (1, 3, 0, 2):
        home, at = homes[shard]
        d_part = d_qkv[shard * 3 * cols : (shard + 1) * 3 * cols, :]
        home[at, :, : 3 * cols] = nt(a_turned, d_part).astype(BF)
        home[at, :, 3 * cols :] = nt(mid_turned, mixed[shard * cols : (shard + 1) * cols, :]).astype(BF)
        d_a = d_a + tn(d_part, packs[shard][: 3 * cols, :])
    d_value, d_gain_one = norm_back(normed, inverse, gain[...], d_a)
    d_input[...] = (grad[...] + d_value).astype(BF)
    d_gain[...] = d_gain_one


def swap(value, axis, bit):
    size = lax.axis_size(axis)
    return lax.ppermute(value, axis, [(i, i ^ bit) for i in range(size)])


def pick(value, index, axis=0):
    return lax.dynamic_index_in_dim(value, index, axis, keepdims=False)


def after(value, token):
    return lax.optimization_barrier((value, token))[0]


def gather_shards(own, direct):
    d_x = swap(direct, "mp", 2)
    e_x = swap(d_x, "dp", 1)
    return (own, swap(own, "mp", 1), d_x, e_x, swap(d_x, "mp", 1), swap(e_x, "mp", 1))


def added(*parts):
    total = parts[0].astype(F32)
    for part in parts[1:]:
        total = total + part.astype(F32)
    return total.astype(BF)


def x_then_y(mine, away):
    half = mine.shape[1] // 2
    other = swap(added(mine[1], away[1]), "mp", 2)
    there = swap(added(mine[0, half:], away[0, half:], other[half:]), "dp", 1)
    return added(mine[0, :half], away[0, :half], other[:half], there)


def y_then_x(mine, away):
    half = mine.shape[1] // 2
    there = swap(added(mine[:, half:], away[:, half:]), "dp", 1)
    other = swap(added(mine[1, :half], away[1, :half], there[1]), "mp", 2)
    return added(mine[0, :half], away[0, :half], there[0], other)


def last_step(value):
    size = lax.axis_size("dp")
    groups = [[i for i in range(size) if i % 2 == side] for side in range(2)]
    value = value.reshape(size // 2, -1, value.shape[1])
    parts = lax.all_to_all(value, "dp", 0, 0, axis_index_groups=groups, tiled=True)
    return jnp.sum(parts.astype(F32), 0)


def spread_rows(value, me):
    across = swap(value, "mp", 2)
    rel = (value, swap(value, "mp", 1), across, swap(across, "mp", 1))
    out = jnp.zeros((SHARDS,) + value.shape, value.dtype)
    for shard, part in enumerate(rel):
        out = lax.dynamic_update_index_in_dim(out, part, me ^ shard, 0)
    return out


def source_rows(width, side):
    size = lax.axis_size("dp")
    blocks = jnp.arange(width, dtype=jnp.int32).reshape(size // 2, 2, width // size)
    order = jnp.where(side == 0, blocks, blocks[:, ::-1])
    return jnp.swapaxes(order, 0, 1).reshape(width, 1)


def body(
    patches, segment_ids, mask_slots, gain_attn, qkv_weight, out_weight, gain_mlp, up_weight, down_weight,
    embed_weight, mask_token, pred_gain_attn, pred_qkv, pred_out, pred_gain_mlp, pred_up, pred_down, cotangent,
):
    me = lax.axis_index("mp")
    side = lax.axis_index("dp") % 2
    dp_size = lax.axis_size("dp")
    length, width = patches.shape[1:]
    channels = cotangent.shape[2]
    cols, hid = qkv_weight.shape[2], up_weight.shape[1]
    p_cols, p_hid = pred_qkv.shape[2], pred_up.shape[1]
    heads = SHARDS * cols // HEAD_DIM
    p_heads = SHARDS * p_cols // P_HEAD_DIM
    pos = jnp.stack([me, side]).astype(jnp.int32)

    attn_own, attn_direct = call(
        pack_attn_kernel, [((4 * cols, width), BF), ((2 * cols, width), BF)], (pos, qkv_weight, out_weight)
    )
    attn = gather_shards(attn_own, attn_direct)
    up_direct, down_direct = call(
        pack_mlp_kernel, [((width, hid // 2), BF), ((hid // 2, width), BF)], (pos, up_weight, down_weight)
    )
    up = gather_shards(up_weight, up_direct)
    down = gather_shards(down_weight, down_direct)
    p_attn_own, p_attn_direct, p_mlp_own, p_mlp_direct = call(
        pack_pred_kernel,
        [((2, 3 * p_cols, channels), BF), ((3 * p_cols, channels), BF),
         ((2, 2, p_hid // 2, channels), BF), ((2, p_hid // 2, channels), BF)],
        (pos, pred_qkv, pred_out, embed_weight, pred_up, pred_down),
    )
    p_attn = gather_shards(p_attn_own, p_attn_direct)
    p_mlp = gather_shards(p_mlp_own, p_mlp_direct)

    x = pick(patches, me)
    segments = pick(segment_ids, me)
    seg_row, seg_col = segments[None, :], segments[:, None]
    slots = pick(mask_slots, me)
    masked = jnp.any(jnp.arange(length, dtype=jnp.int32)[:, None] == slots[None, :], -1, keepdims=True).astype(F32)
    cot = pick(cotangent, me)
    row = lambda gain: gain.astype(F32)[None, :]
    rows_at, p_rows_at = source_rows(width, side), source_rows(channels, side)

    middle, qkv, probs, mixed = call(
        enc_attn_kernel,
        [((length, width), F32), ((3 * width, length), BF), ((heads, length, length), BF), ((width, length), BF)],
        (pos, x, seg_row, seg_col, row(gain_attn)) + attn,
        [((2, 4 * cols, width), BF)],
    )
    hidden, slope, enc = call(
        enc_mlp_kernel,
        [((length, SHARDS * hid), BF), ((length, SHARDS * hid), BF), ((length, width), BF)],
        (pos, middle, row(gain_mlp)) + up + down,
    )
    p_shape = (2, channels, 4 * p_cols + 2 * p_hid)
    predicted, stats, p_mine, p_theirs, d_embedded, d_enc, p_d_gains = call(
        pred_kernel,
        [((length, channels), BF), ((2, channels), F32), (p_shape, BF), (p_shape, BF), ((length, channels), BF),
         ((length, width), F32), ((3, channels), F32)],
        (pos, enc, seg_row, seg_col, masked, row(mask_token), row(pred_gain_attn), row(pred_gain_mlp), cot, p_rows_at)
        + p_attn + p_mlp,
        [((3 * channels, channels), BF), ((channels, channels), BF), ((channels, width), BF),
         ((SHARDS * p_hid, channels), BF), ((SHARDS * p_hid, channels), BF), ((3 * channels, length), BF),
         ((p_heads, length, length), BF), ((channels, length), BF), ((channels, length), BF),
         ((3 * channels, length), BF)],
    )

    d_shape = (2, width, hid)
    d_mine, d_theirs = call(enc_down_kernel, [(d_shape, BF)] * 2, (pos, rows_at, d_enc, hidden))
    u_shape = (2, width, hid + 128)
    u_mine, u_theirs, grad_mid, d_gain_two = call(
        enc_up_kernel,
        [(u_shape, BF), (u_shape, BF), ((length, width), F32), ((1, width), F32)],
        (pos, rows_at, d_enc, d_embedded, enc, middle, row(gain_mlp), slope) + up + down,
    )
    a_shape = (2, width, 4 * cols)
    a_mine, a_theirs, d_input, d_gain_one = call(
        enc_attn_back_kernel,
        [(a_shape, BF), (a_shape, BF), ((length, width), BF), ((1, width), F32)],
        (pos, rows_at, x, row(gain_attn), grad_mid, qkv, probs, mixed) + attn,
        [((2, 4 * cols, width), BF), ((width, length), BF), ((3 * width, length), BF)],
    )

    r_pred = last_step(x_then_y(p_mine, swap(p_theirs, "mp", 1)))
    r_down = last_step(x_then_y(d_mine, swap(d_theirs, "mp", 1)))
    r_up = last_step(y_then_x(u_mine, swap(u_theirs, "mp", 1)))
    a_away = swap(a_theirs, "mp", 1)
    a_half = 2 * cols
    r_attn = last_step(
        jnp.concatenate(
            [x_then_y(a_mine[..., :a_half], a_away[..., :a_half]), y_then_x(a_mine[..., a_half:], a_away[..., a_half:])], -1
        )
    )

    small = jnp.concatenate([part.reshape(-1, 128) for part in (d_gain_one, d_gain_two, p_d_gains, stats)], 0)
    for axis in ("mp", "dp"):
        bit = 1
        while bit < lax.axis_size(axis):
            small = small + swap(small, axis, bit)
            bit *= 2
    small = small.reshape(-1)
    d_index = lax.axis_index("dp")

    def dp_slice(lo, n):
        return lax.dynamic_slice_in_dim(small[lo : lo + n], d_index * (n // dp_size), n // dp_size)

    c0 = 2 * width
    count = dp_size * patches.shape[0] * length
    mean = small[c0 + 3 * channels : c0 + 4 * channels] / count
    square = small[c0 + 4 * channels : c0 + 5 * channels] / count
    n_var = channels // SHARDS
    variance = lax.dynamic_slice_in_dim(square - mean * mean, me * n_var, n_var)

    predictions = spread_rows(predicted, me)
    patches_grad = spread_rows(d_input, me)

    def qkv_of(block, n):
        return jnp.stack([block[:, i * n : (i + 1) * n] for i in range(3)])

    return (
        predictions,
        patches_grad,
        variance,
        dp_slice(0, width),
        qkv_of(r_attn, cols),
        r_attn[:, 3 * cols :].T,
        dp_slice(width, width),
        r_up[:, :hid],
        r_down.T,
        r_up[:, hid : hid + p_cols],
        dp_slice(c0 + 2 * channels, channels),
        dp_slice(c0, channels),
        qkv_of(r_pred, p_cols),
        r_pred[:, 3 * p_cols : 4 * p_cols].T,
        dp_slice(c0 + channels, channels),
        r_pred[:, 4 * p_cols : 4 * p_cols + p_hid],
        r_pred[:, 4 * p_cols + p_hid :].T,
    )


def solution(mesh):
    placed = (
        P("dp", None, None), P("dp", None), P("dp", None), P(), P(None, None, "mp"), P("mp", None), P(),
        P(None, "mp"), P("mp", None), P(None, "mp"), P(), P(), P(None, None, "mp"), P("mp", None), P(),
        P(None, "mp"), P("mp", None), P("dp", None, None),
    )
    return jax.shard_map(
        body,
        mesh=mesh,
        in_specs=placed,
        out_specs=(
            P("dp", None, None), P("dp", None, None), P("mp"), P("dp"), P(None, "dp", "mp"), P("mp", "dp"),
            P("dp"), P("dp", "mp"), P("mp", "dp"), P("dp", "mp"), P("dp"), P("dp"), P(None, "dp", "mp"),
            P("mp", "dp"), P("dp"), P("dp", "mp"), P("mp", "dp"),
        ),
        check_vma=False,
    )
```

```python
import math

import jax
import jax.numpy as jnp
from jax import lax
from jax.experimental import pallas as pl
from jax.experimental.pallas import tpu as pltpu
from jax.sharding import PartitionSpec as P

HEAD_DIM = 64
P_HEAD_DIM = 32
SHARDS = 4
EPS = 1e-06
BF = jnp.bfloat16
F32 = jnp.float32
VMEM_BYTES = 48 * 1024 * 1024


def contract(left, right, at_left, at_right):
    return lax.dot_general(left, right, (((at_left,), (at_right,)), ((), ())), preferred_element_type=F32)


def nn(left, right):
    return contract(left, right, 1, 0)


def nt(left, right):
    return contract(left, right, 1, 1)


def tn(left, right):
    return contract(left, right, 0, 0)


def norm(value):
    centred = value - jnp.mean(value, -1, keepdims=True)
    inverse = lax.rsqrt(jnp.mean(centred * centred, -1, keepdims=True) + EPS)
    return centred * inverse, inverse


def norm_back(normed, inverse, gain, grad):
    scaled = grad * gain
    along = jnp.mean(scaled * normed, -1, keepdims=True)
    d_value = (scaled - jnp.mean(scaled, -1, keepdims=True) - normed * along) * inverse
    return d_value, jnp.sum(grad * normed, 0, keepdims=True)


def gelu_parts(pre):
    cdf = 0.5 * (1.0 + lax.erf(pre * 0.7071067811865476))
    density = 0.3989422804014327 * jnp.exp(-0.5 * pre * pre)
    return pre * cdf, cdf + pre * density


def turned(source_rows, value):
    width = value.shape[1]
    one_hot = (lax.broadcasted_iota(jnp.int32, (width, width), 1) == source_rows).astype(BF)
    return nt(one_hot, value).astype(BF)


def head_rows(head, per, head_dim):
    shard = head // per
    first = shard * (3 * per * head_dim) + (head - shard * per) * head_dim
    return [pl.ds(pl.multiple_of(first + part * per * head_dim, head_dim), head_dim) for part in range(3)]


def attend(qkv_ref, probs_ref, mixed_ref, same, per, head_dim):
    factor = head_dim ** (-0.5) * math.log2(math.e)

    def one_head(head, carry):
        q_at, k_at, u_at = head_rows(head, per, head_dim)
        scores = jnp.where(same, tn(qkv_ref[k_at, :], qkv_ref[q_at, :]), -1e9)
        top = jnp.max(scores, 0, keepdims=True)
        expd = jnp.exp2((scores - top) * factor)
        probs = (expd * (1.0 / jnp.sum(expd, 0, keepdims=True))).astype(BF)
        probs_ref[head] = probs
        at = pl.ds(pl.multiple_of(head * head_dim, head_dim), head_dim)
        mixed_ref[at, :] = nn(qkv_ref[u_at, :], probs).astype(BF)
        return carry

    lax.fori_loop(0, SHARDS * per, one_head, 0, unroll=2)


def attend_back(qkv_ref, probs_ref, d_mixed_ref, d_qkv_ref, per, head_dim):
    scale = head_dim ** (-0.5)

    def one_head(head, carry):
        q_at, k_at, u_at = head_rows(head, per, head_dim)
        at = pl.ds(pl.multiple_of(head * head_dim, head_dim), head_dim)
        d_mixed = d_mixed_ref[at, :]
        low = probs_ref[head]
        probs = low.astype(F32)
        d_probs = tn(qkv_ref[u_at, :], d_mixed)
        along = jnp.sum(d_probs * probs, 0, keepdims=True)
        d_scores = (probs * (d_probs - along)).astype(BF)
        d_qkv_ref[q_at, :] = (nn(qkv_ref[k_at, :], d_scores) * scale).astype(BF)
        d_qkv_ref[k_at, :] = (nt(qkv_ref[q_at, :], d_scores) * scale).astype(BF)
        d_qkv_ref[u_at, :] = nt(d_mixed, low).astype(BF)
        return carry

    lax.fori_loop(0, SHARDS * per, one_head, 0, unroll=2)


ANYWHERE = pl.BlockSpec(memory_space=pl.ANY)


ANYWHERE = pl.BlockSpec(memory_space=pl.ANY)


def call(kernel, outs, args, micros, scratch=(), tokens=()):
    shapes = [jax.ShapeDtypeStruct(shape, kind) for shape, kind in outs]
    moved = sum(math.prod(a.shape) * a.dtype.itemsize for a in list(args) + shapes)
    n_args, n_all = len(args), len(args) + len(tokens)
    return pl.pallas_call(
        lambda *refs: kernel(*refs[:n_args], *refs[n_all:]),
        out_shape=shapes,
        in_specs=[pl.BlockSpec(memory_space=pltpu.SMEM)]
        + [pl.BlockSpec(memory_space=pltpu.VMEM)] * (n_args - 1)
        + [ANYWHERE] * len(tokens),
        out_specs=[pl.BlockSpec(memory_space=pltpu.VMEM)] * len(shapes),
        scratch_shapes=[pltpu.VMEM(shape, kind) for shape, kind in scratch],
        compiler_params=pltpu.CompilerParams(vmem_limit_bytes=VMEM_BYTES),
        cost_estimate=pl.CostEstimate(flops=int(micros * 1e10), bytes_accessed=moved, transcendentals=0),
    )(*args, *tokens)


def gate(values, tokens):
    return pl.pallas_call(
        lambda *refs: None,
        out_shape=[jax.ShapeDtypeStruct(v.shape, v.dtype) for v in values],
        in_specs=[ANYWHERE] * (len(values) + len(tokens)),
        out_specs=[ANYWHERE] * len(values),
        input_output_aliases={at: at for at in range(len(values))},
    )(*values, *tokens)


def units(value):
    return [value[:, at * 128 : (at + 1) * 128] for at in range(value.shape[1] // 128)]


class Segments:
    def __init__(self, rows, cols):
        self.half, blocks = rows // 2, cols // 128
        self.left, self.right = blocks // 2, blocks - blocks // 2
        a, b = self.half * self.left, self.half * self.right
        self.over_x, self.over_y = (0, 2 * a), (2 * a, 2 * b)
        self.then_y, self.then_x = (2 * a + 2 * b, a), (3 * a + 2 * b, b)
        self.keep_left, self.keep_right = (3 * a + 3 * b, a), (4 * a + 3 * b, b)
        self.shape = (4 * (a + b), 128)
        self.a, self.b = a, b

    def put(self, ref, shard, block, value):
        half, a, b = self.half, self.a, self.b
        if shard:
            starts_left = (self.over_x[0], self.over_x[0] + a)
            starts_right = (self.then_x[0], self.over_y[0] + b)
        else:
            starts_left = (self.keep_left[0], self.then_y[0])
            starts_right = (self.keep_right[0], self.over_y[0])
        for side in range(2):
            if isinstance(block, int):
                at = starts_left[side] + block * half if block < self.left else starts_right[side] + (block - self.left) * half
            else:
                at = jnp.where(block < self.left, starts_left[side], starts_right[side] - self.left * half) + block * half
                at = pl.multiple_of(at, half)
            ref[pl.ds(at, half), :] = value[side * half : (side + 1) * half].astype(BF)


def combine(outs, tokens):
    arrays, terms = [], []
    for segments in outs:
        for parts in segments:
            for array, first, size in parts:
                if not any(array is known for known in arrays):
                    arrays.append(array)
                terms.append((next(i for i, known in enumerate(arrays) if known is array), first, size))
    n_in, n_out, n_terms = len(arrays) + len(tokens), len(outs), len(terms)
    sizes = [sum(parts[0][2] for parts in segments) for segments in outs]

    def kernel(*refs):
        held, sem = refs[n_in + n_out : -1], refs[-1]
        copies = [
            pltpu.make_async_copy(refs[which].at[pl.ds(first, size), :], held[at], sem.at[at])
            for at, (which, first, size) in enumerate(terms)
        ]
        for copy in copies:
            copy.start()
        at = 0
        for out, segments in zip(refs[n_in:], outs):
            row = 0
            for parts in segments:
                size = parts[0][2]
                mine = list(range(at, at + len(parts)))
                for term in mine:
                    copies[term].wait()

                def add(step, carry, row=row, mine=mine, out=out):
                    here = pl.ds(pl.multiple_of(step * 64, 64), 64)
                    total = held[mine[0]][here, :].astype(F32)
                    for term in mine[1:]:
                        total = total + held[term][here, :].astype(F32)
                    out[pl.ds(pl.multiple_of(row + step * 64, 64), 64), :] = total.astype(BF)
                    return carry

                lax.fori_loop(0, size // 64, add, 0, unroll=2)
                at += len(parts)
                row += size

    moved = 256 * (sum(t[2] for t in terms) + sum(sizes))
    return pl.pallas_call(
        kernel,
        out_shape=[jax.ShapeDtypeStruct((size, 128), BF) for size in sizes],
        in_specs=[ANYWHERE] * n_in,
        out_specs=[pl.BlockSpec(memory_space=pltpu.VMEM)] * n_out,
        scratch_shapes=[pltpu.VMEM((size, 128), BF) for _, _, size in terms] + [pltpu.SemaphoreType.DMA((n_terms,))],
        compiler_params=pltpu.CompilerParams(vmem_limit_bytes=VMEM_BYTES),
        cost_estimate=pl.CostEstimate(flops=int(3e10), bytes_accessed=moved, transcendentals=0),
    )(*arrays, *tokens)


def pack_attn_kernel(pos, qkv, out, own, direct):
    cols = qkv.shape[2]
    for part in range(3):
        own[part * cols : (part + 1) * cols, :] = qkv[part].T
    own[3 * cols :, :] = out[...]
    half = direct.shape[0]
    direct[...] = own[pl.ds(pl.multiple_of(pos[1] * half, half), half), :]


def pack_mlp_kernel(pos, up, down, up_direct, down_direct):
    half = up_direct.shape[1]
    at = pl.ds(pl.multiple_of(pos[1] * half, half), half)
    up_direct[...] = up[:, at]
    down_direct[...] = down[at, :]


def pack_pred_kernel(pos, qkv, out, embed, up, down, attn, mlp):
    cols, half_width = qkv.shape[2], attn.shape[2]
    attn[0, :cols, :] = qkv[0].T
    attn[0, cols : 2 * cols, :] = qkv[1].T
    attn[0, 2 * cols :, :] = embed[:half_width, :].T
    attn[1, :cols, :] = qkv[2].T
    attn[1, cols : 2 * cols, :] = out[...]
    attn[1, 2 * cols :, :] = embed[half_width:, :].T
    half = mlp.shape[2]
    turned_up = up[...].T
    for side in range(2):
        mlp[side, 0] = turned_up[side * half : (side + 1) * half, :]
        mlp[side, 1] = down[side * half : (side + 1) * half, :]


def enc_attn_kernel(pos, x, seg_row, seg_col, gain, own, core, d_x, e_x, d_c, e_c, middle, qkv, probs, mixed, far):
    side = pos[1]
    half = d_x.shape[0]
    per = own.shape[0] // 4 // HEAD_DIM
    rows = 3 * per * HEAD_DIM
    for at, (first, second) in enumerate(((d_x, e_x), (d_c, e_c))):
        far[at, pl.ds(pl.multiple_of(side * half, half), half), :] = first[...]
        far[at, pl.ds(pl.multiple_of((1 - side) * half, half), half), :] = second[...]
    value = x[...].astype(F32)
    normed, _ = norm(value)
    low = (normed * gain[...]).astype(BF)
    packs = (own, core, far.at[0], far.at[1])
    for shard, pack in enumerate(packs):
        qkv[shard * rows : (shard + 1) * rows, :] = nt(pack[:rows, :], low).astype(BF)
    attend(qkv, probs, mixed, seg_col[...] == seg_row[...], per, HEAD_DIM)
    total = value
    for shard, pack in enumerate(packs):
        total = total + tn(mixed[shard * rows // 3 : (shard + 1) * rows // 3, :], pack[rows:, :])
    middle[...] = total


def hidden_pieces(side, mats, width):
    half = width // 2
    own, core, d_x, e_x, d_c, e_c = mats
    first, second = side * half, (1 - side) * half
    return (
        (own, 0, width), (core, width, width),
        (d_x, 2 * width + first, half), (e_x, 2 * width + second, half),
        (d_c, 3 * width + first, half), (e_c, 3 * width + second, half),
    )


def columns(first, size):
    return pl.ds(first if isinstance(first, int) else pl.multiple_of(first, 128), size)


def enc_up_forward_kernel(pos, middle, gain, *refs):
    ups, (hidden, slope) = refs[:6], refs[6:]
    width = ups[0].shape[1]
    normed, _ = norm(middle[...])
    low = (normed * gain[...]).astype(BF)
    for up, first, size in hidden_pieces(pos[1], ups, width):
        act, back = gelu_parts(nn(low, up[...]))
        hidden[:, columns(first, size)] = act.astype(BF)
        slope[:, columns(first, size)] = back.astype(BF)


def enc_down_forward_kernel(pos, middle, hidden, *refs):
    downs, out = refs[:6], refs[6]
    total = middle[...]
    for down, first, size in hidden_pieces(pos[1], downs, downs[0].shape[0]):
        total = total + nn(hidden[:, columns(first, size)], down[...])
    out[...] = total.astype(BF)


def pred_kernel(
    pos, enc, seg_row, seg_col, masked, token, gain_one, gain_two, cot, rows_at,
    a_own, a_core, a_x, a_xc, m_own, m_core, m_x, m_xc,
    pred_out, stats, g_mine, g_theirs, d_embedded, d_enc, d_gains,
    w_qkv, w_out, w_embed, w_up, w_down, qkv, probs, mixed, d_mixed, d_qkv,
):
    me = pos[0]
    length = cot.shape[0]
    cols = w_out.shape[0] // SHARDS
    segments = Segments(w_out.shape[0], 4 * cols + 4 * m_x.shape[2])
    per = cols // P_HEAD_DIM
    half = m_x.shape[2]
    hid = 2 * half
    width = w_out.shape[1]
    for shard, pack in enumerate((a_own, a_core, a_x, a_xc)):
        w_qkv[shard * 3 * cols : shard * 3 * cols + 2 * cols, :] = pack[0, : 2 * cols]
        w_qkv[shard * 3 * cols + 2 * cols : (shard + 1) * 3 * cols, :] = pack[1, :cols]
        w_out[shard * cols : (shard + 1) * cols, :] = pack[1, cols : 2 * cols]
        at = pl.ds(pl.multiple_of((me ^ shard) * cols, 16), cols)
        w_embed[at, :width] = pack[0, 2 * cols :]
        w_embed[at, width:] = pack[1, 2 * cols :]
    for shard, pack in enumerate((m_own, m_core, m_x, m_xc)):
        for which in range(2):
            at = slice(shard * hid + which * half, shard * hid + (which + 1) * half)
            w_up[at, :] = pack[which, 0]
            w_down[at, :] = pack[which, 1]

    hidden_mask = masked[...] > 0.0
    start = jnp.where(hidden_mask, token[...], nt(enc[...], w_embed[...]))
    n_one, r_one = norm(start)
    a = (n_one * gain_one[...]).astype(BF)
    qkv[...] = nt(w_qkv[...], a).astype(BF)
    attend(qkv, probs, mixed, seg_col[...] == seg_row[...], per, P_HEAD_DIM)
    middle = start + tn(mixed[...], w_out[...])
    n_two, r_two = norm(middle)
    b = (n_two * gain_two[...]).astype(BF)
    act, slope = gelu_parts(nt(b, w_up[...]))
    act = act.astype(BF)
    predicted = middle + nn(act, w_down[...])
    for at, block in enumerate(units(predicted)):
        pred_out[at * length : (at + 1) * length, :] = block.astype(BF)
    stats[0:1, :] = jnp.sum(predicted, 0, keepdims=True)
    stats[1:2, :] = jnp.sum(predicted * predicted, 0, keepdims=True)

    homes = ((g_mine, 0), (g_theirs, 0), (g_mine, 1), (g_theirs, 1))
    grad_low = cot[...]
    d_pre = (nt(grad_low, w_down[...]) * slope).astype(BF)
    source = rows_at[...]
    grad_turned, b_turned = turned(source, grad_low), turned(source, b)
    for shard, (home, at) in enumerate(homes):
        cut = slice(shard * hid, (shard + 1) * hid)
        blocks = units(nn(b_turned, d_pre[:, cut])) + units(nn(grad_turned, act[:, cut]))
        for block, value in enumerate(blocks):
            segments.put(home, at, 4 * cols // 128 + block, value)
    d_middle, d_gain_two = norm_back(n_two, r_two, gain_two[...], nn(d_pre, w_up[...]))
    grad_mid = grad_low.astype(F32) + d_middle
    mid_low = grad_mid.astype(BF)
    d_mixed[...] = nt(w_out[...], mid_low).astype(BF)
    attend_back(qkv, probs, d_mixed, d_qkv, per, P_HEAD_DIM)
    a_turned, mid_turned = turned(source, a), turned(source, mid_low)
    for shard, (home, at) in enumerate(homes):
        g_qkv = nt(a_turned, d_qkv[shard * 3 * cols : (shard + 1) * 3 * cols, :])
        g_out = nt(mid_turned, mixed[shard * cols : (shard + 1) * cols, :])
        for block, value in enumerate(units(jnp.concatenate([g_qkv, g_out], 1))):
            segments.put(home, at, block, value)
    d_value, d_gain_one = norm_back(n_one, r_one, gain_one[...], tn(d_qkv[...], w_qkv[...]))
    d_start = grad_mid + d_value
    d_gains[0:1, :] = d_gain_one
    d_gains[1:2, :] = d_gain_two
    d_gains[2:3, :] = jnp.sum(jnp.where(hidden_mask, d_start, 0.0), 0, keepdims=True)
    d_low = jnp.where(hidden_mask, 0.0, d_start).astype(BF)
    d_embedded[...] = d_low
    d_enc[...] = nn(d_low, w_embed[...])


def enc_down_kernel(pos, rows_at, grad, hidden, mine, theirs):
    width = hidden.shape[1] // SHARDS
    segments = Segments(grad.shape[1], width)
    grad_turned = turned(rows_at[...], grad[...].astype(BF))
    for shard, (home, at) in ((1, (theirs, 0)), (3, (theirs, 1)), (0, (mine, 0)), (2, (mine, 1))):
        for block, value in enumerate(units(nn(grad_turned, hidden[:, shard * width : (shard + 1) * width]))):
            segments.put(home, at, block, value)


def enc_up_kernel(pos, rows_at, grad, middle, gain, slope, *refs):
    ups, downs, (mine, theirs, grad_mid, d_gain) = refs[:6], refs[6:12], refs[12:]
    width = ups[0].shape[1]
    value = middle[...]
    segments = Segments(value.shape[1], width)
    n_two, r_two = norm(value)
    b_turned = turned(rows_at[...], (n_two * gain[...]).astype(BF))
    homes = ((mine, 0), (theirs, 0), (mine, 1), (theirs, 1))
    low = grad[...].astype(BF)
    d_b = jnp.zeros_like(value)
    pieces = hidden_pieces(pos[1], ups, width)
    for piece in (1, 4, 5, 0, 2, 3):
        up, first, size = pieces[piece]
        shard = (0, 1, 2, 2, 3, 3)[piece]
        d_pre = (nt(low, downs[piece][...]) * slope[:, columns(first, size)].astype(F32)).astype(BF)
        d_b = d_b + nt(d_pre, up[...])
        home, at = homes[shard]
        first_block = (first - shard * width) // 128
        for block, part in enumerate(units(nn(b_turned, d_pre))):
            segments.put(home, at, first_block + block, part)
    d_middle, d_gain_two = norm_back(n_two, r_two, gain[...], d_b)
    grad_mid[...] = grad[...] + d_middle
    d_gain[...] = d_gain_two


def enc_attn_back_kernel(
    pos, rows_at, x, gain, grad, qkv, probs, mixed, d_embedded, enc, smalls, own, core, d_x, e_x, d_c, e_c,
    mine, theirs, d_input, far, d_mixed, d_qkv,
):
    me, side = pos[0], pos[1]
    half = d_x.shape[0]
    per = own.shape[0] // 4 // HEAD_DIM
    cols = per * HEAD_DIM
    for at, (first, second) in enumerate(((d_x, e_x), (d_c, e_c))):
        far[at, pl.ds(pl.multiple_of(side * half, half), half), :] = first[...]
        far[at, pl.ds(pl.multiple_of((1 - side) * half, half), half), :] = second[...]
    packs = (own, core, far.at[0], far.at[1])
    low = grad[...].astype(BF)
    for shard, pack in enumerate(packs):
        d_mixed[shard * cols : (shard + 1) * cols, :] = nt(pack[3 * cols :, :], low).astype(BF)
    attend_back(qkv, probs, d_mixed, d_qkv, per, HEAD_DIM)
    value = x[...].astype(F32)
    length, width = value.shape
    normed, inverse = norm(value)
    d_a = jnp.zeros_like(value)
    for shard in range(SHARDS):
        d_a = d_a + tn(d_qkv[shard * 3 * cols : (shard + 1) * 3 * cols, :], packs[shard][: 3 * cols, :])
    d_value, d_gain_one = norm_back(normed, inverse, gain[...], d_a)
    for at, block in enumerate(units(grad[...] + d_value)):
        d_input[at * length : (at + 1) * length, :] = block.astype(BF)

    source = rows_at[...]
    a_turned = turned(source, (normed * gain[...]).astype(BF))
    mid_turned = turned(source, low)
    channels = d_embedded.shape[1]
    e_cols = channels // SHARDS
    row = lax.broadcasted_iota(jnp.int32, (channels, SHARDS * 128), 0)
    column = lax.broadcasted_iota(jnp.int32, (channels, SHARDS * 128), 1)
    within = column & 127
    one_hot = ((((column >> 7) ^ me) * e_cols + within == row) & (within < e_cols)).astype(BF)
    g_embed = nn(turned(source, enc[...]), nn(d_embedded[...], one_hot).astype(BF))
    which = lax.broadcasted_iota(jnp.int32, smalls.shape, 0)
    lines = jnp.where(which == 0, d_gain_one, smalls[...]).astype(BF)
    lane = lax.broadcasted_iota(jnp.int32, (smalls.shape[0], 128), 1)
    line = lax.broadcasted_iota(jnp.int32, (smalls.shape[0], 128), 0)
    g_small = nn(turned(source, lines), (lane == line + e_cols).astype(BF))

    segments = Segments(width, 4 * cols + 128)
    homes = ((mine, 0), (theirs, 0), (mine, 1), (theirs, 1))
    for shard in (1, 3, 0, 2):
        home, at = homes[shard]
        g_qkv = nt(a_turned, d_qkv[shard * 3 * cols : (shard + 1) * 3 * cols, :])
        g_out = nt(mid_turned, mixed[shard * cols : (shard + 1) * cols, :])
        blocks = units(jnp.concatenate([g_qkv, g_out], 1)) + [g_embed[:, shard * 128 : (shard + 1) * 128] + g_small]
        for block, part in enumerate(blocks):
            segments.put(home, at, block, part)


def in_order_kernel(pos, own, core, x, xc, out):
    length = out.shape[1]
    for shard, ref in enumerate((own, core, x, xc)):
        for at in range(out.shape[2] // 128):
            out[pos[0] ^ shard, :, at * 128 : (at + 1) * 128] = ref[at * length : (at + 1) * length, :]


def swap(value, axis, bit):
    size = lax.axis_size(axis)
    return lax.ppermute(value, axis, [(i, i ^ bit) for i in range(size)])


def pick(value, index, axis=0):
    return lax.dynamic_index_in_dim(value, index, axis, keepdims=False)


def send_last(kept, segments):
    size = lax.axis_size("dp")
    groups = [[i for i in range(size) if i % 2 == side] for side in range(2)]
    kept = kept.reshape(segments.left + segments.right, size // 2, -1, 128)
    return lax.all_to_all(jnp.swapaxes(kept, 0, 1), "dp", 0, 0, axis_index_groups=groups, tiled=True)


def summed(parts):
    total = jnp.sum(parts.astype(F32), 0)
    return jnp.swapaxes(total, 0, 1).reshape(total.shape[1], -1)


def source_rows(width, side):
    size = lax.axis_size("dp")
    blocks = jnp.arange(width, dtype=jnp.int32).reshape(size // 2, 2, width // size)
    order = jnp.where(side == 0, blocks, blocks[:, ::-1])
    return jnp.swapaxes(order, 0, 1).reshape(width, 1)


def body(
    patches, segment_ids, mask_slots, gain_attn, qkv_weight, out_weight, gain_mlp, up_weight, down_weight,
    embed_weight, mask_token, pred_gain_attn, pred_qkv, pred_out, pred_gain_mlp, pred_up, pred_down, cotangent,
):
    me = lax.axis_index("mp")
    side = lax.axis_index("dp") % 2
    dp_size = lax.axis_size("dp")
    length, width = patches.shape[1:]
    channels = cotangent.shape[2]
    cols, hid = qkv_weight.shape[2], up_weight.shape[1]
    p_cols, p_hid = pred_qkv.shape[2], pred_up.shape[1]
    heads = SHARDS * cols // HEAD_DIM
    p_heads = SHARDS * p_cols // P_HEAD_DIM
    pos = jnp.stack([me, side]).astype(jnp.int32)

    attn_own, attn_direct = call(
        pack_attn_kernel, [((4 * cols, width), BF), ((2 * cols, width), BF)], (pos, qkv_weight, out_weight), 1
    )
    up_direct, down_direct = call(
        pack_mlp_kernel, [((width, hid // 2), BF), ((hid // 2, width), BF)],
        (pos, up_weight, down_weight), 1, tokens=(attn_direct,),
    )
    p_attn_own, p_mlp_own = call(
        pack_pred_kernel,
        [((2, 3 * p_cols, channels), BF), ((2, 2, p_hid // 2, channels), BF)],
        (pos, pred_qkv, pred_out, embed_weight, pred_up, pred_down), 2, tokens=(up_direct,),
    )

    attn_core, up_core, down_core = swap(attn_own, "mp", 1), swap(up_weight, "mp", 1), swap(down_weight, "mp", 1)
    p_attn_core, p_mlp_core = swap(p_attn_own, "mp", 1), swap(p_mlp_own, "mp", 1)
    attn_x = swap(attn_direct, "mp", 2)
    up_x = swap(up_direct, "mp", 2)
    attn_y = swap(attn_x, "dp", 1)
    (down_direct,) = gate([down_direct], [attn_x])
    down_x = swap(down_direct, "mp", 2)
    up_y = swap(up_x, "dp", 1)
    (p_attn_own,) = gate([p_attn_own], [up_x])
    p_attn_x = swap(p_attn_own, "mp", 2)
    attn = (attn_own, attn_core, attn_x, attn_y, swap(attn_x, "mp", 1), swap(attn_y, "mp", 1))

    x = pick(patches, me)
    segments = pick(segment_ids, me)
    seg_row, seg_col = segments[None, :], segments[:, None]
    slots = pick(mask_slots, me)
    masked = jnp.any(jnp.arange(length, dtype=jnp.int32)[:, None] == slots[None, :], -1, keepdims=True).astype(F32)
    cot = pick(cotangent, me)
    row = lambda gain: gain.astype(F32)[None, :]
    rows_at, p_rows_at = source_rows(width, side), source_rows(channels, side)

    middle, qkv, probs, mixed = call(
        enc_attn_kernel,
        [((length, width), F32), ((3 * width, length), BF), ((heads, length, length), BF), ((width, length), BF)],
        (pos, x, seg_row, seg_col, row(gain_attn)) + attn, 9,
        [((2, 4 * cols, width), BF)], tokens=(up_x,),
    )
    up_y, down_x, p_mlp_own = gate([up_y, down_x, p_mlp_own], [middle])
    up = (up_weight, up_core, up_x, up_y, swap(up_x, "mp", 1), swap(up_y, "mp", 1))
    down_y = swap(down_x, "dp", 1)
    p_mlp_x = swap(p_mlp_own, "mp", 2)
    hidden, slope = call(
        enc_up_forward_kernel, [((length, SHARDS * hid), BF), ((length, SHARDS * hid), BF)],
        (pos, middle, row(gain_mlp)) + up, 6, tokens=(down_x,),
    )
    down_y, p_attn_x = gate([down_y, p_attn_x], [hidden])
    down = (down_weight, down_core, down_x, down_y, swap(down_x, "mp", 1), swap(down_y, "mp", 1))
    p_attn = (p_attn_own, p_attn_core, p_attn_x, swap(p_attn_x, "mp", 1))
    (enc,) = call(enc_down_forward_kernel, [((length, width), BF)], (pos, middle, hidden) + down, 4)
    (p_mlp_x,) = gate([p_mlp_x], [enc])
    p_mlp = (p_mlp_own, p_mlp_core, p_mlp_x, swap(p_mlp_x, "mp", 1))
    p_seg, d_seg = Segments(channels, 4 * p_cols + 2 * p_hid), Segments(width, hid)
    u_seg, a_seg = Segments(width, hid), Segments(width, 4 * cols + 128)
    p_blocks, x_blocks = channels // 128, width // 128
    predicted, stats, p_mine, p_theirs, d_embedded, d_enc, p_d_gains = call(
        pred_kernel,
        [((p_blocks * length, 128), BF), ((2, channels), F32), (p_seg.shape, BF), (p_seg.shape, BF), ((length, channels), BF),
         ((length, width), F32), ((3, channels), F32)],
        (pos, enc, seg_row, seg_col, masked, row(mask_token), row(pred_gain_attn), row(pred_gain_mlp), cot, p_rows_at)
        + p_attn + p_mlp, 30,
        [((3 * channels, channels), BF), ((channels, channels), BF), ((channels, width), BF),
         ((SHARDS * p_hid, channels), BF), ((SHARDS * p_hid, channels), BF), ((3 * channels, length), BF),
         ((p_heads, length, length), BF), ((channels, length), BF), ((channels, length), BF),
         ((3 * channels, length), BF)],
    )

    def hop(value, axis, bit):
        return value + swap(value, axis, bit)

    p_away, stats = swap(p_theirs, "mp", 1), hop(stats, "mp", 1)
    d_mine, d_theirs = call(enc_down_kernel, [(d_seg.shape, BF)] * 2, (pos, rows_at, d_enc, hidden), 4)

    p_own = (p_mine, p_away)
    send_x, send_y = combine(
        [[[(g, *p_seg.over_x) for g in p_own], [(predicted, 0, predicted.shape[0])]], [[(g, *p_seg.over_y) for g in p_own]]],
        [d_theirs],
    )
    (stats,) = gate([stats], [send_x])
    d_away, got_x, got_y, stats = swap(d_theirs, "mp", 1), swap(send_x, "mp", 2), swap(send_y, "dp", 1), hop(stats, "mp", 2)
    p_x, p_y = (got_x, 0, 2 * p_seg.a), (got_y, 0, 2 * p_seg.b)
    u_mine, u_theirs, grad_mid, d_gain_two = call(
        enc_up_kernel,
        [(u_seg.shape, BF), (u_seg.shape, BF), ((length, width), F32), ((1, width), F32)],
        (pos, rows_at, d_enc, middle, row(gain_mlp), slope) + up + down, 14, tokens=(send_x, send_y),
    )

    def first(terms, part):
        return (terms[0], terms[1], part)

    def second(terms, part):
        return (terms[0], terms[1] + part, part)

    d_own = (d_mine, d_away)
    predicted_x = lax.slice_in_dim(got_x, 2 * p_seg.a, got_x.shape[0])
    send_x, send_y = combine(
        [[[(g, *d_seg.over_x) for g in d_own], [(g, *p_seg.then_x) for g in p_own] + [second(p_y, p_seg.b)]],
         [[(g, *d_seg.over_y) for g in d_own], [(g, *p_seg.then_y) for g in p_own] + [second(p_x, p_seg.a)]]],
        [u_theirs],
    )
    predicted, predicted_x, stats = gate([predicted, predicted_x, stats], [send_x])
    u_away, got_x, got_y, stats = swap(u_theirs, "mp", 1), swap(send_x, "mp", 2), swap(send_y, "dp", 1), hop(stats, "dp", 1)
    predicted_c, predicted_xc = swap(predicted, "mp", 1), swap(predicted_x, "mp", 1)
    d_x, p_then_x = (got_x, 0, 2 * d_seg.a), (got_x, 2 * d_seg.a, p_seg.b)
    d_y, p_then_y = (got_y, 0, 2 * d_seg.b), (got_y, 2 * d_seg.b, p_seg.a)
    by_block = lambda left, right: jnp.concatenate([left.reshape(dp_size, -1), right.reshape(dp_size, -1)], 1).reshape(1, width)
    zeros = jnp.zeros((channels,), F32)
    smalls = jnp.concatenate(
        [jnp.zeros((1, width), F32), d_gain_two, by_block(p_d_gains[0], p_d_gains[1]), by_block(p_d_gains[2], zeros),
         jnp.zeros((4, width), F32)]
    )
    a_mine, a_theirs, d_input = call(
        enc_attn_back_kernel,
        [(a_seg.shape, BF), (a_seg.shape, BF), ((x_blocks * length, 128), BF)],
        (pos, rows_at, x, row(gain_attn), grad_mid, qkv, probs, mixed, d_embedded, enc, smalls) + attn, 14,
        [((2, 4 * cols, width), BF), ((width, length), BF), ((3 * width, length), BF)], tokens=(send_x, send_y),
    )

    def kept(own, seg, over_x, over_y, then_x, then_y):
        return [[(g, *seg.keep_left) for g in own] + [first(over_x, seg.a), then_y],
                [(g, *seg.keep_right) for g in own] + [first(over_y, seg.b), then_x]]

    u_own = (u_mine, u_away)
    send_x, send_y, p_kept = combine(
        [[[(g, *u_seg.over_x) for g in u_own], [(g, *d_seg.then_x) for g in d_own] + [second(d_y, d_seg.b)],
          [(d_input, 0, d_input.shape[0])]],
         [[(g, *u_seg.over_y) for g in u_own], [(g, *d_seg.then_y) for g in d_own] + [second(d_x, d_seg.a)]],
         kept(p_own, p_seg, p_x, p_y, p_then_x, p_then_y)],
        [a_theirs, predicted_c, predicted_xc],
    )
    stats, d_input = gate([stats, d_input], [send_x])
    a_away, got_x, got_y = swap(a_theirs, "mp", 1), swap(send_x, "mp", 2), swap(send_y, "dp", 1)
    p_parts, input_c = send_last(p_kept, p_seg), swap(d_input, "mp", 1)
    u_x, d_then_x = (got_x, 0, 2 * u_seg.a), (got_x, 2 * u_seg.a, d_seg.b)
    u_y, d_then_y = (got_y, 0, 2 * u_seg.b), (got_y, 2 * u_seg.b, d_seg.a)
    (predictions,) = call(
        in_order_kernel, [((SHARDS, length, channels), BF)], (pos, predicted, predicted_c, predicted_x, predicted_xc), 2,
        tokens=(send_x, send_y),
    )

    a_own = (a_mine, a_away)
    input_x = lax.slice_in_dim(got_x, 2 * u_seg.a + d_seg.b, got_x.shape[0])
    send_x, send_y, d_kept = combine(
        [[[(g, *a_seg.over_x) for g in a_own], [(g, *u_seg.then_x) for g in u_own] + [second(u_y, u_seg.b)]],
         [[(g, *a_seg.over_y) for g in a_own], [(g, *u_seg.then_y) for g in u_own] + [second(u_x, u_seg.a)]],
         kept(d_own, d_seg, d_x, d_y, d_then_x, d_then_y)],
        [predictions, p_parts, input_c],
    )
    input_x, p_parts = gate([input_x, p_parts], [send_x])
    got_x, got_y, d_parts, input_xc = swap(send_x, "mp", 2), swap(send_y, "dp", 1), send_last(d_kept, d_seg), swap(input_x, "mp", 1)
    a_x, u_then_x = (got_x, 0, 2 * a_seg.a), (got_x, 2 * a_seg.a, u_seg.b)
    a_y, u_then_y = (got_y, 0, 2 * a_seg.b), (got_y, 2 * a_seg.b, u_seg.a)
    r_pred = summed(p_parts)

    send_x, send_y, u_kept = combine(
        [[[(g, *a_seg.then_x) for g in a_own] + [second(a_y, a_seg.b)]], [[(g, *a_seg.then_y) for g in a_own] + [second(a_x, a_seg.a)]],
         kept(u_own, u_seg, u_x, u_y, u_then_x, u_then_y)],
        [r_pred, d_parts, input_xc],
    )
    (d_parts,) = gate([d_parts], [send_x])
    got_x, got_y, u_parts = swap(send_x, "mp", 2), swap(send_y, "dp", 1), send_last(u_kept, u_seg)
    r_down = summed(d_parts)
    (patches_grad,) = call(
        in_order_kernel, [((SHARDS, length, width), BF)], (pos, d_input, input_c, input_x, input_xc), 2, tokens=(send_x, send_y)
    )
    (stats,) = gate([stats], [send_x])
    bit = 2
    while bit < dp_size:
        stats = hop(stats, "dp", bit)
        bit *= 2

    (a_kept,) = combine([kept(a_own, a_seg, a_x, a_y, (got_x, 0, a_seg.b), (got_y, 0, a_seg.a))], [patches_grad])
    a_parts = send_last(a_kept, a_seg)
    r_up, r_attn = summed(u_parts), summed(a_parts)

    count = dp_size * patches.shape[0] * length
    mean, square = stats[0] / count, stats[1] / count
    n_var = channels // SHARDS
    variance = lax.dynamic_slice_in_dim(square - mean * mean, me * n_var, n_var)
    tail = r_attn[:, 4 * cols + p_cols :]
    n_small = channels // dp_size

    def qkv_of(block, n):
        return jnp.stack([block[:, i * n : (i + 1) * n] for i in range(3)])

    return (
        predictions,
        patches_grad,
        variance,
        tail[:, 0],
        qkv_of(r_attn, cols),
        r_attn[:, 3 * cols : 4 * cols].T,
        tail[:, 1],
        r_up,
        r_down.T,
        r_attn[:, 4 * cols : 4 * cols + p_cols],
        tail[:n_small, 3],
        tail[:n_small, 2],
        qkv_of(r_pred, p_cols),
        r_pred[:, 3 * p_cols : 4 * p_cols].T,
        tail[n_small:, 2],
        r_pred[:, 4 * p_cols : 4 * p_cols + p_hid],
        r_pred[:, 4 * p_cols + p_hid :].T,
    )


def solution(mesh):
    placed = (
        P("dp", None, None), P("dp", None), P("dp", None), P(), P(None, None, "mp"), P("mp", None), P(),
        P(None, "mp"), P("mp", None), P(None, "mp"), P(), P(), P(None, None, "mp"), P("mp", None), P(),
        P(None, "mp"), P("mp", None), P("dp", None, None),
    )
    return jax.shard_map(
        body,
        mesh=mesh,
        in_specs=placed,
        out_specs=(
            P("dp", None, None), P("dp", None, None), P("mp"), P("dp"), P(None, "dp", "mp"), P("mp", "dp"),
            P("dp"), P("dp", "mp"), P("mp", "dp"), P("dp", "mp"), P("dp"), P("dp"), P(None, "dp", "mp"),
            P("mp", "dp"), P("dp"), P("dp", "mp"), P("mp", "dp"),
        ),
        check_vma=False,
    )
```

```python
import math

import jax
import jax.numpy as jnp
from jax import lax
from jax.experimental import pallas as pl
from jax.experimental.pallas import tpu as pltpu
from jax.sharding import PartitionSpec as P

HEAD_DIM = 64
P_HEAD_DIM = 32
SHARDS = 4
EPS = 1e-06
BF = jnp.bfloat16
F32 = jnp.float32
COST = 1.15e9
VMEM_BYTES = 48 * 1024 * 1024


def contract(left, right, at_left, at_right):
    return lax.dot_general(left, right, (((at_left,), (at_right,)), ((), ())), preferred_element_type=F32)


def nn(left, right):
    return contract(left, right, 1, 0)


def nt(left, right):
    return contract(left, right, 1, 1)


def tn(left, right):
    return contract(left, right, 0, 0)


def norm(value):
    centred = value - jnp.mean(value, -1, keepdims=True)
    inverse = lax.rsqrt(jnp.mean(centred * centred, -1, keepdims=True) + EPS)
    return centred * inverse, inverse


def norm_back(normed, inverse, gain, grad):
    scaled = grad * gain
    along = jnp.mean(scaled * normed, -1, keepdims=True)
    d_value = (scaled - jnp.mean(scaled, -1, keepdims=True) - normed * along) * inverse
    return d_value, jnp.sum(grad * normed, 0, keepdims=True)


def gelu_parts(pre):
    cdf = 0.5 * (1.0 + lax.erf(pre * 0.7071067811865476))
    density = 0.3989422804014327 * jnp.exp(-0.5 * pre * pre)
    return pre * cdf, cdf + pre * density


def turned(source_rows, value):
    width = value.shape[1]
    one_hot = (lax.broadcasted_iota(jnp.int32, (width, width), 1) == source_rows).astype(BF)
    return nt(one_hot, value).astype(BF)


def head_rows(head, per, head_dim):
    shard = head // per
    first = shard * (3 * per * head_dim) + (head - shard * per) * head_dim
    return [pl.ds(pl.multiple_of(first + part * per * head_dim, head_dim), head_dim) for part in range(3)]


def attend(qkv_ref, probs_ref, mixed_ref, same, per, head_dim):
    factor = head_dim ** (-0.5) * math.log2(math.e)

    def one_head(head, carry):
        q_at, k_at, u_at = head_rows(head, per, head_dim)
        scores = jnp.where(same, tn(qkv_ref[k_at, :], qkv_ref[q_at, :]), -1e9)
        top = jnp.max(scores, 0, keepdims=True)
        expd = jnp.exp2((scores - top) * factor)
        probs = (expd * (1.0 / jnp.sum(expd, 0, keepdims=True))).astype(BF)
        probs_ref[head] = probs
        at = pl.ds(pl.multiple_of(head * head_dim, head_dim), head_dim)
        mixed_ref[at, :] = nn(qkv_ref[u_at, :], probs).astype(BF)
        return carry

    lax.fori_loop(0, SHARDS * per, one_head, 0, unroll=2)


def attend_back(qkv_ref, probs_ref, d_mixed_ref, d_qkv_ref, per, head_dim):
    scale = head_dim ** (-0.5)

    def one_head(head, carry):
        q_at, k_at, u_at = head_rows(head, per, head_dim)
        at = pl.ds(pl.multiple_of(head * head_dim, head_dim), head_dim)
        d_mixed = d_mixed_ref[at, :]
        low = probs_ref[head]
        probs = low.astype(F32)
        d_probs = tn(qkv_ref[u_at, :], d_mixed)
        along = jnp.sum(d_probs * probs, 0, keepdims=True)
        d_scores = (probs * (d_probs - along)).astype(BF)
        d_qkv_ref[q_at, :] = (nn(qkv_ref[k_at, :], d_scores) * scale).astype(BF)
        d_qkv_ref[k_at, :] = (nt(qkv_ref[q_at, :], d_scores) * scale).astype(BF)
        d_qkv_ref[u_at, :] = nt(d_mixed, low).astype(BF)
        return carry

    lax.fori_loop(0, SHARDS * per, one_head, 0, unroll=2)


ANYWHERE = pl.BlockSpec(memory_space=pl.ANY)


ANYWHERE = pl.BlockSpec(memory_space=pl.ANY)


def call(kernel, outs, args, micros, scratch=(), tokens=()):
    shapes = [jax.ShapeDtypeStruct(shape, kind) for shape, kind in outs]
    moved = sum(math.prod(a.shape) * a.dtype.itemsize for a in list(args) + shapes)
    n_args, n_all = len(args), len(args) + len(tokens)
    return pl.pallas_call(
        lambda *refs: kernel(*refs[:n_args], *refs[n_all:]),
        out_shape=shapes,
        in_specs=[pl.BlockSpec(memory_space=pltpu.SMEM)]
        + [pl.BlockSpec(memory_space=pltpu.VMEM)] * (n_args - 1)
        + [ANYWHERE] * len(tokens),
        out_specs=[pl.BlockSpec(memory_space=pltpu.VMEM)] * len(shapes),
        scratch_shapes=[pltpu.VMEM(shape, kind) for shape, kind in scratch],
        compiler_params=pltpu.CompilerParams(vmem_limit_bytes=VMEM_BYTES),
        cost_estimate=pl.CostEstimate(flops=int(micros * COST), bytes_accessed=moved if micros else 0, transcendentals=0),
    )(*args, *tokens)


def gate(values, tokens):
    return pl.pallas_call(
        lambda *refs: None,
        out_shape=[jax.ShapeDtypeStruct(v.shape, v.dtype) for v in values],
        in_specs=[ANYWHERE] * (len(values) + len(tokens)),
        out_specs=[ANYWHERE] * len(values),
        input_output_aliases={at: at for at in range(len(values))},
    )(*values, *tokens)


def units(value):
    return [value[:, at * 128 : (at + 1) * 128] for at in range(value.shape[1] // 128)]


class Segments:
    def __init__(self, rows, cols):
        self.half, blocks = rows // 2, cols // 128
        self.left, self.right = blocks // 2, blocks - blocks // 2
        a, b = self.half * self.left, self.half * self.right
        self.over_x, self.over_y = (0, 2 * a), (2 * a, 2 * b)
        self.then_y, self.then_x = (2 * a + 2 * b, a), (3 * a + 2 * b, b)
        self.keep_left, self.keep_right = (3 * a + 3 * b, a), (4 * a + 3 * b, b)
        self.shape = (4 * (a + b), 128)
        self.a, self.b = a, b

    def put(self, ref, shard, block, value):
        half, a, b = self.half, self.a, self.b
        if shard:
            starts_left = (self.over_x[0], self.over_x[0] + a)
            starts_right = (self.then_x[0], self.over_y[0] + b)
        else:
            starts_left = (self.keep_left[0], self.then_y[0])
            starts_right = (self.keep_right[0], self.over_y[0])
        for side in range(2):
            if isinstance(block, int):
                at = starts_left[side] + block * half if block < self.left else starts_right[side] + (block - self.left) * half
            else:
                at = jnp.where(block < self.left, starts_left[side], starts_right[side] - self.left * half) + block * half
                at = pl.multiple_of(at, half)
            ref[pl.ds(at, half), :] = value[side * half : (side + 1) * half].astype(BF)


def combine(outs, tokens, micros, sums=()):
    arrays, terms = [], []
    for segments in outs:
        for parts in segments:
            for array, first, size in parts:
                if not any(array is known for known in arrays):
                    arrays.append(array)
                terms.append((next(i for i, known in enumerate(arrays) if known is array), first, size))
    n_sums, n_arrays, n_out, n_terms = len(sums), len(arrays), len(outs), len(terms)
    n_in = n_sums + n_arrays + len(tokens)
    sizes = [sum(parts[0][2] for parts in segments) for segments in outs]

    def kernel(*refs):
        held, sem = refs[-1 - n_terms : -1], refs[-1]
        copies = [
            pltpu.make_async_copy(refs[n_sums + which].at[pl.ds(first, size), :], held[at], sem.at[at])
            for at, (which, first, size) in enumerate(terms)
        ]
        for copy in copies:
            copy.start()
        if sums:
            refs[n_in + n_out][...] = refs[0][...] + refs[1][...]
        at = 0
        for out, segments in zip(refs[n_in:], outs):
            row = 0
            for parts in segments:
                size = parts[0][2]
                mine = list(range(at, at + len(parts)))
                for term in mine:
                    copies[term].wait()

                def add(step, carry, row=row, mine=mine, out=out):
                    here = pl.ds(pl.multiple_of(step * 64, 64), 64)
                    total = held[mine[0]][here, :].astype(F32)
                    for term in mine[1:]:
                        total = total + held[term][here, :].astype(F32)
                    out[pl.ds(pl.multiple_of(row + step * 64, 64), 64), :] = total.astype(BF)
                    return carry

                lax.fori_loop(0, size // 64, add, 0, unroll=2)
                at += len(parts)
                row += size

    moved = 256 * (sum(t[2] for t in terms) + sum(sizes))
    in_vmem = pl.BlockSpec(memory_space=pltpu.VMEM)
    return pl.pallas_call(
        kernel,
        out_shape=[jax.ShapeDtypeStruct((size, 128), BF) for size in sizes]
        + ([jax.ShapeDtypeStruct(sums[0].shape, F32)] if sums else []),
        in_specs=[in_vmem] * n_sums + [ANYWHERE] * (n_in - n_sums),
        out_specs=[in_vmem] * (n_out + (1 if sums else 0)),
        scratch_shapes=[pltpu.VMEM((size, 128), BF) for _, _, size in terms] + [pltpu.SemaphoreType.DMA((n_terms,))],
        compiler_params=pltpu.CompilerParams(vmem_limit_bytes=VMEM_BYTES),
        cost_estimate=pl.CostEstimate(flops=int(micros * COST), bytes_accessed=moved if micros else 0, transcendentals=0),
    )(*sums, *arrays, *tokens)


def pack_attn_kernel(pos, qkv, out, own, direct):
    cols = qkv.shape[1]
    for part in range(3):
        own[part * cols : (part + 1) * cols, :] = qkv[part]
    own[3 * cols :, :] = out[...]
    half = direct.shape[0]
    direct[...] = own[pl.ds(pl.multiple_of(pos[1] * half, half), half), :]


def pack_rest_kernel(pos, up, down, qkv, out, embed, p_up, p_down, up_direct, down_direct, pred):
    half = up_direct.shape[1]
    at = pl.ds(pl.multiple_of(pos[1] * half, half), half)
    up_direct[...] = up[:, at]
    down_direct[...] = down[at, :]
    width = pred.shape[1]
    row = 0
    for part in (qkv[0], qkv[1], qkv[2], out[...], embed[:, :width], embed[:, width:], p_up[...], p_down[...]):
        pred[row : row + part.shape[0], :] = part
        row += part.shape[0]


def enc_attn_kernel(pos, x, seg_row, seg_col, gain, own, core, d_x, e_x, d_c, e_c, middle, qkv, probs, mixed, far):
    side = pos[1]
    half = d_x.shape[0]
    per = own.shape[0] // 4 // HEAD_DIM
    rows = 3 * per * HEAD_DIM
    for at, (first, second) in enumerate(((d_x, e_x), (d_c, e_c))):
        far[at, pl.ds(pl.multiple_of(side * half, half), half), :] = first[...]
        far[at, pl.ds(pl.multiple_of((1 - side) * half, half), half), :] = second[...]
    value = x[...].astype(F32)
    normed, _ = norm(value)
    low = (normed * gain[...]).astype(BF)
    packs = (own, core, far.at[0], far.at[1])
    for shard, pack in enumerate(packs):
        qkv[shard * rows : (shard + 1) * rows, :] = nt(pack[:rows, :], low).astype(BF)
    attend(qkv, probs, mixed, seg_col[...] == seg_row[...], per, HEAD_DIM)
    total = value
    for shard, pack in enumerate(packs):
        total = total + tn(mixed[shard * rows // 3 : (shard + 1) * rows // 3, :], pack[rows:, :])
    middle[...] = total


def hidden_pieces(side, mats, width):
    half = width // 2
    own, core, d_x, e_x, d_c, e_c = mats
    first, second = side * half, (1 - side) * half
    return (
        (own, 0, width), (core, width, width),
        (d_x, 2 * width + first, half), (e_x, 2 * width + second, half),
        (d_c, 3 * width + first, half), (e_c, 3 * width + second, half),
    )


def columns(first, size):
    return pl.ds(first if isinstance(first, int) else pl.multiple_of(first, 128), size)


def enc_up_forward_kernel(pos, middle, gain, *refs):
    ups, (hidden, slope) = refs[:6], refs[6:]
    width = ups[0].shape[1]
    normed, _ = norm(middle[...])
    low = (normed * gain[...]).astype(BF)
    for up, first, size in hidden_pieces(pos[1], ups, width):
        act, back = gelu_parts(nn(low, up[...]))
        hidden[:, columns(first, size)] = act.astype(BF)
        slope[:, columns(first, size)] = back.astype(BF)


def enc_down_forward_kernel(pos, middle, hidden, *refs):
    downs, out = refs[:6], refs[6]
    total = middle[...]
    for down, first, size in hidden_pieces(pos[1], downs, downs[0].shape[0]):
        total = total + nn(hidden[:, columns(first, size)], down[...])
    out[...] = total.astype(BF)


def pred_kernel(
    pos, enc, seg_row, seg_col, masked, token, gain_one, gain_two, cot, rows_at,
    p_own, p_core, p_x, p_xc,
    pred_out, stats, g_mine, g_theirs, d_embedded, d_enc, d_gains,
    w_qkv, w_out, w_embed, w_up, w_down, qkv, probs, mixed, d_mixed, d_qkv,
):
    me = pos[0]
    length = cot.shape[0]
    cols = w_out.shape[0] // SHARDS
    hid = w_down.shape[0] // SHARDS
    segments = Segments(w_out.shape[0], 4 * cols + 2 * hid)
    per = cols // P_HEAD_DIM
    width = w_out.shape[1]
    for shard, pack in enumerate((p_own, p_core, p_x, p_xc)):
        w_qkv[shard * 3 * cols : (shard + 1) * 3 * cols, :] = pack[: 3 * cols, :]
        w_out[shard * cols : (shard + 1) * cols, :] = pack[3 * cols : 4 * cols, :]
        at = pl.ds(pl.multiple_of((me ^ shard) * cols, 16), cols)
        w_embed[at, :width] = pack[4 * cols : 5 * cols, :]
        w_embed[at, width:] = pack[5 * cols : 6 * cols, :]
        w_up[:, shard * hid : (shard + 1) * hid] = pack[6 * cols : 6 * cols + width, :]
        w_down[shard * hid : (shard + 1) * hid, :] = pack[6 * cols + width :, :]

    hidden_mask = masked[...] > 0.0
    start = jnp.where(hidden_mask, token[...], nt(enc[...], w_embed[...]))
    n_one, r_one = norm(start)
    a = (n_one * gain_one[...]).astype(BF)
    qkv[...] = nt(w_qkv[...], a).astype(BF)
    attend(qkv, probs, mixed, seg_col[...] == seg_row[...], per, P_HEAD_DIM)
    middle = start + tn(mixed[...], w_out[...])
    n_two, r_two = norm(middle)
    b = (n_two * gain_two[...]).astype(BF)
    act, slope = gelu_parts(nn(b, w_up[...]))
    act = act.astype(BF)
    predicted = middle + nn(act, w_down[...])
    for at, block in enumerate(units(predicted)):
        pred_out[at * length : (at + 1) * length, :] = block.astype(BF)
    stats[...] = jnp.zeros_like(stats)
    stats[0:1, :] = jnp.sum(predicted, 0, keepdims=True)
    stats[1:2, :] = jnp.sum(predicted * predicted, 0, keepdims=True)

    homes = ((g_mine, 0), (g_theirs, 0), (g_mine, 1), (g_theirs, 1))
    grad_low = cot[...]
    d_pre = (nt(grad_low, w_down[...]) * slope).astype(BF)
    source = rows_at[...]
    grad_turned, b_turned = turned(source, grad_low), turned(source, b)
    for shard, (home, at) in enumerate(homes):
        cut = slice(shard * hid, (shard + 1) * hid)
        blocks = units(nn(b_turned, d_pre[:, cut])) + units(nn(grad_turned, act[:, cut]))
        for block, value in enumerate(blocks):
            segments.put(home, at, 4 * cols // 128 + block, value)
    d_middle, d_gain_two = norm_back(n_two, r_two, gain_two[...], nt(d_pre, w_up[...]))
    grad_mid = grad_low.astype(F32) + d_middle
    mid_low = grad_mid.astype(BF)
    d_mixed[...] = nt(w_out[...], mid_low).astype(BF)
    attend_back(qkv, probs, d_mixed, d_qkv, per, P_HEAD_DIM)
    a_turned, mid_turned = turned(source, a), turned(source, mid_low)
    for shard, (home, at) in enumerate(homes):
        g_qkv = nt(a_turned, d_qkv[shard * 3 * cols : (shard + 1) * 3 * cols, :])
        g_out = nt(mid_turned, mixed[shard * cols : (shard + 1) * cols, :])
        for block, value in enumerate(units(jnp.concatenate([g_qkv, g_out], 1))):
            segments.put(home, at, block, value)
    d_value, d_gain_one = norm_back(n_one, r_one, gain_one[...], tn(d_qkv[...], w_qkv[...]))
    d_start = grad_mid + d_value
    d_gains[...] = jnp.zeros_like(d_gains)
    d_gains[0:1, :] = d_gain_one
    d_gains[1:2, :] = d_gain_two
    d_gains[2:3, :] = jnp.sum(jnp.where(hidden_mask, d_start, 0.0), 0, keepdims=True)
    d_low = jnp.where(hidden_mask, 0.0, d_start).astype(BF)
    d_embedded[...] = d_low
    d_enc[...] = nn(d_low, w_embed[...])


def enc_down_kernel(pos, rows_at, grad, hidden, mine, theirs):
    width = hidden.shape[1] // SHARDS
    segments = Segments(grad.shape[1], width)
    grad_turned = turned(rows_at[...], grad[...].astype(BF))
    for shard, (home, at) in ((1, (theirs, 0)), (3, (theirs, 1)), (0, (mine, 0)), (2, (mine, 1))):
        for block, value in enumerate(units(nn(grad_turned, hidden[:, shard * width : (shard + 1) * width]))):
            segments.put(home, at, block, value)


def enc_up_kernel(pos, rows_at, grad, middle, gain, slope, *refs):
    ups, downs, (mine, theirs, grad_mid, d_gain) = refs[:6], refs[6:12], refs[12:]
    width = ups[0].shape[1]
    value = middle[...]
    segments = Segments(value.shape[1], width)
    n_two, r_two = norm(value)
    b_turned = turned(rows_at[...], (n_two * gain[...]).astype(BF))
    homes = ((mine, 0), (theirs, 0), (mine, 1), (theirs, 1))
    low = grad[...].astype(BF)
    d_b = jnp.zeros_like(value)
    pieces = hidden_pieces(pos[1], ups, width)
    for piece in (1, 4, 5, 0, 2, 3):
        up, first, size = pieces[piece]
        shard = (0, 1, 2, 2, 3, 3)[piece]
        d_pre = (nt(low, downs[piece][...]) * slope[:, columns(first, size)].astype(F32)).astype(BF)
        d_b = d_b + nt(d_pre, up[...])
        home, at = homes[shard]
        first_block = (first - shard * width) // 128
        for block, part in enumerate(units(nn(b_turned, d_pre))):
            segments.put(home, at, first_block + block, part)
    d_middle, d_gain_two = norm_back(n_two, r_two, gain[...], d_b)
    grad_mid[...] = grad[...] + d_middle
    d_gain[...] = d_gain_two


def enc_attn_back_kernel(
    pos, rows_at, x, gain, grad, qkv, probs, mixed, d_embedded, enc, d_gain_two, p_rows_at, p_d_gains, own, core, d_x, e_x, d_c, e_c,
    mine, theirs, d_input, far, d_mixed, d_qkv,
):
    me, side = pos[0], pos[1]
    half = d_x.shape[0]
    per = own.shape[0] // 4 // HEAD_DIM
    cols = per * HEAD_DIM
    for at, (first, second) in enumerate(((d_x, e_x), (d_c, e_c))):
        far[at, pl.ds(pl.multiple_of(side * half, half), half), :] = first[...]
        far[at, pl.ds(pl.multiple_of((1 - side) * half, half), half), :] = second[...]
    packs = (own, core, far.at[0], far.at[1])
    low = grad[...].astype(BF)
    for shard, pack in enumerate(packs):
        d_mixed[shard * cols : (shard + 1) * cols, :] = nt(pack[3 * cols :, :], low).astype(BF)
    attend_back(qkv, probs, d_mixed, d_qkv, per, HEAD_DIM)
    value = x[...].astype(F32)
    length, width = value.shape
    normed, inverse = norm(value)
    d_a = jnp.zeros_like(value)
    for shard in range(SHARDS):
        d_a = d_a + tn(d_qkv[shard * 3 * cols : (shard + 1) * 3 * cols, :], packs[shard][: 3 * cols, :])
    d_value, d_gain_one = norm_back(normed, inverse, gain[...], d_a)
    for at, block in enumerate(units(grad[...] + d_value)):
        d_input[at * length : (at + 1) * length, :] = block.astype(BF)

    source = rows_at[...]
    a_turned = turned(source, (normed * gain[...]).astype(BF))
    mid_turned = turned(source, low)
    channels = d_embedded.shape[1]
    e_cols = channels // SHARDS
    row = lax.broadcasted_iota(jnp.int32, (channels, SHARDS * 128), 0)
    column = lax.broadcasted_iota(jnp.int32, (channels, SHARDS * 128), 1)
    within = column & 127
    one_hot = ((((column >> 7) ^ me) * e_cols + within == row) & (within < e_cols)).astype(BF)
    g_embed = nn(turned(source, enc[...]), nn(d_embedded[...], one_hot).astype(BF))
    line = lax.broadcasted_iota(jnp.int32, (8, width), 0)
    lines = jnp.where(line == 0, d_gain_one, jnp.where(line == 1, d_gain_two[...], 0.0)).astype(BF)
    lane = lax.broadcasted_iota(jnp.int32, (8, 128), 1) - lax.broadcasted_iota(jnp.int32, (8, 128), 0)
    p_one_hot = (lax.broadcasted_iota(jnp.int32, (width, channels), 1) == p_rows_at[...]).astype(BF)
    g_small = nn(turned(source, lines), (lane == e_cols).astype(BF)) + nn(
        nt(p_one_hot, p_d_gains[...].astype(BF)).astype(BF), (lane == e_cols + 2).astype(BF)
    )

    segments = Segments(width, 4 * cols + 128)
    homes = ((mine, 0), (theirs, 0), (mine, 1), (theirs, 1))
    for shard in (1, 3, 0, 2):
        home, at = homes[shard]
        g_qkv = nt(a_turned, d_qkv[shard * 3 * cols : (shard + 1) * 3 * cols, :])
        g_out = nt(mid_turned, mixed[shard * cols : (shard + 1) * cols, :])
        blocks = units(jnp.concatenate([g_qkv, g_out], 1)) + [g_embed[:, shard * 128 : (shard + 1) * 128] + g_small]
        for block, part in enumerate(blocks):
            segments.put(home, at, block, part)


def in_order_kernel(pos, own, core, x, xc, out):
    length = out.shape[1]
    for shard, ref in enumerate((own, core, x, xc)):
        for at in range(out.shape[2] // 128):
            out[pos[0] ^ shard, :, at * 128 : (at + 1) * 128] = ref[at * length : (at + 1) * length, :]


def swap(value, axis, bit):
    size = lax.axis_size(axis)
    return lax.ppermute(value, axis, [(i, i ^ bit) for i in range(size)])


def pick(value, index, axis=0):
    return lax.dynamic_index_in_dim(value, index, axis, keepdims=False)


def send_last(kept, segments):
    size = lax.axis_size("dp")
    groups = [[i for i in range(size) if i % 2 == side] for side in range(2)]
    kept = kept.reshape(segments.left + segments.right, size // 2, -1, 128)
    return lax.all_to_all(jnp.swapaxes(kept, 0, 1), "dp", 0, 0, axis_index_groups=groups, tiled=True)


def summed(parts):
    total = jnp.sum(parts.astype(F32), 0)
    return jnp.swapaxes(total, 0, 1).reshape(total.shape[1], -1)


def source_rows(width, side):
    size = lax.axis_size("dp")
    blocks = jnp.arange(width, dtype=jnp.int32).reshape(size // 2, 2, width // size)
    order = jnp.where(side == 0, blocks, blocks[:, ::-1])
    return jnp.swapaxes(order, 0, 1).reshape(width, 1)


def body(
    patches, segment_ids, mask_slots, gain_attn, qkv_weight, out_weight, gain_mlp, up_weight, down_weight,
    embed_weight, mask_token, pred_gain_attn, pred_qkv, pred_out, pred_gain_mlp, pred_up, pred_down, cotangent,
):
    me = lax.axis_index("mp")
    side = lax.axis_index("dp") % 2
    dp_size = lax.axis_size("dp")
    length, width = patches.shape[1:]
    channels = cotangent.shape[2]
    cols, hid = qkv_weight.shape[2], up_weight.shape[1]
    p_cols, p_hid = pred_qkv.shape[2], pred_up.shape[1]
    heads = SHARDS * cols // HEAD_DIM
    p_heads = SHARDS * p_cols // P_HEAD_DIM
    pos = jnp.stack([me, side]).astype(jnp.int32)

    attn_own, attn_direct = call(
        pack_attn_kernel, [((4 * cols, width), BF), ((2 * cols, width), BF)],
        (pos, jnp.swapaxes(qkv_weight, 1, 2), out_weight), 1,
    )
    up_direct, down_direct, p_own = call(
        pack_rest_kernel,
        [((width, hid // 2), BF), ((hid // 2, width), BF), ((6 * p_cols + channels + p_hid, channels), BF)],
        (pos, up_weight, down_weight, jnp.swapaxes(pred_qkv, 1, 2), pred_out, embed_weight.T, pred_up, pred_down), 3,
        tokens=(attn_direct,),
    )

    attn_core, up_core, down_core = swap(attn_own, "mp", 1), swap(up_weight, "mp", 1), swap(down_weight, "mp", 1)
    p_core = swap(p_own, "mp", 1)
    attn_x = swap(attn_direct, "mp", 2)
    attn_x, up_direct = gate([attn_x, up_direct], [p_own])
    up_x = swap(up_direct, "mp", 2)
    attn_y = swap(attn_x, "dp", 1)
    (down_direct,) = gate([down_direct], [up_x])
    down_x = swap(down_direct, "mp", 2)
    up_y = swap(up_x, "dp", 1)
    (p_send,) = gate([p_own], [down_x])
    p_x = swap(p_send, "mp", 2)
    attn = (attn_own, attn_core, attn_x, attn_y, swap(attn_x, "mp", 1), swap(attn_y, "mp", 1))

    x = pick(patches, me)
    segments = pick(segment_ids, me)
    seg_row, seg_col = segments[None, :], segments[:, None]
    slots = pick(mask_slots, me)
    masked = jnp.any(jnp.arange(length, dtype=jnp.int32)[:, None] == slots[None, :], -1, keepdims=True).astype(F32)
    cot = pick(cotangent, me)
    row = lambda gain: gain.astype(F32)[None, :]
    rows_at, p_rows_at = source_rows(width, side), source_rows(channels, side)
    n_rows, n_small = width // dp_size, channels // dp_size
    small_rows_at = rows_at // n_rows * n_small + rows_at % n_small

    middle, qkv, probs, mixed = call(
        enc_attn_kernel,
        [((length, width), F32), ((3 * width, length), BF), ((heads, length, length), BF), ((width, length), BF)],
        (pos, x, seg_row, seg_col, row(gain_attn)) + attn, 9,
        [((2, 4 * cols, width), BF)],
    )
    (up_y,) = gate([up_y], [middle])
    up = (up_weight, up_core, up_x, up_y, swap(up_x, "mp", 1), swap(up_y, "mp", 1))
    down_y = swap(down_x, "dp", 1)
    hidden, slope = call(
        enc_up_forward_kernel, [((length, SHARDS * hid), BF), ((length, SHARDS * hid), BF)],
        (pos, middle, row(gain_mlp)) + up, 6,
    )
    (down_y,) = gate([down_y], [hidden])
    down = (down_weight, down_core, down_x, down_y, swap(down_x, "mp", 1), swap(down_y, "mp", 1))
    (enc,) = call(enc_down_forward_kernel, [((length, width), BF)], (pos, middle, hidden) + down, 4)
    p_packs = (p_send, p_core, p_x, swap(p_x, "mp", 1))
    p_seg, d_seg = Segments(channels, 4 * p_cols + 2 * p_hid), Segments(width, hid)
    u_seg, a_seg = Segments(width, hid), Segments(width, 4 * cols + 128)
    p_blocks, x_blocks = channels // 128, width // 128
    predicted, stats, p_mine, p_theirs, d_embedded, d_enc, p_d_gains = call(
        pred_kernel,
        [((p_blocks * length, 128), BF), ((8, channels), F32), (p_seg.shape, BF), (p_seg.shape, BF), ((length, channels), BF),
         ((length, width), F32), ((8, channels), F32)],
        (pos, enc, seg_row, seg_col, masked, row(mask_token), row(pred_gain_attn), row(pred_gain_mlp), cot, p_rows_at)
        + p_packs, 30,
        [((3 * channels, channels), BF), ((channels, channels), BF), ((channels, width), BF),
         ((channels, SHARDS * p_hid), BF), ((SHARDS * p_hid, channels), BF), ((3 * channels, length), BF),
         ((p_heads, length, length), BF), ((channels, length), BF), ((channels, length), BF),
         ((3 * channels, length), BF)],
    )

    def first(own, seg):
        return [(g, *seg.over_x) for g in own], [(g, *seg.over_y) for g in own]

    def second(own, seg, got):
        return [(g, *seg.then_x) for g in own] + [(got[1][0], got[1][1] + seg.b, seg.b)], [
            (g, *seg.then_y) for g in own
        ] + [(got[0][0], got[0][1] + seg.a, seg.a)]

    def kept(own, seg, got, then):
        return [[(g, *seg.keep_left) for g in own] + [(*got[0], seg.a), (*then[1], seg.a)],
                [(g, *seg.keep_right) for g in own] + [(*got[1], seg.b), (*then[0], seg.b)]]

    def stage(parts, tokens, micros, sums=()):
        send = combine([[x for x, _ in parts], [y for _, y in parts]], tokens, micros, sums)
        got, at = (swap(send[0], "mp", 2), swap(send[1], "dp", 1)), [0, 0]
        places = []
        for x, y in parts:
            places.append(((got[0], at[0]), (got[1], at[1])))
            at = [at[0] + x[0][2], at[1] + y[0][2]]
        return send[:2], got, places, send[2] if sums else None

    p_away, stats_got = swap(p_theirs, "mp", 1), swap(stats, "mp", 1)
    d_mine, d_theirs = call(enc_down_kernel, [(d_seg.shape, BF)] * 2, (pos, rows_at, d_enc, hidden), 30)
    d_away, p_own = swap(d_theirs, "mp", 1), (p_mine, p_away)
    send, p_arrived, p_got, stats = stage([first(p_own, p_seg)], [d_theirs], 30, (stats, stats_got))
    (predicted,) = gate([predicted], send)
    d_own, p_got = (d_mine, d_away), p_got[0]
    stats_got, predicted_x = swap(stats, "dp", 2), swap(predicted, "mp", 2)
    u_mine, u_theirs, grad_mid, d_gain_two = call(
        enc_up_kernel,
        [(u_seg.shape, BF), (u_seg.shape, BF), ((length, width), F32), ((1, width), F32)],
        (pos, rows_at, d_enc, middle, row(gain_mlp), slope) + up + down, 100, tokens=send,
    )
    u_away = swap(u_theirs, "mp", 1)
    predicted_x, d_away = gate([predicted_x, d_away], [u_theirs])
    d_own = (d_mine, d_away)
    send, d_arrived, (d_got, p_then), stats = stage(
        [first(d_own, d_seg), second(p_own, p_seg, p_got)], [u_theirs], 30, (stats, stats_got)
    )
    predicted, predicted_x = gate([predicted, predicted_x], send)
    stats_got, predicted_c, predicted_xc = swap(stats, "dp", dp_size // 2), swap(predicted, "mp", 1), swap(predicted_x, "mp", 1)
    a_mine, a_theirs, d_input = call(
        enc_attn_back_kernel,
        [(a_seg.shape, BF), (a_seg.shape, BF), ((x_blocks * length, 128), BF)],
        (pos, rows_at, x, row(gain_attn), grad_mid, qkv, probs, mixed, d_embedded, enc, d_gain_two, small_rows_at, p_d_gains)
        + attn, 100,
        [((2, 4 * cols, width), BF), ((width, length), BF), ((3 * width, length), BF)], tokens=send,
    )

    a_away = swap(a_theirs, "mp", 1)
    u_away, predicted_c, predicted_xc = gate([u_away, predicted_c, predicted_xc], [a_theirs])
    u_own, a_own = (u_mine, u_away), (a_mine, a_away)
    ud_send, _, (u_got, d_then), stats = stage(
        [first(u_own, u_seg), second(d_own, d_seg, d_got)], [a_theirs, predicted_c, predicted_xc], 60, (stats, stats_got)
    )
    (p_kept,) = combine([kept(p_own, p_seg, p_got, p_then)], ud_send, 30)
    (predictions,) = call(
        in_order_kernel, [((SHARDS, length, channels), BF)], (pos, predicted, predicted_c, predicted_x, predicted_xc), 30,
        tokens=[p_kept],
    )
    stats_got = swap(stats, "mp", 2)
    a_send, _, (a_got,), _ = stage([first(a_own, a_seg)], [*ud_send, predictions], 1)
    p_parts = send_last(p_kept, p_seg)
    u_send, _, (u_then,), stats = stage([second(u_own, u_seg, u_got)], a_send, 1, (stats, stats_got))
    (d_kept,) = combine([kept(d_own, d_seg, d_got, d_then)], u_send, 1)
    p_parts, d_input = gate([p_parts, d_input], u_send)
    stats_got = swap(stats, "dp", 1)
    d_parts = send_last(d_kept, d_seg)
    r_pred = summed(p_parts)
    a_send, _, (a_then,), stats = stage([second(a_own, a_seg, a_got)], [*u_send, r_pred], 1, (stats, stats_got))
    input_x, input_c = swap(d_input, "mp", 2), swap(d_input, "mp", 1)
    (u_kept,) = combine([kept(u_own, u_seg, u_got, u_then)], a_send, 1)
    (d_parts,) = gate([d_parts], a_send)
    for at in range(2, dp_size.bit_length() - 2):
        stats = stats + swap(stats, "dp", 1 << at)
    u_parts = send_last(u_kept, u_seg)
    r_down = summed(d_parts)
    (a_kept,) = combine([kept(a_own, a_seg, a_got, a_then)], [u_kept], 1)
    a_parts = send_last(a_kept, a_seg)
    (patches_grad,) = call(
        in_order_kernel, [((SHARDS, length, width), BF)], (pos, d_input, input_c, input_x, swap(input_x, "mp", 1)), 2,
    )
    r_up, r_attn = summed(u_parts), summed(a_parts)

    count = dp_size * patches.shape[0] * length
    mean, square = stats[0] / count, stats[1] / count
    n_var = channels // SHARDS
    variance = lax.dynamic_slice_in_dim(square - mean * mean, me * n_var, n_var)
    tail = r_attn[:, 4 * cols + p_cols :]

    def qkv_of(block, n):
        return jnp.stack([block[:, i * n : (i + 1) * n] for i in range(3)])

    return (
        predictions,
        patches_grad,
        variance,
        tail[:, 0],
        qkv_of(r_attn, cols),
        r_attn[:, 3 * cols : 4 * cols].T,
        tail[:, 1],
        r_up,
        r_down.T,
        r_attn[:, 4 * cols : 4 * cols + p_cols],
        tail[:n_small, 4],
        tail[:n_small, 2],
        qkv_of(r_pred, p_cols),
        r_pred[:, 3 * p_cols : 4 * p_cols].T,
        tail[:n_small, 3],
        r_pred[:, 4 * p_cols : 4 * p_cols + p_hid],
        r_pred[:, 4 * p_cols + p_hid :].T,
    )


def solution(mesh):
    placed = (
        P("dp", None, None), P("dp", None), P("dp", None), P(), P(None, None, "mp"), P("mp", None), P(),
        P(None, "mp"), P("mp", None), P(None, "mp"), P(), P(), P(None, None, "mp"), P("mp", None), P(),
        P(None, "mp"), P("mp", None), P("dp", None, None),
    )
    return jax.shard_map(
        body,
        mesh=mesh,
        in_specs=placed,
        out_specs=(
            P("dp", None, None), P("dp", None, None), P("mp"), P("dp"), P(None, "dp", "mp"), P("mp", "dp"),
            P("dp"), P("dp", "mp"), P("mp", "dp"), P("dp", "mp"), P("dp"), P("dp"), P(None, "dp", "mp"),
            P("mp", "dp"), P("dp"), P("dp", "mp"), P("mp", "dp"),
        ),
        check_vma=False,
    )
```

```python
import math

import jax
import jax.numpy as jnp
from jax import lax
from jax.experimental import pallas as pl
from jax.experimental.pallas import tpu as pltpu
from jax.sharding import PartitionSpec as P

HEAD_DIM = 64
P_HEAD_DIM = 32
SHARDS = 4
EPS = 1e-06
BF = jnp.bfloat16
F32 = jnp.float32
COST = 1.15e9
VMEM_BYTES = 48 * 1024 * 1024


def contract(left, right, at_left, at_right):
    return lax.dot_general(left, right, (((at_left,), (at_right,)), ((), ())), preferred_element_type=F32)


def nn(left, right):
    return contract(left, right, 1, 0)


def nt(left, right):
    return contract(left, right, 1, 1)


def tn(left, right):
    return contract(left, right, 0, 0)


def norm(value):
    centred = value - jnp.mean(value, -1, keepdims=True)
    inverse = lax.rsqrt(jnp.mean(centred * centred, -1, keepdims=True) + EPS)
    return centred * inverse, inverse


def norm_back(normed, inverse, gain, grad):
    scaled = grad * gain
    along = jnp.mean(scaled * normed, -1, keepdims=True)
    d_value = (scaled - jnp.mean(scaled, -1, keepdims=True) - normed * along) * inverse
    return d_value, jnp.sum(grad * normed, 0, keepdims=True)


def gelu_parts(pre):
    cdf = 0.5 * (1.0 + lax.erf(pre * 0.7071067811865476))
    density = 0.3989422804014327 * jnp.exp(-0.5 * pre * pre)
    return pre * cdf, cdf + pre * density


def turned(source_rows, value):
    width = value.shape[1]
    one_hot = (lax.broadcasted_iota(jnp.int32, (width, width), 1) == source_rows).astype(BF)
    return nt(one_hot, value).astype(BF)


def head_rows(head, per, head_dim):
    shard = head // per
    first = shard * (3 * per * head_dim) + (head - shard * per) * head_dim
    return [pl.ds(pl.multiple_of(first + part * per * head_dim, head_dim), head_dim) for part in range(3)]


def attend(qkv_ref, probs_ref, mixed_ref, same, per, head_dim):
    factor = head_dim ** (-0.5) * math.log2(math.e)

    def one_head(head, carry):
        q_at, k_at, u_at = head_rows(head, per, head_dim)
        scores = jnp.where(same, tn(qkv_ref[k_at, :], qkv_ref[q_at, :]), -1e9)
        top = jnp.max(scores, 0, keepdims=True)
        expd = jnp.exp2((scores - top) * factor)
        probs = (expd * (1.0 / jnp.sum(expd, 0, keepdims=True))).astype(BF)
        probs_ref[head] = probs
        at = pl.ds(pl.multiple_of(head * head_dim, head_dim), head_dim)
        mixed_ref[at, :] = nn(qkv_ref[u_at, :], probs).astype(BF)
        return carry

    lax.fori_loop(0, SHARDS * per, one_head, 0, unroll=2)


def attend_back(qkv_ref, probs_ref, d_mixed_ref, d_qkv_ref, per, head_dim):
    scale = head_dim ** (-0.5)

    def one_head(head, carry):
        q_at, k_at, u_at = head_rows(head, per, head_dim)
        at = pl.ds(pl.multiple_of(head * head_dim, head_dim), head_dim)
        d_mixed = d_mixed_ref[at, :]
        low = probs_ref[head]
        probs = low.astype(F32)
        d_probs = tn(qkv_ref[u_at, :], d_mixed)
        along = jnp.sum(d_probs * probs, 0, keepdims=True)
        d_scores = (probs * (d_probs - along)).astype(BF)
        d_qkv_ref[q_at, :] = (nn(qkv_ref[k_at, :], d_scores) * scale).astype(BF)
        d_qkv_ref[k_at, :] = (nt(qkv_ref[q_at, :], d_scores) * scale).astype(BF)
        d_qkv_ref[u_at, :] = nt(d_mixed, low).astype(BF)
        return carry

    lax.fori_loop(0, SHARDS * per, one_head, 0, unroll=2)


ANYWHERE = pl.BlockSpec(memory_space=pl.ANY)


def in_hbm(arrays):
    return [pltpu.with_memory_space_constraint(a, pltpu.HBM) if n_bytes(a) >= 256 * 1700 else a for a in arrays]


def n_bytes(array):
    return math.prod(array.shape) * array.dtype.itemsize


ANYWHERE = pl.BlockSpec(memory_space=pl.ANY)


def in_hbm(arrays):
    return [pltpu.with_memory_space_constraint(a, pltpu.HBM) if n_bytes(a) >= 256 * 1700 else a for a in arrays]


def n_bytes(array):
    return math.prod(array.shape) * array.dtype.itemsize


def call(kernel, outs, args, micros, scratch=(), tokens=()):
    shapes = [jax.ShapeDtypeStruct(shape, kind) for shape, kind in outs]
    moved = sum(math.prod(a.shape) * a.dtype.itemsize for a in list(args) + shapes)
    n_args, n_all = len(args), len(args) + len(tokens)
    return pl.pallas_call(
        lambda *refs: kernel(*refs[:n_args], *refs[n_all:]),
        out_shape=shapes,
        in_specs=[pl.BlockSpec(memory_space=pltpu.SMEM)]
        + [pl.BlockSpec(memory_space=pltpu.VMEM)] * (n_args - 1)
        + [ANYWHERE] * len(tokens),
        out_specs=[pl.BlockSpec(memory_space=pltpu.VMEM)] * len(shapes),
        scratch_shapes=[pltpu.VMEM(shape, kind) for shape, kind in scratch],
        compiler_params=pltpu.CompilerParams(vmem_limit_bytes=VMEM_BYTES),
        cost_estimate=pl.CostEstimate(flops=int(micros * COST), bytes_accessed=moved if micros else 0, transcendentals=0),
    )(*args, *in_hbm(tokens))


def gate(values, tokens):
    return pl.pallas_call(
        lambda *refs: None,
        out_shape=[jax.ShapeDtypeStruct(v.shape, v.dtype) for v in values],
        in_specs=[ANYWHERE] * (len(values) + len(tokens)),
        out_specs=[ANYWHERE] * len(values),
        input_output_aliases={at: at for at in range(len(values))},
    )(*in_hbm(values), *in_hbm(tokens))


def units(value):
    return [value[:, at * 128 : (at + 1) * 128] for at in range(value.shape[1] // 128)]


class Segments:
    def __init__(self, rows, cols):
        self.eighth, blocks = rows // 8, cols // 128
        self.left, self.right = blocks // 2, blocks - blocks // 2
        a, b = 4 * self.eighth * self.left, 4 * self.eighth * self.right
        self.over_x, self.over_y = (0, 2 * a), (2 * a, 2 * b)
        self.then_y, self.then_x = (2 * a + 2 * b, a), (3 * a + 2 * b, b)
        self.keep_left, self.keep_right = (3 * a + 3 * b, a), (4 * a + 3 * b, b)
        self.shape = (4 * (a + b), 128)
        self.a, self.b = a, b

    def put(self, refs, shard, block, value):
        a, b, size = self.a, self.b, self.eighth
        if shard:
            starts_left = (self.over_x[0], self.over_x[0] + a)
            starts_right = (self.then_x[0], self.over_y[0] + b)
        else:
            starts_left = (self.keep_left[0], self.then_y[0])
            starts_right = (self.keep_right[0], self.over_y[0])
        is_left = block < self.left
        count, index = (self.left, block) if is_left else (self.right, block - self.left)
        for number in range(8):
            start = (starts_left if is_left else starts_right)[number // 4]
            at = start + (number % 4 * count + index) * size
            for ref in refs:
                if at < ref.shape[0]:
                    ref[at : at + size, :] = value[number * size : (number + 1) * size].astype(BF)
                    break
                at -= ref.shape[0]

    def parts(self):
        return [((size, 128), BF) for size in (self.over_x[1], self.over_y[1], 2 * (self.a + self.b))]


def combine(outs, tokens, micros, sums=(), kind=BF):
    arrays, terms = [], []
    for segments in outs:
        for parts in segments:
            for array, first, size in parts:
                if not any(array is known for known in arrays):
                    arrays.append(array)
                terms.append((next(i for i, known in enumerate(arrays) if known is array), first, size))
    n_sums, n_arrays, n_out, n_terms = len(sums), len(arrays), len(outs), len(terms)
    n_in = n_sums + n_arrays + len(tokens)
    sizes = [sum(parts[0][2] for parts in segments) for segments in outs]

    def kernel(*refs):
        held, sem = refs[-1 - n_terms : -1], refs[-1]
        copies = [
            pltpu.make_async_copy(refs[n_sums + which].at[pl.ds(first, size), :], held[at], sem.at[at])
            for at, (which, first, size) in enumerate(terms)
        ]
        for copy in copies:
            copy.start()
        if sums:
            refs[n_in + n_out][...] = refs[0][...] + refs[1][...]
        at = 0
        for out, segments in zip(refs[n_in:], outs):
            row = 0
            for parts in segments:
                size = parts[0][2]
                mine = list(range(at, at + len(parts)))
                for term in mine:
                    copies[term].wait()

                def add(step, carry, row=row, mine=mine, out=out):
                    here = pl.ds(pl.multiple_of(step * 48, 48), 48)
                    total = held[mine[0]][here, :].astype(F32)
                    for term in mine[1:]:
                        total = total + held[term][here, :].astype(F32)
                    out[pl.ds(pl.multiple_of(row + step * 48, 16), 48), :] = total.astype(kind)
                    return carry

                lax.fori_loop(0, size // 48, add, 0, unroll=2)
                at += len(parts)
                row += size

    moved = 256 * (sum(t[2] for t in terms) + sum(sizes))
    in_vmem = pl.BlockSpec(memory_space=pltpu.VMEM)
    return pl.pallas_call(
        kernel,
        out_shape=[jax.ShapeDtypeStruct((size, 128), kind) for size in sizes]
        + ([jax.ShapeDtypeStruct(sums[0].shape, F32)] if sums else []),
        in_specs=[in_vmem] * n_sums + [ANYWHERE] * (n_in - n_sums),
        out_specs=[in_vmem] * (n_out + (1 if sums else 0)),
        scratch_shapes=[pltpu.VMEM((size, 128), BF) for _, _, size in terms] + [pltpu.SemaphoreType.DMA((n_terms,))],
        compiler_params=pltpu.CompilerParams(vmem_limit_bytes=VMEM_BYTES),
        cost_estimate=pl.CostEstimate(flops=int(micros * COST), bytes_accessed=moved if micros else 0, transcendentals=0),
    )(*sums, *in_hbm(arrays), *in_hbm(tokens))


def pack_attn_kernel(pos, qkv, out, own, direct):
    cols = qkv.shape[1]
    for part in range(3):
        own[part * cols : (part + 1) * cols, :] = qkv[part]
    own[3 * cols :, :] = out[...]
    half = direct.shape[0]
    direct[...] = own[pl.ds(pl.multiple_of(pos[1] * half, half), half), :]


def pack_rest_kernel(pos, up, down, qkv, out, embed, p_up, p_down, up_direct, down_direct, pred):
    half = up_direct.shape[1]
    at = pl.ds(pl.multiple_of(pos[1] * half, half), half)
    up_direct[...] = up[:, at]
    down_direct[...] = down[at, :]
    width = pred.shape[1]
    row = 0
    for part in (qkv[0], qkv[1], qkv[2], out[...], embed[:, :width], embed[:, width:], p_up[...], p_down[...]):
        pred[row : row + part.shape[0], :] = part
        row += part.shape[0]


def enc_attn_kernel(pos, x, seg_row, seg_col, gain, own, core, d_x, e_x, d_c, e_c, middle, qkv, probs, mixed, far):
    side = pos[1]
    half = d_x.shape[0]
    per = own.shape[0] // 4 // HEAD_DIM
    rows = 3 * per * HEAD_DIM
    for at, (first, second) in enumerate(((d_x, e_x), (d_c, e_c))):
        far[at, pl.ds(pl.multiple_of(side * half, half), half), :] = first[...]
        far[at, pl.ds(pl.multiple_of((1 - side) * half, half), half), :] = second[...]
    value = x[...].astype(F32)
    normed, _ = norm(value)
    low = (normed * gain[...]).astype(BF)
    packs = (own, core, far.at[0], far.at[1])
    for shard, pack in enumerate(packs):
        qkv[shard * rows : (shard + 1) * rows, :] = nt(pack[:rows, :], low).astype(BF)
    attend(qkv, probs, mixed, seg_col[...] == seg_row[...], per, HEAD_DIM)
    total = value
    for shard, pack in enumerate(packs):
        total = total + tn(mixed[shard * rows // 3 : (shard + 1) * rows // 3, :], pack[rows:, :])
    middle[...] = total


def hidden_pieces(side, mats, width):
    half = width // 2
    own, core, d_x, e_x, d_c, e_c = mats
    first, second = side * half, (1 - side) * half
    return (
        (own, 0, width), (core, width, width),
        (d_x, 2 * width + first, half), (e_x, 2 * width + second, half),
        (d_c, 3 * width + first, half), (e_c, 3 * width + second, half),
    )


def columns(first, size):
    return pl.ds(first if isinstance(first, int) else pl.multiple_of(first, 128), size)


def enc_up_forward_kernel(pos, middle, gain, *refs):
    ups, (hidden, slope) = refs[:6], refs[6:]
    width = ups[0].shape[1]
    normed, _ = norm(middle[...])
    low = (normed * gain[...]).astype(BF)
    for up, first, size in hidden_pieces(pos[1], ups, width):
        act, back = gelu_parts(nn(low, up[...]))
        hidden[:, columns(first, size)] = act.astype(BF)
        slope[:, columns(first, size)] = back.astype(BF)


def enc_down_forward_kernel(pos, middle, hidden, *refs):
    downs, out = refs[:6], refs[6]
    total = middle[...]
    for down, first, size in hidden_pieces(pos[1], downs, downs[0].shape[0]):
        total = total + nn(hidden[:, columns(first, size)], down[...])
    out[...] = total.astype(BF)


def pred_kernel(
    pos, enc, seg_row, seg_col, masked, token, gain_one, gain_two, cot, rows_at,
    p_own, p_core, p_x, p_xc,
    pred_out, stats, g_mine, g_theirs, d_embedded, d_enc, d_gains,
    w_qkv, w_out, w_embed, w_up, w_down, qkv, probs, mixed, d_mixed, d_qkv,
):
    me = pos[0]
    length = cot.shape[0]
    cols = w_out.shape[0] // SHARDS
    hid = w_down.shape[0] // SHARDS
    segments = Segments(w_out.shape[0], 4 * cols + 2 * hid)
    per = cols // P_HEAD_DIM
    width = w_out.shape[1]
    for shard, pack in enumerate((p_own, p_core, p_x, p_xc)):
        w_qkv[shard * 3 * cols : (shard + 1) * 3 * cols, :] = pack[: 3 * cols, :]
        w_out[shard * cols : (shard + 1) * cols, :] = pack[3 * cols : 4 * cols, :]
        at = pl.ds(pl.multiple_of((me ^ shard) * cols, 16), cols)
        w_embed[at, :width] = pack[4 * cols : 5 * cols, :]
        w_embed[at, width:] = pack[5 * cols : 6 * cols, :]
        w_up[:, shard * hid : (shard + 1) * hid] = pack[6 * cols : 6 * cols + width, :]
        w_down[shard * hid : (shard + 1) * hid, :] = pack[6 * cols + width :, :]

    hidden_mask = masked[...] > 0.0
    start = jnp.where(hidden_mask, token[...], nt(enc[...], w_embed[...]))
    n_one, r_one = norm(start)
    a = (n_one * gain_one[...]).astype(BF)
    qkv[...] = nt(w_qkv[...], a).astype(BF)
    attend(qkv, probs, mixed, seg_col[...] == seg_row[...], per, P_HEAD_DIM)
    middle = start + tn(mixed[...], w_out[...])
    n_two, r_two = norm(middle)
    b = (n_two * gain_two[...]).astype(BF)
    act, slope = gelu_parts(nn(b, w_up[...]))
    act = act.astype(BF)
    predicted = middle + nn(act, w_down[...])
    for at, block in enumerate(units(predicted)):
        pred_out[at * length : (at + 1) * length, :] = block.astype(BF)
    stats[...] = jnp.zeros_like(stats)
    stats[0:1, :] = jnp.sum(predicted, 0, keepdims=True)
    stats[1:2, :] = jnp.sum(predicted * predicted, 0, keepdims=True)

    homes = (((g_mine,), 0), ((g_theirs,), 0), ((g_mine,), 1), ((g_theirs,), 1))
    grad_low = cot[...]
    d_pre = (nt(grad_low, w_down[...]) * slope).astype(BF)
    source = rows_at[...]
    grad_turned, b_turned = turned(source, grad_low), turned(source, b)
    for shard, (home, at) in enumerate(homes):
        cut = slice(shard * hid, (shard + 1) * hid)
        blocks = units(nn(b_turned, d_pre[:, cut])) + units(nn(grad_turned, act[:, cut]))
        for block, value in enumerate(blocks):
            segments.put(home, at, 4 * cols // 128 + block, value)
    d_middle, d_gain_two = norm_back(n_two, r_two, gain_two[...], nt(d_pre, w_up[...]))
    grad_mid = grad_low.astype(F32) + d_middle
    mid_low = grad_mid.astype(BF)
    d_mixed[...] = nt(w_out[...], mid_low).astype(BF)
    attend_back(qkv, probs, d_mixed, d_qkv, per, P_HEAD_DIM)
    a_turned, mid_turned = turned(source, a), turned(source, mid_low)
    for shard, (home, at) in enumerate(homes):
        g_qkv = nt(a_turned, d_qkv[shard * 3 * cols : (shard + 1) * 3 * cols, :])
        g_out = nt(mid_turned, mixed[shard * cols : (shard + 1) * cols, :])
        for block, value in enumerate(units(jnp.concatenate([g_qkv, g_out], 1))):
            segments.put(home, at, block, value)
    d_value, d_gain_one = norm_back(n_one, r_one, gain_one[...], tn(d_qkv[...], w_qkv[...]))
    d_start = grad_mid + d_value
    d_gains[...] = jnp.zeros_like(d_gains)
    d_gains[0:1, :] = d_gain_one
    d_gains[1:2, :] = d_gain_two
    d_gains[2:3, :] = jnp.sum(jnp.where(hidden_mask, d_start, 0.0), 0, keepdims=True)
    d_low = jnp.where(hidden_mask, 0.0, d_start).astype(BF)
    d_embedded[...] = d_low
    d_enc[...] = nn(d_low, w_embed[...])


def enc_down_kernel(pos, rows_at, grad, hidden, mine, *theirs):
    width = hidden.shape[1] // SHARDS
    segments = Segments(grad.shape[1], width)
    grad_turned = turned(rows_at[...], grad[...].astype(BF))
    for shard, (home, at) in ((1, (theirs, 0)), (3, (theirs, 1)), (0, ((mine,), 0)), (2, ((mine,), 1))):
        for block, value in enumerate(units(nn(grad_turned, hidden[:, shard * width : (shard + 1) * width]))):
            segments.put(home, at, block, value)


def enc_up_kernel(pos, rows_at, grad, middle, gain, slope, *refs):
    ups, downs, (grad_mid, d_gain, mine), theirs = refs[:6], refs[6:12], refs[12:15], refs[15:]
    side = pos[1]
    width = ups[0].shape[1]
    value = middle[...]
    segments = Segments(value.shape[1], width)
    n_two, r_two = norm(value)
    b_turned = turned(rows_at[...], (n_two * gain[...]).astype(BF))
    homes = (((mine,), 0), (theirs, 0), ((mine,), 1), (theirs, 1))
    low = grad[...].astype(BF)
    d_b = jnp.zeros_like(value)
    pieces = hidden_pieces(side, ups, width)
    for piece in (1, 4, 5, 0, 2, 3):
        up, first, size = pieces[piece]
        home, at = homes[(0, 1, 2, 2, 3, 3)[piece]]
        d_pre = (nt(low, downs[piece][...]) * slope[:, columns(first, size)].astype(F32)).astype(BF)
        d_b = d_b + nt(d_pre, up[...])
        blocks = units(nn(b_turned, d_pre))

        def put(first_block, home=home, at=at, blocks=blocks):
            for block, part in enumerate(blocks):
                segments.put(home, at, first_block + block, part)

        if piece < 2:
            put(0)
        else:
            second_half = side if piece in (2, 4) else 1 - side
            pl.when(second_half == 0)(lambda put=put: put(0))
            pl.when(second_half == 1)(lambda put=put, blocks=blocks: put(len(blocks)))
    d_middle, d_gain_two = norm_back(n_two, r_two, gain[...], d_b)
    grad_mid[...] = grad[...] + d_middle
    d_gain[...] = d_gain_two


def enc_attn_back_kernel(
    pos, x, gain, grad, qkv, probs, own, core, d_x, e_x, d_c, e_c, d_qkv, d_input, d_gain, far, d_mixed
):
    side = pos[1]
    half = d_x.shape[0]
    per = own.shape[0] // 4 // HEAD_DIM
    cols = per * HEAD_DIM
    for at, (first, second) in enumerate(((d_x, e_x), (d_c, e_c))):
        far[at, pl.ds(pl.multiple_of(side * half, half), half), :] = first[...]
        far[at, pl.ds(pl.multiple_of((1 - side) * half, half), half), :] = second[...]
    packs = (own, core, far.at[0], far.at[1])
    low = grad[...].astype(BF)
    for shard, pack in enumerate(packs):
        d_mixed[shard * cols : (shard + 1) * cols, :] = nt(pack[3 * cols :, :], low).astype(BF)
    attend_back(qkv, probs, d_mixed, d_qkv, per, HEAD_DIM)
    value = x[...].astype(F32)
    length = value.shape[0]
    normed, inverse = norm(value)
    d_a = jnp.zeros_like(value)
    for shard in range(SHARDS):
        d_a = d_a + tn(d_qkv[shard * 3 * cols : (shard + 1) * 3 * cols, :], packs[shard][: 3 * cols, :])
    d_value, d_gain_one = norm_back(normed, inverse, gain[...], d_a)
    d_gain[...] = d_gain_one
    for at, block in enumerate(units(grad[...] + d_value)):
        d_input[at * length : (at + 1) * length, :] = block.astype(BF)


def enc_attn_weights_kernel(
    pos, rows_at, x, gain, grad, mixed, d_qkv, d_embedded, enc, d_gain_one, d_gain_two, p_d_gains, mine, *theirs
):
    me = pos[0]
    value = x[...].astype(F32)
    width = value.shape[1]
    cols = width // SHARDS
    normed, _ = norm(value)
    source = rows_at[...]
    a_turned = turned(source, (normed * gain[...]).astype(BF))
    mid_turned = turned(source, grad[...].astype(BF))
    channels = d_embedded.shape[1]
    e_cols = channels // SHARDS
    row = lax.broadcasted_iota(jnp.int32, (channels, SHARDS * 128), 0)
    column = lax.broadcasted_iota(jnp.int32, (channels, SHARDS * 128), 1)
    within = column & 127
    one_hot = ((((column >> 7) ^ me) * e_cols + within == row) & (within < e_cols)).astype(BF)
    g_embed = nn(turned(source, enc[...]), nn(d_embedded[...], one_hot).astype(BF))
    line = lax.broadcasted_iota(jnp.int32, (8, width), 0)
    lines = jnp.where(line == 0, d_gain_one[...], jnp.where(line == 1, d_gain_two[...], 0.0)).astype(BF)
    lane = lax.broadcasted_iota(jnp.int32, (8, 128), 1) - lax.broadcasted_iota(jnp.int32, (8, 128), 0)
    n_rows, n_small = pos[2], pos[3]
    device = ((source.astype(F32) + 0.5) / n_rows.astype(F32)).astype(jnp.int32)
    within_device = source - device * n_rows
    p_source = device * n_small + jnp.where(within_device >= n_small, within_device - n_small, within_device)
    p_one_hot = (lax.broadcasted_iota(jnp.int32, (width, channels), 1) == p_source).astype(BF)
    g_small = nn(turned(source, lines), (lane == e_cols).astype(BF)) + nn(
        nt(p_one_hot, p_d_gains[...].astype(BF)).astype(BF), (lane == e_cols + 2).astype(BF)
    )

    segments = Segments(width, 4 * cols + 128)
    homes = (((mine,), 0), (theirs, 0), ((mine,), 1), (theirs, 1))
    for shard in (1, 3, 0, 2):
        home, at = homes[shard]
        g_qkv = nt(a_turned, d_qkv[shard * 3 * cols : (shard + 1) * 3 * cols, :])
        g_out = nt(mid_turned, mixed[shard * cols : (shard + 1) * cols, :])
        blocks = units(jnp.concatenate([g_qkv, g_out], 1)) + [g_embed[:, shard * 128 : (shard + 1) * 128] + g_small]
        for block, part in enumerate(blocks):
            segments.put(home, at, block, part)


def in_order_kernel(pos, own, core, x, xc, out):
    length = out.shape[1]
    for shard, ref in enumerate((own, core, x, xc)):
        for at in range(out.shape[2] // 128):
            out[pos[0] ^ shard, :, at * 128 : (at + 1) * 128] = ref[at * length : (at + 1) * length, :]


def swap(value, axis, bit):
    size = lax.axis_size(axis)
    return lax.ppermute(value, axis, [(i, i ^ bit) for i in range(size)])


def pick(value, index, axis=0):
    return lax.dynamic_index_in_dim(value, index, axis, keepdims=False)


def source_rows(width):
    size = lax.axis_size("dp")
    number = jnp.arange(8, dtype=jnp.int32)
    owner = (lax.axis_index("dp") & 7) ^ (number >> 2 | number & 2 | (number & 1) << 2)
    inner = jnp.arange(width // 8, dtype=jnp.int32).reshape(1, size // 8, width // size)
    high = jnp.arange(size // 8, dtype=jnp.int32)[None, :, None]
    rows = (high * 8 + owner[:, None, None]) * (width // size) + inner % (width // size)
    return rows.reshape(width, 1)


def body(
    patches, segment_ids, mask_slots, gain_attn, qkv_weight, out_weight, gain_mlp, up_weight, down_weight,
    embed_weight, mask_token, pred_gain_attn, pred_qkv, pred_out, pred_gain_mlp, pred_up, pred_down, cotangent,
):
    me = lax.axis_index("mp")
    side = lax.axis_index("dp") % 2
    dp_size = lax.axis_size("dp")
    length, width = patches.shape[1:]
    channels = cotangent.shape[2]
    cols, hid = qkv_weight.shape[2], up_weight.shape[1]
    p_cols, p_hid = pred_qkv.shape[2], pred_up.shape[1]
    heads = SHARDS * cols // HEAD_DIM
    p_heads = SHARDS * p_cols // P_HEAD_DIM
    pos = jnp.stack([me, side, width // dp_size, channels // dp_size]).astype(jnp.int32)

    attn_own, attn_direct = call(
        pack_attn_kernel, [((4 * cols, width), BF), ((2 * cols, width), BF)],
        (pos, jnp.swapaxes(qkv_weight, 1, 2), out_weight), 1,
    )
    up_direct, down_direct, p_own = call(
        pack_rest_kernel,
        [((width, hid // 2), BF), ((hid // 2, width), BF), ((6 * p_cols + channels + p_hid, channels), BF)],
        (pos, up_weight, down_weight, jnp.swapaxes(pred_qkv, 1, 2), pred_out, embed_weight.T, pred_up, pred_down), 3,
        tokens=(attn_direct,),
    )

    attn_core, up_core, down_core = swap(attn_own, "mp", 1), swap(up_weight, "mp", 1), swap(down_weight, "mp", 1)
    p_core = swap(p_own, "mp", 1)
    attn_x = swap(attn_direct, "mp", 2)
    attn_x, up_direct = gate([attn_x, up_direct], [p_own])
    up_x = swap(up_direct, "mp", 2)
    attn_y = swap(attn_x, "dp", 1)
    (down_direct,) = gate([down_direct], [up_x])
    down_x = swap(down_direct, "mp", 2)
    up_y = swap(up_x, "dp", 1)
    (p_send,) = gate([p_own], [down_x])
    p_x = swap(p_send, "mp", 2)
    attn = (attn_own, attn_core, attn_x, attn_y, swap(attn_x, "mp", 1), swap(attn_y, "mp", 1))

    x = pick(patches, me)
    segments = pick(segment_ids, me)
    seg_row, seg_col = segments[None, :], segments[:, None]
    slots = pick(mask_slots, me)
    masked = jnp.any(jnp.arange(length, dtype=jnp.int32)[:, None] == slots[None, :], -1, keepdims=True).astype(F32)
    cot = pick(cotangent, me)
    row = lambda gain: gain.astype(F32)[None, :]
    rows_at, p_rows_at = source_rows(width), source_rows(channels)
    n_rows, n_small = width // dp_size, channels // dp_size

    middle, qkv, probs, mixed = call(
        enc_attn_kernel,
        [((length, width), F32), ((3 * width, length), BF), ((heads, length, length), BF), ((width, length), BF)],
        (pos, x, seg_row, seg_col, row(gain_attn)) + attn, 9,
        [((2, 4 * cols, width), BF)],
    )
    (up_y,) = gate([up_y], [middle])
    up = (up_weight, up_core, up_x, up_y, swap(up_x, "mp", 1), swap(up_y, "mp", 1))
    down_y = swap(down_x, "dp", 1)
    hidden, slope = call(
        enc_up_forward_kernel, [((length, SHARDS * hid), BF), ((length, SHARDS * hid), BF)],
        (pos, middle, row(gain_mlp)) + up, 6,
    )
    (down_y,) = gate([down_y], [hidden])
    down = (down_weight, down_core, down_x, down_y, swap(down_x, "mp", 1), swap(down_y, "mp", 1))
    (enc,) = call(enc_down_forward_kernel, [((length, width), BF)], (pos, middle, hidden) + down, 4)
    p_packs = (p_send, p_core, p_x, swap(p_x, "mp", 1))
    p_seg, d_seg = Segments(channels, 4 * p_cols + 2 * p_hid), Segments(width, hid)
    u_seg, a_seg = Segments(width, hid), Segments(width, 4 * cols + 128)
    p_blocks, x_blocks = channels // 128, width // 128
    predicted, stats, p_mine, p_theirs, d_embedded, d_enc, p_d_gains = call(
        pred_kernel,
        [((p_blocks * length, 128), BF), ((8, channels), F32), (p_seg.shape, BF), (p_seg.shape, BF), ((length, channels), BF),
         ((length, width), F32), ((8, channels), F32)],
        (pos, enc, seg_row, seg_col, masked, row(mask_token), row(pred_gain_attn), row(pred_gain_mlp), cot, p_rows_at)
        + p_packs, 30,
        [((3 * channels, channels), BF), ((channels, channels), BF), ((channels, width), BF),
         ((channels, SHARDS * p_hid), BF), ((SHARDS * p_hid, channels), BF), ((3 * channels, length), BF),
         ((p_heads, length, length), BF), ((channels, length), BF), ((channels, length), BF),
         ((3 * channels, length), BF)],
    )

    def from_core(theirs):
        return [swap(part, "mp", 1) for part in theirs]

    def both(own, at, size):
        mine, away = own
        segments, start = [], 0
        for part in away:
            low, high = max(at, start), min(at + size, start + part.shape[0])
            if low < high:
                segments.append([(mine, low, high - low), (part, low - start, high - low)])
            start += part.shape[0]
        return segments

    def with_term(segments, array, at):
        result = []
        for parts in segments:
            result.append(parts + [(array, at, parts[0][2])])
            at += parts[0][2]
        return result

    def first(own, seg):
        return both(own, *seg.over_x), both(own, *seg.over_y)

    def second(own, seg, got):
        (x, x_at), (y, y_at) = got
        return with_term(both(own, *seg.then_x), y, y_at + seg.b), with_term(both(own, *seg.then_y), x, x_at + seg.a)

    def kept(own, seg, got, then, low, high, extra=()):
        segments = []
        for (start, size), over, after, right in (
            (seg.keep_left, got[0], then[1], 0), (seg.keep_right, got[1], then[0], 1)
        ):
            at, rows = low * size // 4, (high - low) * size // 4
            part = both(own, start + at, rows)
            for array, array_at in (over, after):
                part = with_term(part, array, array_at + at)
            for array, array_at in extra:
                part = with_term(part, array, array_at + right * seg.a * (high - low) // 4)
            segments += part
        return segments

    def stage(parts, tokens, micros, sums=(), z=()):
        outs = [sum((x for x, _ in parts), []), sum((y for _, y in parts), [])] if parts else []
        send = combine(outs + list(z), tokens, micros, sums)
        got, at = ((swap(send[0], "mp", 2), swap(send[1], "dp", 1)) if parts else ()), [0, 0]
        places = []
        for x, y in parts:
            places.append(((got[0], at[0]), (got[1], at[1])))
            at = [at[0] + sum(p[0][2] for p in x), at[1] + sum(p[0][2] for p in y)]
        return send, got, places

    p_away = swap(p_theirs, "mp", 1)
    d_mine, *d_theirs = call(enc_down_kernel, [(d_seg.shape, BF)] + d_seg.parts(), (pos, rows_at, d_enc, hidden), 30)
    p_own, d_own = (p_mine, [p_away]), (d_mine, from_core(d_theirs))
    send, p_arrived, (p_got, d_got, at_predicted) = stage(
        [first(p_own, p_seg), first(d_own, d_seg), ([[(predicted, 0, predicted.shape[0])]], [])], [], 30
    )
    grad_mid, d_gain_two, u_mine, *u_theirs = call(
        enc_up_kernel,
        [((length, width), F32), ((1, width), F32), (u_seg.shape, BF)] + u_seg.parts(),
        (pos, rows_at, d_enc, middle, row(gain_mlp), slope) + up + down, 100, tokens=send,
    )
    u_away = from_core(u_theirs)
    d_qkv, d_input, d_gain_one = call(
        enc_attn_back_kernel,
        [((3 * width, length), BF), ((x_blocks * length, 128), BF), ((1, width), F32)],
        (pos, x, row(gain_attn), grad_mid, qkv, probs) + attn, 1,
        [((2, 4 * cols, width), BF), ((width, length), BF)],
    )
    got_x, got_y, *u_away[:2] = gate([*p_arrived, *u_away[:2]], [d_gain_one])
    moved = lambda places: ((got_x, places[0][1]), (got_y, places[1][1]))
    p_got, d_got, u_own = moved(p_got), moved(d_got), (u_mine, u_away)
    predicted_x = lax.slice_in_dim(got_x, at_predicted[0][1], got_x.shape[0])
    filler = [[(d_input, 0, p_seg.b - p_seg.a)]]
    send, _, (u_got, d_then, p_then, _) = stage(
        [first(u_own, u_seg), second(d_own, d_seg, d_got), second(p_own, p_seg, p_got), ([], filler)], [], 30
    )
    predicted, predicted_x, d_input = gate([predicted, predicted_x, d_input], send)
    a_mine, *a_theirs = call(
        enc_attn_weights_kernel, [(a_seg.shape, BF)] + a_seg.parts(),
        (pos, rows_at, x, row(gain_attn), grad_mid, mixed, d_qkv, d_embedded, enc, d_gain_one, d_gain_two, p_d_gains), 100, tokens=send,
    )
    a_own = (a_mine, from_core(a_theirs))
    a_send, _, (a_got,) = stage([first(a_own, a_seg)], [], 0)
    p_z = (p_own, p_seg, p_got, p_then)
    d_z = (d_own, d_seg, d_got, d_then)
    (*u_send, z_send), _, (u_then,) = stage(
        [second(u_own, u_seg, u_got)], a_send, 3, (), [kept(*p_z, 2, 4) + kept(*d_z, 2, 4)]
    )
    (stats,) = gate([stats], u_send)
    u_z = (u_own, u_seg, u_got, u_then)
    stats_got, z_got = swap(stats, "mp", 1), swap(z_send, "dp", 2)
    p_rows, d_rows, u_rows = ((seg.a + seg.b) // 4 for seg in (p_seg, d_seg, u_seg))
    p_one, d_one = (z_got, 0), (z_got, 2 * p_rows)

    def later(one, seg, quarter):
        array, at = one
        return [(array, at + quarter * seg.a // 4), (array, at + seg.a // 2 + quarter * seg.b // 4)]

    def last(z, one, quarter, two=None):
        own, seg, got, then = z
        segments = []
        lefts_rights = later(one, seg, quarter)
        for part, (start, size), over, after, (array, at), shift in (
            (0, seg.keep_left, got[0], then[1], lefts_rights[0], 0), (1, seg.keep_right, got[1], then[0], lefts_rights[1], seg.a // 4)
        ):
            begin, rows = quarter * size // 4, size // 4
            terms = both(own, start + begin, rows)
            for more, more_at in (over, after):
                terms = with_term(terms, more, more_at + begin)
            terms = with_term(terms, array, at)
            if two is not None:
                terms = with_term(terms, two[0], two[1] + shift)
            segments += terms
        return segments

    (*a_send, z_send, stats), _, (a_then,) = stage(
        [second(a_own, a_seg, a_got)], u_send, 3, (stats, stats_got), [last(p_z, p_one, 1) + last(d_z, d_one, 1)]
    )
    a_z = (a_own, a_seg, a_got, a_then)
    z_got = swap(z_send, "dp", 4)
    (z_send,) = combine([kept(*u_z, 2, 4)], a_send, 3)
    u_one, stats_got = (swap(z_send, "dp", 2), 0), swap(stats, "dp", 2)
    predicted, predicted_x = gate([predicted, predicted_x], [z_send])
    predicted_c, predicted_xc = swap(predicted, "mp", 1), swap(predicted_x, "mp", 1)
    z_send, z_send_u, stats = combine([kept(*a_z, 2, 4), last(u_z, u_one, 1)], [z_send], 3, (stats, stats_got))
    a_one, u_two = (swap(z_send, "dp", 2), 0), (swap(z_send_u, "dp", 4), 0)
    d_input, stats, p_two_array = gate([d_input, stats, z_got], [z_send])
    p_two, d_two = (p_two_array, 0), (p_two_array, p_rows)
    stats_got, input_x, input_c = swap(stats, "dp", 4), swap(d_input, "mp", 2), swap(d_input, "mp", 1)
    p_sum, d_sum = combine([last(p_z, p_one, 0, p_two), last(d_z, d_one, 0, d_two)], [z_send], 3, kind=F32)
    (predictions,) = call(
        in_order_kernel, [((SHARDS, length, channels), BF)], (pos, predicted, predicted_c, predicted_x, predicted_xc), 3,
        tokens=(p_sum,),
    )
    z_send, stats = combine([last(a_z, a_one, 1)], [predictions], 3, (stats, stats_got))
    a_two = (swap(z_send, "dp", 4), 0)
    (input_x,) = gate([input_x], [z_send])
    u_sum, stats = combine([last(u_z, u_one, 0, u_two)], [z_send], 3, (stats, swap(stats, "mp", 2)), kind=F32)
    stats_got = swap(stats, "dp", 1)
    (patches_grad,) = call(
        in_order_kernel, [((SHARDS, length, width), BF)], (pos, d_input, input_c, input_x, swap(input_x, "mp", 1)), 2,
        tokens=(u_sum,),
    )
    a_sum, stats = combine([last(a_z, a_one, 0, a_two)], [patches_grad], 3, (stats, stats_got), kind=F32)
    for at in range(3, dp_size.bit_length() - 1):
        stats = stats + swap(stats, "dp", 1 << at)

    def own_rows(total, seg):
        total = total.reshape(seg.left + seg.right, -1, 128)
        if dp_size > 8:
            groups = [[high * 8 + low for high in range(dp_size // 8)] for low in range(8)]
            total = lax.psum_scatter(total, "dp", scatter_dimension=1, axis_index_groups=groups, tiled=True)
        return jnp.swapaxes(total, 0, 1).reshape(total.shape[1], -1)

    r_pred, r_down, r_up, r_attn = (
        own_rows(total, seg) for total, seg in ((p_sum, p_seg), (d_sum, d_seg), (u_sum, u_seg), (a_sum, a_seg))
    )

    count = dp_size * patches.shape[0] * length
    mean, square = stats[0] / count, stats[1] / count
    n_var = channels // SHARDS
    variance = lax.dynamic_slice_in_dim(square - mean * mean, me * n_var, n_var)
    tail = r_attn[:, 4 * cols + p_cols :]

    def qkv_of(block, n):
        return jnp.stack([block[:, i * n : (i + 1) * n] for i in range(3)])

    return (
        predictions,
        patches_grad,
        variance,
        tail[:, 0],
        qkv_of(r_attn, cols),
        r_attn[:, 3 * cols : 4 * cols].T,
        tail[:, 1],
        r_up,
        r_down.T,
        r_attn[:, 4 * cols : 4 * cols + p_cols],
        tail[:n_small, 4],
        tail[:n_small, 2],
        qkv_of(r_pred, p_cols),
        r_pred[:, 3 * p_cols : 4 * p_cols].T,
        tail[:n_small, 3],
        r_pred[:, 4 * p_cols : 4 * p_cols + p_hid],
        r_pred[:, 4 * p_cols + p_hid :].T,
    )


def solution(mesh):
    placed = (
        P("dp", None, None), P("dp", None), P("dp", None), P(), P(None, None, "mp"), P("mp", None), P(),
        P(None, "mp"), P("mp", None), P(None, "mp"), P(), P(), P(None, None, "mp"), P("mp", None), P(),
        P(None, "mp"), P("mp", None), P("dp", None, None),
    )
    return jax.shard_map(
        body,
        mesh=mesh,
        in_specs=placed,
        out_specs=(
            P("dp", None, None), P("dp", None, None), P("mp"), P("dp"), P(None, "dp", "mp"), P("mp", "dp"),
            P("dp"), P("dp", "mp"), P("mp", "dp"), P("dp", "mp"), P("dp"), P("dp"), P(None, "dp", "mp"),
            P("mp", "dp"), P("dp"), P("dp", "mp"), P("mp", "dp"),
        ),
        check_vma=False,
    )
```

```python
import math
from functools import partial

import jax
import jax.numpy as jnp
from jax import lax
from jax.experimental import pallas as pl
from jax.experimental.pallas import tpu as pltpu
from jax.sharding import PartitionSpec as P

HEAD_DIM = 64
P_HEAD_DIM = 32
SHARDS = 4
EPS = 1e-06
BF = jnp.bfloat16
F32 = jnp.float32
COST = 1.15e9
VMEM_BYTES = 48 * 1024 * 1024


def contract(left, right, at_left, at_right):
    return lax.dot_general(left, right, (((at_left,), (at_right,)), ((), ())), preferred_element_type=F32)


def nn(left, right):
    return contract(left, right, 1, 0)


def nt(left, right):
    return contract(left, right, 1, 1)


def tn(left, right):
    return contract(left, right, 0, 0)


def norm(value):
    centred = value - jnp.mean(value, -1, keepdims=True)
    inverse = lax.rsqrt(jnp.mean(centred * centred, -1, keepdims=True) + EPS)
    return centred * inverse, inverse


def norm_back(normed, inverse, gain, grad):
    scaled = grad * gain
    along = jnp.mean(scaled * normed, -1, keepdims=True)
    d_value = (scaled - jnp.mean(scaled, -1, keepdims=True) - normed * along) * inverse
    return d_value, jnp.sum(grad * normed, 0, keepdims=True)


def gelu_parts(pre):
    cdf = 0.5 * (1.0 + lax.erf(pre * 0.7071067811865476))
    density = 0.3989422804014327 * jnp.exp(-0.5 * pre * pre)
    return pre * cdf, cdf + pre * density


def turned(source_rows, value):
    width = value.shape[1]
    one_hot = (lax.broadcasted_iota(jnp.int32, (width, width), 1) == source_rows).astype(BF)
    return nt(one_hot, value).astype(BF)


def head_rows(head, per, head_dim):
    shard = head // per
    first = shard * (3 * per * head_dim) + (head - shard * per) * head_dim
    return [pl.ds(pl.multiple_of(first + part * per * head_dim, head_dim), head_dim) for part in range(3)]


def attend(qkv_ref, probs_ref, mixed_ref, same, per, head_dim):
    factor = head_dim ** (-0.5) * math.log2(math.e)

    def one_head(head, carry):
        q_at, k_at, u_at = head_rows(head, per, head_dim)
        scores = jnp.where(same, tn(qkv_ref[k_at, :], qkv_ref[q_at, :]), -1e9)
        top = jnp.max(scores, 0, keepdims=True)
        expd = jnp.exp2((scores - top) * factor)
        probs = (expd * (1.0 / jnp.sum(expd, 0, keepdims=True))).astype(BF)
        probs_ref[head] = probs
        at = pl.ds(pl.multiple_of(head * head_dim, head_dim), head_dim)
        mixed_ref[at, :] = nn(qkv_ref[u_at, :], probs).astype(BF)
        return carry

    lax.fori_loop(0, SHARDS * per, one_head, 0, unroll=4)


def attend_back(qkv_ref, probs_ref, d_mixed_ref, d_qkv_ref, per, head_dim):
    scale = head_dim ** (-0.5)

    def one_head(head, carry):
        q_at, k_at, u_at = head_rows(head, per, head_dim)
        at = pl.ds(pl.multiple_of(head * head_dim, head_dim), head_dim)
        d_mixed = d_mixed_ref[at, :]
        low = probs_ref[head]
        probs = low.astype(F32)
        d_probs = tn(qkv_ref[u_at, :], d_mixed)
        along = jnp.sum(d_probs * probs, 0, keepdims=True)
        d_scores = (probs * (d_probs - along)).astype(BF)
        d_qkv_ref[q_at, :] = (nn(qkv_ref[k_at, :], d_scores) * scale).astype(BF)
        d_qkv_ref[k_at, :] = (nt(qkv_ref[q_at, :], d_scores) * scale).astype(BF)
        d_qkv_ref[u_at, :] = nt(d_mixed, low).astype(BF)
        return carry

    lax.fori_loop(0, SHARDS * per, one_head, 0, unroll=4)


ANYWHERE = pl.BlockSpec(memory_space=pl.ANY)


def in_hbm(arrays, least=256 * 1700):
    return [pltpu.with_memory_space_constraint(a, pltpu.HBM) if n_bytes(a) >= least else a for a in arrays]


def n_bytes(array):
    return math.prod(array.shape) * array.dtype.itemsize


ANYWHERE = pl.BlockSpec(memory_space=pl.ANY)


def in_hbm(arrays, least=256 * 1700):
    return [pltpu.with_memory_space_constraint(a, pltpu.HBM) if n_bytes(a) >= least else a for a in arrays]


def n_bytes(array):
    return math.prod(array.shape) * array.dtype.itemsize


def call(kernel, outs, args, micros, scratch=(), tokens=()):
    shapes = [jax.ShapeDtypeStruct(shape, kind) for shape, kind in outs]
    moved = sum(math.prod(a.shape) * a.dtype.itemsize for a in list(args) + shapes)
    n_args, n_all = len(args), len(args) + len(tokens)
    return pl.pallas_call(
        lambda *refs: kernel(*refs[:n_args], *refs[n_all:]),
        out_shape=shapes,
        in_specs=[pl.BlockSpec(memory_space=pltpu.SMEM)]
        + [pl.BlockSpec(memory_space=pltpu.VMEM)] * (n_args - 1)
        + [ANYWHERE] * len(tokens),
        out_specs=[pl.BlockSpec(memory_space=pltpu.VMEM)] * len(shapes),
        scratch_shapes=[pltpu.VMEM(shape, kind) for shape, kind in scratch],
        compiler_params=pltpu.CompilerParams(vmem_limit_bytes=VMEM_BYTES),
        cost_estimate=pl.CostEstimate(flops=int(micros * COST), bytes_accessed=moved if micros else 0, transcendentals=0),
    )(*args, *in_hbm(tokens, 0))


def gate(values, tokens):
    return pl.pallas_call(
        lambda *refs: None,
        out_shape=[jax.ShapeDtypeStruct(v.shape, v.dtype) for v in values],
        in_specs=[ANYWHERE] * (len(values) + len(tokens)),
        out_specs=[ANYWHERE] * len(values),
        input_output_aliases={at: at for at in range(len(values))},
    )(*in_hbm(values), *in_hbm(tokens, 0))


def units(value):
    return [value[:, at * 128 : (at + 1) * 128] for at in range(value.shape[1] // 128)]


class Segments:
    def __init__(self, rows, cols):
        self.eighth, blocks = rows // 8, cols // 128
        self.left, self.right = blocks // 2, blocks - blocks // 2
        a, b = 4 * self.eighth * self.left, 4 * self.eighth * self.right
        self.over_x, self.over_y = (0, 2 * a), (2 * a, 2 * b)
        self.then_y, self.then_x = (2 * a + 2 * b, a), (3 * a + 2 * b, b)
        self.keep_left, self.keep_right = (3 * a + 3 * b, a), (4 * a + 3 * b, b)
        self.shape = (4 * (a + b), 128)
        self.a, self.b = a, b

    def put(self, refs, shard, block, value):
        a, b, size = self.a, self.b, self.eighth
        if shard:
            starts_left = (self.over_x[0], self.over_x[0] + a)
            starts_right = (self.then_x[0], self.over_y[0] + b)
        else:
            starts_left = (self.keep_left[0], self.then_y[0])
            starts_right = (self.keep_right[0], self.over_y[0])
        is_left = block < self.left
        count, index = (self.left, block) if is_left else (self.right, block - self.left)
        for number in range(8):
            start = (starts_left if is_left else starts_right)[number // 4]
            at = start + (number % 4 * count + index) * size
            for ref in refs:
                if at < ref.shape[0]:
                    ref[at : at + size, :] = value[number * size : (number + 1) * size].astype(BF)
                    break
                at -= ref.shape[0]

    def parts(self):
        return [((size, 128), BF) for size in (self.over_x[1], self.over_y[1], 2 * (self.a + self.b))]


def combine(outs, tokens, micros, sums=(), kind=BF, cuts=None):
    arrays, terms = [], []
    for segments in outs:
        for parts in segments:
            for array, first, size in parts:
                if not any(array is known for known in arrays):
                    arrays.append(array)
                terms.append((next(i for i, known in enumerate(arrays) if known is array), first, size))
    n_sums, n_arrays, n_out, n_terms = len(sums), len(arrays), len(outs), len(terms)
    n_in = n_sums + n_arrays + len(tokens)
    sizes = [sum(parts[0][2] for parts in segments) for segments in outs]
    shapes = [jax.ShapeDtypeStruct((size, 128), kind) for size in sizes]
    n_results = n_out
    if cuts:
        shapes = []
        for (rows, cut) in cuts:
            for first, size, count, is_turned in cut:
                shape = (count, rows, size) if count > 1 else (size, rows) if is_turned else (rows, size)
                shapes.append(jax.ShapeDtypeStruct(shape, F32))
        n_results = len(shapes)

    def kernel(*refs):
        held, sem = refs[-1 - n_terms : -1], refs[-1]
        totals = refs[n_in : n_in + n_out] if not cuts else refs[n_in + n_results + bool(sums) : -1 - n_terms]
        copies = [
            pltpu.make_async_copy(refs[n_sums + which].at[pl.ds(first, size), :], held[at], sem.at[at])
            for at, (which, first, size) in enumerate(terms)
        ]
        for copy in copies:
            copy.start()
        if sums:
            refs[n_in + n_results][...] = refs[0][...] + refs[1][...]
        at = 0
        for out, segments in zip(totals, outs):
            row = 0
            for parts in segments:
                size = parts[0][2]
                mine = list(range(at, at + len(parts)))
                for term in mine:
                    copies[term].wait()

                def add(step, carry, row=row, mine=mine, out=out):
                    here = pl.ds(pl.multiple_of(step * 48, 48), 48)
                    total = held[mine[0]][here, :].astype(F32)
                    for term in mine[1:]:
                        total = total + held[term][here, :].astype(F32)
                    out[pl.ds(pl.multiple_of(row + step * 48, 16), 48), :] = total.astype(kind)
                    return carry

                lax.fori_loop(0, size // 48, add, 0, unroll=2)
                at += len(parts)
                row += size
        if cuts:
            results = iter(refs[n_in : n_in + n_results])
            for out, (rows, cut) in zip(totals, cuts):
                whole = jnp.concatenate([out[u * rows : (u + 1) * rows, :] for u in range(out.shape[0] // rows)], 1)
                for value in finals(whole, cut):
                    next(results)[...] = value

    moved = 256 * (sum(t[2] for t in terms) + sum(sizes))
    in_vmem = pl.BlockSpec(memory_space=pltpu.VMEM)
    return pl.pallas_call(
        kernel,
        out_shape=shapes + ([jax.ShapeDtypeStruct(sums[0].shape, F32)] if sums else []),
        in_specs=[in_vmem] * n_sums + [ANYWHERE] * (n_in - n_sums),
        out_specs=[in_vmem] * (n_results + (1 if sums else 0)),
        scratch_shapes=[pltpu.VMEM((size, 128), F32) for size in sizes if cuts]
        + [pltpu.VMEM((size, 128), BF) for _, _, size in terms]
        + [pltpu.SemaphoreType.DMA((n_terms,))],
        compiler_params=pltpu.CompilerParams(vmem_limit_bytes=VMEM_BYTES),
        cost_estimate=pl.CostEstimate(flops=int(micros * COST), bytes_accessed=moved if micros else 0, transcendentals=0),
    )(*sums, *in_hbm(arrays), *in_hbm(tokens, 0))


def pack_attn_kernel(pos, qkv, out, own, direct):
    cols = qkv.shape[1]
    for part in range(3):
        own[part * cols : (part + 1) * cols, :] = qkv[part]
    own[3 * cols :, :] = out[...]
    half = direct.shape[0]
    direct[...] = own[pl.ds(pl.multiple_of(pos[1] * half, half), half), :]


def pack_rest_kernel(pos, up, down, qkv, out, embed, p_up, p_down, up_direct, down_direct, pred):
    half = up_direct.shape[1]
    at = pl.ds(pl.multiple_of(pos[1] * half, half), half)
    up_direct[...] = up[:, at]
    down_direct[...] = down[at, :]
    width = pred.shape[1]
    row = 0
    for part in (qkv[0], qkv[1], qkv[2], out[...], embed[:, :width], embed[:, width:], p_up[...], p_down[...]):
        pred[row : row + part.shape[0], :] = part
        row += part.shape[0]


def enc_attn_kernel(pos, x, seg_row, seg_col, gain, own, core, d_x, e_x, d_c, e_c, middle, qkv, probs, mixed, far):
    side = pos[1]
    half = d_x.shape[0]
    per = own.shape[0] // 4 // HEAD_DIM
    rows = 3 * per * HEAD_DIM
    for at, (first, second) in enumerate(((d_x, e_x), (d_c, e_c))):
        far[at, pl.ds(pl.multiple_of(side * half, half), half), :] = first[...]
        far[at, pl.ds(pl.multiple_of((1 - side) * half, half), half), :] = second[...]
    value = x[...].astype(F32)
    normed, _ = norm(value)
    low = (normed * gain[...]).astype(BF)
    packs = (own, core, far.at[0], far.at[1])
    for shard, pack in enumerate(packs):
        qkv[shard * rows : (shard + 1) * rows, :] = nt(pack[:rows, :], low).astype(BF)
    attend(qkv, probs, mixed, seg_col[...] == seg_row[...], per, HEAD_DIM)
    total = value
    for shard, pack in enumerate(packs):
        total = total + tn(mixed[shard * rows // 3 : (shard + 1) * rows // 3, :], pack[rows:, :])
    middle[...] = total


def hidden_pieces(side, mats, width):
    half = width // 2
    own, core, d_x, e_x, d_c, e_c = mats
    first, second = side * half, (1 - side) * half
    return (
        (own, 0, width), (core, width, width),
        (d_x, 2 * width + first, half), (e_x, 2 * width + second, half),
        (d_c, 3 * width + first, half), (e_c, 3 * width + second, half),
    )


def columns(first, size):
    return pl.ds(first if isinstance(first, int) else pl.multiple_of(first, 128), size)


def enc_up_forward_kernel(pos, middle, gain, *refs):
    ups, (hidden, slope) = refs[:6], refs[6:]
    width = ups[0].shape[1]
    normed, _ = norm(middle[...])
    low = (normed * gain[...]).astype(BF)
    for up, first, size in hidden_pieces(pos[1], ups, width):
        act, back = gelu_parts(nn(low, up[...]))
        hidden[:, columns(first, size)] = act.astype(BF)
        slope[:, columns(first, size)] = back.astype(BF)


def enc_down_forward_kernel(pos, middle, hidden, *refs):
    downs, out = refs[:6], refs[6]
    total = middle[...]
    for down, first, size in hidden_pieces(pos[1], downs, downs[0].shape[0]):
        total = total + nn(hidden[:, columns(first, size)], down[...])
    out[...] = total.astype(BF)


def pred_kernel(
    pos, enc, seg_row, seg_col, masked, token, gain_one, gain_two, cot, rows_at,
    p_own, p_core, p_x, p_xc,
    pred_out, stats, g_mine, g_theirs, d_embedded, d_enc, d_gains,
    w_qkv, w_out, w_embed, w_up, w_down, qkv, probs, mixed, d_mixed, d_qkv,
):
    me = pos[0]
    length = cot.shape[0]
    cols = w_out.shape[0] // SHARDS
    hid = w_down.shape[0] // SHARDS
    segments = Segments(w_out.shape[0], 4 * cols + 2 * hid)
    per = cols // P_HEAD_DIM
    width = w_out.shape[1]
    for shard, pack in enumerate((p_own, p_core, p_x, p_xc)):
        w_qkv[shard * 3 * cols : (shard + 1) * 3 * cols, :] = pack[: 3 * cols, :]
        w_out[shard * cols : (shard + 1) * cols, :] = pack[3 * cols : 4 * cols, :]
        at = pl.ds(pl.multiple_of((me ^ shard) * cols, 16), cols)
        w_embed[at, :width] = pack[4 * cols : 5 * cols, :]
        w_embed[at, width:] = pack[5 * cols : 6 * cols, :]
        w_up[:, shard * hid : (shard + 1) * hid] = pack[6 * cols : 6 * cols + width, :]
        w_down[shard * hid : (shard + 1) * hid, :] = pack[6 * cols + width :, :]

    hidden_mask = masked[...] > 0.0
    start = jnp.where(hidden_mask, token[...], nt(enc[...], w_embed[...]))
    n_one, r_one = norm(start)
    a = (n_one * gain_one[...]).astype(BF)
    qkv[...] = nt(w_qkv[...], a).astype(BF)
    attend(qkv, probs, mixed, seg_col[...] == seg_row[...], per, P_HEAD_DIM)
    middle = start + tn(mixed[...], w_out[...])
    n_two, r_two = norm(middle)
    b = (n_two * gain_two[...]).astype(BF)
    act, slope = gelu_parts(nn(b, w_up[...]))
    act = act.astype(BF)
    predicted = middle + nn(act, w_down[...])
    for at, block in enumerate(units(predicted)):
        pred_out[at * length : (at + 1) * length, :] = block.astype(BF)
    stats[...] = jnp.zeros_like(stats)
    stats[0:1, :] = jnp.sum(predicted, 0, keepdims=True)
    stats[1:2, :] = jnp.sum(predicted * predicted, 0, keepdims=True)

    homes = (((g_mine,), 0), ((g_theirs,), 0), ((g_mine,), 1), ((g_theirs,), 1))
    grad_low = cot[...]
    d_pre = (nt(grad_low, w_down[...]) * slope).astype(BF)
    source = rows_at[...]
    grad_turned, b_turned = turned(source, grad_low), turned(source, b)
    for shard, (home, at) in enumerate(homes):
        cut = slice(shard * hid, (shard + 1) * hid)
        blocks = units(nn(b_turned, d_pre[:, cut])) + units(nn(grad_turned, act[:, cut]))
        for block, value in enumerate(blocks):
            segments.put(home, at, 4 * cols // 128 + block, value)
    d_middle, d_gain_two = norm_back(n_two, r_two, gain_two[...], nt(d_pre, w_up[...]))
    grad_mid = grad_low.astype(F32) + d_middle
    mid_low = grad_mid.astype(BF)
    d_mixed[...] = nt(w_out[...], mid_low).astype(BF)
    attend_back(qkv, probs, d_mixed, d_qkv, per, P_HEAD_DIM)
    a_turned, mid_turned = turned(source, a), turned(source, mid_low)
    for shard, (home, at) in enumerate(homes):
        g_qkv = nt(a_turned, d_qkv[shard * 3 * cols : (shard + 1) * 3 * cols, :])
        g_out = nt(mid_turned, mixed[shard * cols : (shard + 1) * cols, :])
        for block, value in enumerate(units(jnp.concatenate([g_qkv, g_out], 1))):
            segments.put(home, at, block, value)
    d_value, d_gain_one = norm_back(n_one, r_one, gain_one[...], tn(d_qkv[...], w_qkv[...]))
    d_start = grad_mid + d_value
    d_gains[...] = jnp.zeros_like(d_gains)
    d_gains[0:1, :] = d_gain_one
    d_gains[1:2, :] = d_gain_two
    d_gains[2:3, :] = jnp.sum(jnp.where(hidden_mask, d_start, 0.0), 0, keepdims=True)
    d_low = jnp.where(hidden_mask, 0.0, d_start).astype(BF)
    d_embedded[...] = d_low
    d_enc[...] = nn(d_low, w_embed[...])


def enc_down_kernel(first, pos, rows_at, grad, hidden, *homes):
    width = hidden.shape[1] // SHARDS
    segments = Segments(grad.shape[1], width)
    grad_turned = turned(rows_at[...], grad[...].astype(BF))
    for at in range(2):
        shard = first + 2 * at
        for block, value in enumerate(units(nn(grad_turned, hidden[:, shard * width : (shard + 1) * width]))):
            segments.put(homes, at, block, value)


def enc_up_kernel(pos, rows_at, grad, middle, gain, slope, *refs):
    ups, downs, (grad_mid, d_gain, mine), theirs = refs[:6], refs[6:12], refs[12:15], refs[15:]
    side = pos[1]
    width = ups[0].shape[1]
    value = middle[...]
    segments = Segments(value.shape[1], width)
    n_two, r_two = norm(value)
    b_turned = turned(rows_at[...], (n_two * gain[...]).astype(BF))
    homes = (((mine,), 0), (theirs, 0), ((mine,), 1), (theirs, 1))
    low = grad[...].astype(BF)
    d_b = jnp.zeros_like(value)
    pieces = hidden_pieces(side, ups, width)
    for piece in (1, 4, 5, 0, 2, 3):
        up, first, size = pieces[piece]
        home, at = homes[(0, 1, 2, 2, 3, 3)[piece]]
        d_pre = (nt(low, downs[piece][...]) * slope[:, columns(first, size)].astype(F32)).astype(BF)
        d_b = d_b + nt(d_pre, up[...])
        blocks = units(nn(b_turned, d_pre))

        def put(first_block, home=home, at=at, blocks=blocks):
            for block, part in enumerate(blocks):
                segments.put(home, at, first_block + block, part)

        if piece < 2:
            put(0)
        else:
            second_half = side if piece in (2, 4) else 1 - side
            pl.when(second_half == 0)(lambda put=put: put(0))
            pl.when(second_half == 1)(lambda put=put, blocks=blocks: put(len(blocks)))
    d_middle, d_gain_two = norm_back(n_two, r_two, gain[...], d_b)
    grad_mid[...] = grad[...] + d_middle
    d_gain[...] = d_gain_two


def enc_attn_back_kernel(
    pos, x, gain, grad, qkv, probs, own, core, d_x, e_x, d_c, e_c, d_qkv, d_input, d_gain, far, d_mixed
):
    side = pos[1]
    half = d_x.shape[0]
    per = own.shape[0] // 4 // HEAD_DIM
    cols = per * HEAD_DIM
    for at, (first, second) in enumerate(((d_x, e_x), (d_c, e_c))):
        far[at, pl.ds(pl.multiple_of(side * half, half), half), :] = first[...]
        far[at, pl.ds(pl.multiple_of((1 - side) * half, half), half), :] = second[...]
    packs = (own, core, far.at[0], far.at[1])
    low = grad[...].astype(BF)
    for shard, pack in enumerate(packs):
        d_mixed[shard * cols : (shard + 1) * cols, :] = nt(pack[3 * cols :, :], low).astype(BF)
    attend_back(qkv, probs, d_mixed, d_qkv, per, HEAD_DIM)
    value = x[...].astype(F32)
    length = value.shape[0]
    normed, inverse = norm(value)
    d_a = jnp.zeros_like(value)
    for shard in range(SHARDS):
        d_a = d_a + tn(d_qkv[shard * 3 * cols : (shard + 1) * 3 * cols, :], packs[shard][: 3 * cols, :])
    d_value, d_gain_one = norm_back(normed, inverse, gain[...], d_a)
    d_gain[...] = d_gain_one
    for at, block in enumerate(units(grad[...] + d_value)):
        d_input[at * length : (at + 1) * length, :] = block.astype(BF)


def enc_attn_weights_kernel(
    pos, rows_at, x, gain, grad, mixed, d_qkv, d_embedded, enc, d_gain_one, d_gain_two, p_d_gains, mine, *theirs
):
    me = pos[0]
    value = x[...].astype(F32)
    width = value.shape[1]
    cols = width // SHARDS
    normed, _ = norm(value)
    source = rows_at[...]
    a_turned = turned(source, (normed * gain[...]).astype(BF))
    mid_turned = turned(source, grad[...].astype(BF))
    channels = d_embedded.shape[1]
    e_cols = channels // SHARDS
    row = lax.broadcasted_iota(jnp.int32, (channels, SHARDS * 128), 0)
    column = lax.broadcasted_iota(jnp.int32, (channels, SHARDS * 128), 1)
    within = column & 127
    one_hot = ((((column >> 7) ^ me) * e_cols + within == row) & (within < e_cols)).astype(BF)
    g_embed = nn(turned(source, enc[...]), nn(d_embedded[...], one_hot).astype(BF))
    line = lax.broadcasted_iota(jnp.int32, (8, width), 0)
    lines = jnp.where(line == 0, d_gain_one[...], jnp.where(line == 1, d_gain_two[...], 0.0)).astype(BF)
    lane = lax.broadcasted_iota(jnp.int32, (8, 128), 1) - lax.broadcasted_iota(jnp.int32, (8, 128), 0)
    n_rows, n_small = pos[2], pos[3]
    device = ((source.astype(F32) + 0.5) / n_rows.astype(F32)).astype(jnp.int32)
    within_device = source - device * n_rows
    p_source = device * n_small + jnp.where(within_device >= n_small, within_device - n_small, within_device)
    p_one_hot = (lax.broadcasted_iota(jnp.int32, (width, channels), 1) == p_source).astype(BF)
    g_small = nn(turned(source, lines), (lane == e_cols).astype(BF)) + nn(
        nt(p_one_hot, p_d_gains[...].astype(BF)).astype(BF), (lane == e_cols + 2).astype(BF)
    )

    segments = Segments(width, 4 * cols + 128)
    homes = (((mine,), 0), (theirs, 0), ((mine,), 1), (theirs, 1))
    for shard in (1, 3, 0, 2):
        home, at = homes[shard]
        g_qkv = nt(a_turned, d_qkv[shard * 3 * cols : (shard + 1) * 3 * cols, :])
        g_out = nt(mid_turned, mixed[shard * cols : (shard + 1) * cols, :])
        blocks = units(jnp.concatenate([g_qkv, g_out], 1)) + [g_embed[:, shard * 128 : (shard + 1) * 128] + g_small]
        for block, part in enumerate(blocks):
            segments.put(home, at, block, part)


def in_order_kernel(pos, own, core, x, xc, out):
    length = out.shape[1]
    for shard, ref in enumerate((own, core, x, xc)):
        for at in range(out.shape[2] // 128):
            out[pos[0] ^ shard, :, at * 128 : (at + 1) * 128] = ref[at * length : (at + 1) * length, :]


def swap(value, axis, bit):
    size = lax.axis_size(axis)
    return lax.ppermute(value, axis, [(i, i ^ bit) for i in range(size)])


def pick(value, index, axis=0):
    return lax.dynamic_index_in_dim(value, index, axis, keepdims=False)


def finals(total, cuts):
    results = []
    for first, size, count, is_turned in cuts:
        parts = [total[:, first + at * size : first + (at + 1) * size] for at in range(count)]
        results.append(jnp.stack(parts) if count > 1 else parts[0].T if is_turned else parts[0])
    return results


def source_rows(width):
    size = lax.axis_size("dp")
    number = jnp.arange(8, dtype=jnp.int32)
    owner = (lax.axis_index("dp") & 7) ^ (number >> 2 | number & 2 | (number & 1) << 2)
    inner = jnp.arange(width // 8, dtype=jnp.int32).reshape(1, size // 8, width // size)
    high = jnp.arange(size // 8, dtype=jnp.int32)[None, :, None]
    rows = (high * 8 + owner[:, None, None]) * (width // size) + inner % (width // size)
    return rows.reshape(width, 1)


def body(
    patches, segment_ids, mask_slots, gain_attn, qkv_weight, out_weight, gain_mlp, up_weight, down_weight,
    embed_weight, mask_token, pred_gain_attn, pred_qkv, pred_out, pred_gain_mlp, pred_up, pred_down, cotangent,
):
    me = lax.axis_index("mp")
    side = lax.axis_index("dp") % 2
    dp_size = lax.axis_size("dp")
    length, width = patches.shape[1:]
    channels = cotangent.shape[2]
    cols, hid = qkv_weight.shape[2], up_weight.shape[1]
    p_cols, p_hid = pred_qkv.shape[2], pred_up.shape[1]
    heads = SHARDS * cols // HEAD_DIM
    p_heads = SHARDS * p_cols // P_HEAD_DIM
    pos = jnp.stack([me, side, width // dp_size, channels // dp_size]).astype(jnp.int32)

    attn_own, attn_direct = call(
        pack_attn_kernel, [((4 * cols, width), BF), ((2 * cols, width), BF)],
        (pos, jnp.swapaxes(qkv_weight, 1, 2), out_weight), 1,
    )
    up_direct, down_direct, p_own = call(
        pack_rest_kernel,
        [((width, hid // 2), BF), ((hid // 2, width), BF), ((6 * p_cols + channels + p_hid, channels), BF)],
        (pos, up_weight, down_weight, jnp.swapaxes(pred_qkv, 1, 2), pred_out, embed_weight.T, pred_up, pred_down), 3,
        tokens=(attn_direct,),
    )

    attn_core, up_core, down_core = swap(attn_own, "mp", 1), swap(up_weight, "mp", 1), swap(down_weight, "mp", 1)
    p_core = swap(p_own, "mp", 1)
    attn_x = swap(attn_direct, "mp", 2)
    attn_x, up_direct = gate([attn_x, up_direct], [p_own])
    up_x = swap(up_direct, "mp", 2)
    attn_y = swap(attn_x, "dp", 1)
    (down_direct,) = gate([down_direct], [up_x])
    down_x = swap(down_direct, "mp", 2)
    up_y = swap(up_x, "dp", 1)
    (p_send,) = gate([p_own], [down_x])
    p_x = swap(p_send, "mp", 2)
    attn = (attn_own, attn_core, attn_x, attn_y, swap(attn_x, "mp", 1), swap(attn_y, "mp", 1))

    x = pick(patches, me)
    segments = pick(segment_ids, me)
    seg_row, seg_col = segments[None, :], segments[:, None]
    slots = pick(mask_slots, me)
    masked = jnp.any(jnp.arange(length, dtype=jnp.int32)[:, None] == slots[None, :], -1, keepdims=True).astype(F32)
    cot = pick(cotangent, me)
    row = lambda gain: gain.astype(F32)[None, :]
    rows_at, p_rows_at = source_rows(width), source_rows(channels)
    n_rows, n_small = width // dp_size, channels // dp_size

    middle, qkv, probs, mixed = call(
        enc_attn_kernel,
        [((length, width), F32), ((3 * width, length), BF), ((heads, length, length), BF), ((width, length), BF)],
        (pos, x, seg_row, seg_col, row(gain_attn)) + attn, 9,
        [((2, 4 * cols, width), BF)],
    )
    (up_y,) = gate([up_y], [middle])
    up = (up_weight, up_core, up_x, up_y, swap(up_x, "mp", 1), swap(up_y, "mp", 1))
    down_y = swap(down_x, "dp", 1)
    hidden, slope = call(
        enc_up_forward_kernel, [((length, SHARDS * hid), BF), ((length, SHARDS * hid), BF)],
        (pos, middle, row(gain_mlp)) + up, 6,
    )
    (down_y,) = gate([down_y], [hidden])
    down = (down_weight, down_core, down_x, down_y, swap(down_x, "mp", 1), swap(down_y, "mp", 1))
    (enc,) = call(enc_down_forward_kernel, [((length, width), BF)], (pos, middle, hidden) + down, 4)
    (p_x,) = gate([p_x], [enc])
    p_packs = (p_send, p_core, p_x, swap(p_x, "mp", 1))
    p_seg, d_seg = Segments(channels, 4 * p_cols + 2 * p_hid), Segments(width, hid)
    u_seg, a_seg = Segments(width, hid), Segments(width, 4 * cols + 128)
    p_blocks, x_blocks = channels // 128, width // 128
    predicted, stats, p_mine, p_theirs, d_embedded, d_enc, p_d_gains = call(
        pred_kernel,
        [((p_blocks * length, 128), BF), ((8, channels), F32), (p_seg.shape, BF), (p_seg.shape, BF), ((length, channels), BF),
         ((length, width), F32), ((8, channels), F32)],
        (pos, enc, seg_row, seg_col, masked, row(mask_token), row(pred_gain_attn), row(pred_gain_mlp), cot, p_rows_at)
        + p_packs, 30,
        [((3 * channels, channels), BF), ((channels, channels), BF), ((channels, width), BF),
         ((channels, SHARDS * p_hid), BF), ((SHARDS * p_hid, channels), BF), ((3 * channels, length), BF),
         ((p_heads, length, length), BF), ((channels, length), BF), ((channels, length), BF),
         ((3 * channels, length), BF)],
    )

    p_cuts = [(0, p_cols, 3, False), (3 * p_cols, p_cols, 1, True), (4 * p_cols, p_hid, 1, False), (4 * p_cols + p_hid, p_hid, 1, True)]
    d_cuts, u_cuts = [(0, hid, 1, True)], [(0, hid, 1, False)]
    a_cuts = [(0, cols, 3, False), (3 * cols, cols, 1, True), (4 * cols, p_cols, 1, False), (4 * cols + p_cols, 128 - p_cols, 1, True)]
    small = dp_size == 8

    def sums_of(pieces, tokens, micros, sums=()):
        outs = [segments for segments, _, _ in pieces]
        if small:
            cuts = [(seg.eighth, cut) for _, seg, cut in pieces]
            return combine(outs, tokens, micros, sums, kind=F32, cuts=cuts)
        totals = combine(outs, tokens, micros, sums, kind=F32)
        groups = [[high * 8 + low for high in range(dp_size // 8)] for low in range(8)]
        results = []
        for total, (_, seg, cut) in zip(totals, pieces):
            total = total.reshape(seg.left + seg.right, -1, 128)
            total = lax.psum_scatter(total, "dp", scatter_dimension=1, axis_index_groups=groups, tiled=True)
            results += finals(jnp.swapaxes(total, 0, 1).reshape(total.shape[1], -1), cut)
        return results + list(totals[len(pieces) :])

    def from_core(theirs):
        return [swap(part, "mp", 1) for part in theirs]

    def both(own, at, size):
        mine, away = own
        segments, start = [], 0
        for part in away:
            low, high = max(at, start), min(at + size, start + part.shape[0])
            if low < high:
                segments.append([(mine, low, high - low), (part, low - start, high - low)])
            start += part.shape[0]
        return segments

    def with_term(segments, array, at):
        result = []
        for parts in segments:
            result.append(parts + [(array, at, parts[0][2])])
            at += parts[0][2]
        return result

    def first(own, seg):
        return both(own, *seg.over_x), both(own, *seg.over_y)

    def second(own, seg, got):
        (x, x_at), (y, y_at) = got
        return with_term(both(own, *seg.then_x), y, y_at + seg.b), with_term(both(own, *seg.then_y), x, x_at + seg.a)

    def kept(own, seg, got, then, low, high, extra=()):
        segments = []
        for (start, size), over, after, right in (
            (seg.keep_left, got[0], then[1], 0), (seg.keep_right, got[1], then[0], 1)
        ):
            at, rows = low * size // 4, (high - low) * size // 4
            part = both(own, start + at, rows)
            for array, array_at in (over, after):
                part = with_term(part, array, array_at + at)
            for array, array_at in extra:
                part = with_term(part, array, array_at + right * seg.a * (high - low) // 4)
            segments += part
        return segments

    def stage(parts, tokens, micros, sums=(), z=()):
        outs = [sum((x for x, _ in parts), []), sum((y for _, y in parts), [])] if parts else []
        send = combine(outs + list(z), tokens, micros, sums)
        got, at = ((swap(send[0], "mp", 2), swap(send[1], "dp", 1)) if parts else ()), [0, 0]
        places = []
        for x, y in parts:
            places.append(((got[0], at[0]), (got[1], at[1])))
            at = [at[0] + sum(p[0][2] for p in x), at[1] + sum(p[0][2] for p in y)]
        return send, got, places

    p_away = swap(p_theirs, "mp", 1)
    d_theirs = call(partial(enc_down_kernel, 1), d_seg.parts(), (pos, rows_at, d_enc, hidden), 30)
    (d_mine,) = call(partial(enc_down_kernel, 0), [(d_seg.shape, BF)], (pos, rows_at, d_enc, hidden), 30, tokens=d_theirs[:1])
    p_own, d_own = (p_mine, [p_away]), (d_mine, from_core(d_theirs))
    send, p_arrived, (p_got, d_got, at_predicted) = stage(
        [first(p_own, p_seg), first(d_own, d_seg), ([[(predicted, 0, predicted.shape[0])]], [])], [], 30
    )
    grad_mid, d_gain_two, u_mine, *u_theirs = call(
        enc_up_kernel,
        [((length, width), F32), ((1, width), F32), (u_seg.shape, BF)] + u_seg.parts(),
        (pos, rows_at, d_enc, middle, row(gain_mlp), slope) + up + down, 100, tokens=send,
    )
    u_away = from_core(u_theirs)
    d_qkv, d_input, d_gain_one = call(
        enc_attn_back_kernel,
        [((3 * width, length), BF), ((x_blocks * length, 128), BF), ((1, width), F32)],
        (pos, x, row(gain_attn), grad_mid, qkv, probs) + attn, 1,
        [((2, 4 * cols, width), BF), ((width, length), BF)],
    )
    got_x, got_y, *u_away[:2] = gate([*p_arrived, *u_away[:2]], [d_gain_one])
    moved = lambda places: ((got_x, places[0][1]), (got_y, places[1][1]))
    p_got, d_got, u_own = moved(p_got), moved(d_got), (u_mine, u_away)
    predicted_x = lax.slice_in_dim(got_x, at_predicted[0][1], got_x.shape[0])
    filler = [[(d_input, 0, p_seg.b - p_seg.a)]]
    send, _, (u_got, d_then, p_then, _) = stage(
        [first(u_own, u_seg), second(d_own, d_seg, d_got), second(p_own, p_seg, p_got), ([], filler)], [], 30
    )
    predicted, predicted_x, d_input = gate([predicted, predicted_x, d_input], send)
    a_mine, *a_theirs = call(
        enc_attn_weights_kernel, [(a_seg.shape, BF)] + a_seg.parts(),
        (pos, rows_at, x, row(gain_attn), grad_mid, mixed, d_qkv, d_embedded, enc, d_gain_one, d_gain_two, p_d_gains), 100, tokens=send,
    )
    a_own = (a_mine, from_core(a_theirs))
    a_send, _, (a_got,) = stage([first(a_own, a_seg)], [], 0)
    p_z = (p_own, p_seg, p_got, p_then)
    d_z = (d_own, d_seg, d_got, d_then)
    (*u_send, z_send), _, (u_then,) = stage(
        [second(u_own, u_seg, u_got)], a_send, 3, (), [kept(*p_z, 2, 4) + kept(*d_z, 2, 4)]
    )
    (stats,) = gate([stats], u_send)
    u_z = (u_own, u_seg, u_got, u_then)
    stats_got, z_got = swap(stats, "mp", 1), swap(z_send, "dp", 2)
    p_rows, d_rows, u_rows = ((seg.a + seg.b) // 4 for seg in (p_seg, d_seg, u_seg))
    p_one, d_one = (z_got, 0), (z_got, 2 * p_rows)

    def later(one, seg, quarter):
        array, at = one
        return [(array, at + quarter * seg.a // 4), (array, at + seg.a // 2 + quarter * seg.b // 4)]

    def last(z, one, quarter, two=None):
        own, seg, got, then = z
        segments = []
        lefts_rights = later(one, seg, quarter)
        for part, (start, size), over, after, (array, at), shift in (
            (0, seg.keep_left, got[0], then[1], lefts_rights[0], 0), (1, seg.keep_right, got[1], then[0], lefts_rights[1], seg.a // 4)
        ):
            begin, rows = quarter * size // 4, size // 4
            terms = both(own, start + begin, rows)
            for more, more_at in (over, after):
                terms = with_term(terms, more, more_at + begin)
            terms = with_term(terms, array, at)
            if two is not None:
                terms = with_term(terms, two[0], two[1] + shift)
            segments += terms
        return segments

    filler = [[(a_got[0][0], 0, a_seg.b - a_seg.a)]]
    (*a_send, z_send, stats), _, (a_then, _) = stage(
        [second(a_own, a_seg, a_got), ([], filler)], u_send, 3, (stats, stats_got), [last(p_z, p_one, 1) + last(d_z, d_one, 1)]
    )
    a_z = (a_own, a_seg, a_got, a_then)
    z_got = swap(z_send, "dp", 4)
    (z_send,) = combine([kept(*u_z, 2, 4)], a_send, 3)
    u_one, stats_got = (swap(z_send, "dp", 2), 0), swap(stats, "dp", 2)
    predicted, predicted_x = gate([predicted, predicted_x], [z_send])
    predicted_c, predicted_xc = swap(predicted, "mp", 1), swap(predicted_x, "mp", 1)
    z_send, z_send_u, stats = combine([kept(*a_z, 2, 4), last(u_z, u_one, 1)], [z_send], 3, (stats, stats_got))
    a_one, u_two = (swap(z_send, "dp", 2), 0), (swap(z_send_u, "dp", 4), 0)
    d_input, stats, p_two_array = gate([d_input, stats, z_got], [z_send])
    p_two, d_two = (p_two_array, 0), (p_two_array, p_rows)
    stats_got, input_x, input_c = swap(stats, "dp", 4), swap(d_input, "mp", 2), swap(d_input, "mp", 1)
    *p_results, r_down = sums_of(
        [(last(p_z, p_one, 0, p_two), p_seg, p_cuts), (last(d_z, d_one, 0, d_two), d_seg, d_cuts)], [z_send], 3
    )
    (predictions,) = call(
        in_order_kernel, [((SHARDS, length, channels), BF)], (pos, predicted, predicted_c, predicted_x, predicted_xc), 3,
        tokens=(p_results[1],),
    )
    z_send, stats = combine([last(a_z, a_one, 1)], [predictions], 3, (stats, stats_got))
    a_two = (swap(z_send, "dp", 4), 0)
    (input_x,) = gate([input_x], [z_send])
    r_up, stats = sums_of([(last(u_z, u_one, 0, u_two), u_seg, u_cuts)], [z_send], 3, (stats, swap(stats, "mp", 2)))
    stats_got = swap(stats, "dp", 1)
    (patches_grad,) = call(
        in_order_kernel, [((SHARDS, length, width), BF)], (pos, d_input, input_c, input_x, swap(input_x, "mp", 1)), 2,
        tokens=(r_up,),
    )
    *a_results, stats = sums_of([(last(a_z, a_one, 0, a_two), a_seg, a_cuts)], [patches_grad], 3, (stats, stats_got))
    for at in range(3, dp_size.bit_length() - 1):
        stats = stats + swap(stats, "dp", 1 << at)

    count = dp_size * patches.shape[0] * length
    mean, square = stats[0] / count, stats[1] / count
    n_var = channels // SHARDS
    variance = lax.dynamic_slice_in_dim(square - mean * mean, me * n_var, n_var)
    tail = a_results[3]

    return (
        predictions,
        patches_grad,
        variance,
        tail[0],
        a_results[0],
        a_results[1],
        tail[1],
        r_up,
        r_down,
        a_results[2],
        tail[4, :n_small],
        tail[2, :n_small],
        p_results[0],
        p_results[1],
        tail[3, :n_small],
        p_results[2],
        p_results[3],
    )


def solution(mesh):
    placed = (
        P("dp", None, None), P("dp", None), P("dp", None), P(), P(None, None, "mp"), P("mp", None), P(),
        P(None, "mp"), P("mp", None), P(None, "mp"), P(), P(), P(None, None, "mp"), P("mp", None), P(),
        P(None, "mp"), P("mp", None), P("dp", None, None),
    )
    return jax.shard_map(
        body,
        mesh=mesh,
        in_specs=placed,
        out_specs=(
            P("dp", None, None), P("dp", None, None), P("mp"), P("dp"), P(None, "dp", "mp"), P("mp", "dp"),
            P("dp"), P("dp", "mp"), P("mp", "dp"), P("dp", "mp"), P("dp"), P("dp"), P(None, "dp", "mp"),
            P("mp", "dp"), P("dp"), P("dp", "mp"), P("mp", "dp"),
        ),
        check_vma=False,
    )
```

```python
import math
from functools import partial

import jax
import jax.numpy as jnp
from jax import lax
from jax.experimental import pallas as pl
from jax.experimental.pallas import tpu as pltpu
from jax.sharding import PartitionSpec as P

HEAD_DIM = 64
P_HEAD_DIM = 32
SHARDS = 4
EPS = 1e-06
BF = jnp.bfloat16
F32 = jnp.float32
COST = 1.15e9
VMEM_BYTES = 48 * 1024 * 1024


def contract(left, right, at_left, at_right):
    return lax.dot_general(left, right, (((at_left,), (at_right,)), ((), ())), preferred_element_type=F32)


def nn(left, right):
    return contract(left, right, 1, 0)


def nt(left, right):
    return contract(left, right, 1, 1)


def tn(left, right):
    return contract(left, right, 0, 0)


def norm(value):
    centred = value - jnp.mean(value, -1, keepdims=True)
    inverse = lax.rsqrt(jnp.mean(centred * centred, -1, keepdims=True) + EPS)
    return centred * inverse, inverse


def norm_back(normed, inverse, gain, grad):
    scaled = grad * gain
    along = jnp.mean(scaled * normed, -1, keepdims=True)
    d_value = (scaled - jnp.mean(scaled, -1, keepdims=True) - normed * along) * inverse
    return d_value, jnp.sum(grad * normed, 0, keepdims=True)


def gelu_parts(pre):
    cdf = 0.5 * (1.0 + lax.erf(pre * 0.7071067811865476))
    density = 0.3989422804014327 * jnp.exp(-0.5 * pre * pre)
    return pre * cdf, cdf + pre * density


def turned(source_rows, value):
    width = value.shape[1]
    one_hot = (lax.broadcasted_iota(jnp.int32, (width, width), 1) == source_rows).astype(BF)
    return nt(one_hot, value).astype(BF)


def head_rows(head, per, head_dim):
    shard = head // per
    first = shard * (3 * per * head_dim) + (head - shard * per) * head_dim
    return [pl.ds(pl.multiple_of(first + part * per * head_dim, head_dim), head_dim) for part in range(3)]


def attend(qkv_ref, probs_ref, mixed_ref, same, per, head_dim):
    factor = head_dim ** (-0.5) * math.log2(math.e)

    def one_head(head, carry):
        q_at, k_at, u_at = head_rows(head, per, head_dim)
        scores = jnp.where(same, tn(qkv_ref[k_at, :], qkv_ref[q_at, :]), -1e9)
        top = jnp.max(scores, 0, keepdims=True)
        expd = jnp.exp2((scores - top) * factor)
        probs = (expd * (1.0 / jnp.sum(expd, 0, keepdims=True))).astype(BF)
        probs_ref[head] = probs
        at = pl.ds(pl.multiple_of(head * head_dim, head_dim), head_dim)
        mixed_ref[at, :] = nn(qkv_ref[u_at, :], probs).astype(BF)
        return carry

    lax.fori_loop(0, SHARDS * per, one_head, 0, unroll=6)


def attend_back(qkv_ref, probs_ref, d_mixed_ref, d_qkv_ref, per, head_dim):
    scale = head_dim ** (-0.5)

    def one_head(head, carry):
        q_at, k_at, u_at = head_rows(head, per, head_dim)
        at = pl.ds(pl.multiple_of(head * head_dim, head_dim), head_dim)
        d_mixed = d_mixed_ref[at, :]
        low = probs_ref[head]
        probs = low.astype(F32)
        d_probs = tn(qkv_ref[u_at, :], d_mixed)
        along = jnp.sum(d_probs * probs, 0, keepdims=True)
        d_scores = (probs * (d_probs - along)).astype(BF)
        d_qkv_ref[q_at, :] = (nn(qkv_ref[k_at, :], d_scores) * scale).astype(BF)
        d_qkv_ref[k_at, :] = (nt(qkv_ref[q_at, :], d_scores) * scale).astype(BF)
        d_qkv_ref[u_at, :] = nt(d_mixed, low).astype(BF)
        return carry

    lax.fori_loop(0, SHARDS * per, one_head, 0, unroll=6)


ANYWHERE = pl.BlockSpec(memory_space=pl.ANY)


def in_hbm(arrays, least=256 * 1700):
    return [pltpu.with_memory_space_constraint(a, pltpu.HBM) if n_bytes(a) >= least else a for a in arrays]


def n_bytes(array):
    return math.prod(array.shape) * array.dtype.itemsize


ANYWHERE = pl.BlockSpec(memory_space=pl.ANY)


def in_hbm(arrays, least=256 * 1700):
    return [pltpu.with_memory_space_constraint(a, pltpu.HBM) if n_bytes(a) >= least else a for a in arrays]


def n_bytes(array):
    return math.prod(array.shape) * array.dtype.itemsize


def call(kernel, outs, args, micros, scratch=(), tokens=()):
    shapes = [jax.ShapeDtypeStruct(shape, kind) for shape, kind in outs]
    moved = sum(math.prod(a.shape) * a.dtype.itemsize for a in list(args) + shapes)
    n_args, n_all = len(args), len(args) + len(tokens)
    return pl.pallas_call(
        lambda *refs: kernel(*refs[:n_args], *refs[n_all:]),
        out_shape=shapes,
        in_specs=[pl.BlockSpec(memory_space=pltpu.SMEM)]
        + [pl.BlockSpec(memory_space=pltpu.VMEM)] * (n_args - 1)
        + [ANYWHERE] * len(tokens),
        out_specs=[pl.BlockSpec(memory_space=pltpu.VMEM)] * len(shapes),
        scratch_shapes=[pltpu.VMEM(shape, kind) for shape, kind in scratch],
        compiler_params=pltpu.CompilerParams(vmem_limit_bytes=VMEM_BYTES),
        cost_estimate=pl.CostEstimate(flops=int(micros * COST), bytes_accessed=moved if micros else 0, transcendentals=0),
    )(*args, *in_hbm(tokens, 0))


def gate(values, tokens):
    return pl.pallas_call(
        lambda *refs: None,
        out_shape=[jax.ShapeDtypeStruct(v.shape, v.dtype) for v in values],
        in_specs=[ANYWHERE] * (len(values) + len(tokens)),
        out_specs=[ANYWHERE] * len(values),
        input_output_aliases={at: at for at in range(len(values))},
    )(*in_hbm(values), *in_hbm(tokens, 0))


def units(value):
    return [value[:, at * 128 : (at + 1) * 128] for at in range(value.shape[1] // 128)]


class Segments:
    def __init__(self, rows, cols):
        self.eighth, blocks = rows // 8, cols // 128
        self.left, self.right = blocks // 2, blocks - blocks // 2
        a, b = 4 * self.eighth * self.left, 4 * self.eighth * self.right
        self.over_x, self.over_y = (0, 2 * a), (2 * a, 2 * b)
        self.then_y, self.then_x = (2 * a + 2 * b, a), (3 * a + 2 * b, b)
        self.keep_left, self.keep_right = (3 * a + 3 * b, a), (4 * a + 3 * b, b)
        self.shape = (4 * (a + b), 128)
        self.a, self.b = a, b

    def put(self, refs, shard, block, value):
        a, b, size = self.a, self.b, self.eighth
        if shard:
            starts_left = (self.over_x[0], self.over_x[0] + a)
            starts_right = (self.then_x[0], self.over_y[0] + b)
        else:
            starts_left = (self.keep_left[0], self.then_y[0])
            starts_right = (self.keep_right[0], self.over_y[0])
        is_left = block < self.left
        count, index = (self.left, block) if is_left else (self.right, block - self.left)
        for number in range(8):
            start = (starts_left if is_left else starts_right)[number // 4]
            at = start + (number % 4 * count + index) * size
            for ref in refs:
                if at < ref.shape[0]:
                    ref[at : at + size, :] = value[number * size : (number + 1) * size].astype(BF)
                    break
                at -= ref.shape[0]

    def parts(self):
        return [((size, 128), BF) for size in (self.over_x[1], self.over_y[1], 2 * (self.a + self.b))]


def combine(outs, tokens, micros, sums=(), kind=BF, cuts=None):
    arrays, terms = [], []
    for segments in outs:
        for parts in segments:
            for array, first, size in parts:
                if not any(array is known for known in arrays):
                    arrays.append(array)
                terms.append((next(i for i, known in enumerate(arrays) if known is array), first, size))
    n_sums, n_arrays, n_out, n_terms = len(sums), len(arrays), len(outs), len(terms)
    n_in = n_sums + n_arrays + len(tokens)
    sizes = [sum(parts[0][2] for parts in segments) for segments in outs]
    shapes = [jax.ShapeDtypeStruct((size, 128), kind) for size in sizes]
    n_results = n_out
    if cuts:
        shapes = []
        for (rows, cut) in cuts:
            for first, size, count, is_turned in cut:
                shape = (count, rows, size) if count > 1 else (size, rows) if is_turned else (rows, size)
                shapes.append(jax.ShapeDtypeStruct(shape, F32))
        n_results = len(shapes)

    def kernel(*refs):
        held, sem = refs[-1 - n_terms : -1], refs[-1]
        totals = refs[n_in : n_in + n_out] if not cuts else refs[n_in + n_results + bool(sums) : -1 - n_terms]
        copies = [
            pltpu.make_async_copy(refs[n_sums + which].at[pl.ds(first, size), :], held[at], sem.at[at])
            for at, (which, first, size) in enumerate(terms)
        ]
        for copy in copies:
            copy.start()
        if sums:
            refs[n_in + n_results][...] = refs[0][...] + refs[1][...]
        at = 0
        for out, segments in zip(totals, outs):
            row = 0
            for parts in segments:
                size = parts[0][2]
                mine = list(range(at, at + len(parts)))
                for term in mine:
                    copies[term].wait()

                def add(step, carry, row=row, mine=mine, out=out):
                    here = pl.ds(pl.multiple_of(step * 48, 48), 48)
                    total = held[mine[0]][here, :].astype(F32)
                    for term in mine[1:]:
                        total = total + held[term][here, :].astype(F32)
                    out[pl.ds(pl.multiple_of(row + step * 48, 16), 48), :] = total.astype(kind)
                    return carry

                lax.fori_loop(0, size // 48, add, 0, unroll=2)
                at += len(parts)
                row += size
        if cuts:
            results = iter(refs[n_in : n_in + n_results])
            for out, (rows, cut) in zip(totals, cuts):
                whole = jnp.concatenate([out[u * rows : (u + 1) * rows, :] for u in range(out.shape[0] // rows)], 1)
                for value in finals(whole, cut):
                    next(results)[...] = value

    moved = 256 * (sum(t[2] for t in terms) + sum(sizes))
    in_vmem = pl.BlockSpec(memory_space=pltpu.VMEM)
    return pl.pallas_call(
        kernel,
        out_shape=shapes + ([jax.ShapeDtypeStruct(sums[0].shape, F32)] if sums else []),
        in_specs=[in_vmem] * n_sums + [ANYWHERE] * (n_in - n_sums),
        out_specs=[in_vmem] * (n_results + (1 if sums else 0)),
        scratch_shapes=[pltpu.VMEM((size, 128), F32) for size in sizes if cuts]
        + [pltpu.VMEM((size, 128), BF) for _, _, size in terms]
        + [pltpu.SemaphoreType.DMA((n_terms,))],
        compiler_params=pltpu.CompilerParams(vmem_limit_bytes=VMEM_BYTES),
        cost_estimate=pl.CostEstimate(flops=int(micros * COST), bytes_accessed=moved if micros else 0, transcendentals=0),
    )(*sums, *in_hbm(arrays), *in_hbm(tokens, 0))


def pack_attn_kernel(pos, qkv, out, own, direct):
    cols = qkv.shape[1]
    for part in range(3):
        own[part * cols : (part + 1) * cols, :] = qkv[part]
    own[3 * cols :, :] = out[...]
    half = direct.shape[0]
    direct[...] = own[pl.ds(pl.multiple_of(pos[1] * half, half), half), :]


def pack_rest_kernel(pos, up, down, qkv, out, embed, p_up, p_down, up_direct, down_direct, pred):
    half = up_direct.shape[1]
    at = pl.ds(pl.multiple_of(pos[1] * half, half), half)
    up_direct[...] = up[:, at]
    down_direct[...] = down[at, :]
    width = pred.shape[1]
    row = 0
    for part in (qkv[0], qkv[1], qkv[2], out[...], embed[:, :width], embed[:, width:], p_up[...], p_down[...]):
        pred[row : row + part.shape[0], :] = part
        row += part.shape[0]


def enc_attn_kernel(pos, x, seg_row, seg_col, gain, own, core, d_x, e_x, d_c, e_c, middle, qkv, probs, mixed, far):
    side = pos[1]
    half = d_x.shape[0]
    per = own.shape[0] // 4 // HEAD_DIM
    rows = 3 * per * HEAD_DIM
    for at, (first, second) in enumerate(((d_x, e_x), (d_c, e_c))):
        far[at, pl.ds(pl.multiple_of(side * half, half), half), :] = first[...]
        far[at, pl.ds(pl.multiple_of((1 - side) * half, half), half), :] = second[...]
    value = x[...].astype(F32)
    normed, _ = norm(value)
    low = (normed * gain[...]).astype(BF)
    packs = (own, core, far.at[0], far.at[1])
    for shard, pack in enumerate(packs):
        qkv[shard * rows : (shard + 1) * rows, :] = nt(pack[:rows, :], low).astype(BF)
    attend(qkv, probs, mixed, seg_col[...] == seg_row[...], per, HEAD_DIM)
    total = value
    for shard, pack in enumerate(packs):
        total = total + tn(mixed[shard * rows // 3 : (shard + 1) * rows // 3, :], pack[rows:, :])
    middle[...] = total


def hidden_pieces(side, mats, width):
    half = width // 2
    own, core, d_x, e_x, d_c, e_c = mats
    first, second = side * half, (1 - side) * half
    return (
        (own, 0, width), (core, width, width),
        (d_x, 2 * width + first, half), (e_x, 2 * width + second, half),
        (d_c, 3 * width + first, half), (e_c, 3 * width + second, half),
    )


def columns(first, size):
    return pl.ds(first if isinstance(first, int) else pl.multiple_of(first, 128), size)


def enc_up_forward_kernel(pos, middle, gain, *refs):
    ups, (hidden, slope) = refs[:6], refs[6:]
    width = ups[0].shape[1]
    normed, _ = norm(middle[...])
    low = (normed * gain[...]).astype(BF)
    for up, first, size in hidden_pieces(pos[1], ups, width):
        act, back = gelu_parts(nn(low, up[...]))
        hidden[:, columns(first, size)] = act.astype(BF)
        slope[:, columns(first, size)] = back.astype(BF)


def enc_down_forward_kernel(pos, middle, hidden, *refs):
    downs, out = refs[:6], refs[6]
    total = middle[...]
    for down, first, size in hidden_pieces(pos[1], downs, downs[0].shape[0]):
        total = total + nn(hidden[:, columns(first, size)], down[...])
    out[...] = total.astype(BF)


def pred_kernel(
    pos, enc, seg_row, seg_col, masked, token, gain_one, gain_two, cot, rows_at,
    p_own, p_core, p_x, p_xc,
    pred_out, stats, g_mine, g_theirs, d_embedded, d_enc, d_gains,
    w_qkv, w_out, w_embed, w_up, w_down, qkv, probs, mixed, d_mixed, d_qkv,
):
    me = pos[0]
    length = cot.shape[0]
    cols = w_out.shape[0] // SHARDS
    hid = w_down.shape[0] // SHARDS
    segments = Segments(w_out.shape[0], 4 * cols + 2 * hid)
    per = cols // P_HEAD_DIM
    width = w_out.shape[1]
    for shard, pack in enumerate((p_own, p_core, p_x, p_xc)):
        w_qkv[shard * 3 * cols : (shard + 1) * 3 * cols, :] = pack[: 3 * cols, :]
        w_out[shard * cols : (shard + 1) * cols, :] = pack[3 * cols : 4 * cols, :]
        at = pl.ds(pl.multiple_of((me ^ shard) * cols, 16), cols)
        w_embed[at, :width] = pack[4 * cols : 5 * cols, :]
        w_embed[at, width:] = pack[5 * cols : 6 * cols, :]
        w_up[:, shard * hid : (shard + 1) * hid] = pack[6 * cols : 6 * cols + width, :]
        w_down[shard * hid : (shard + 1) * hid, :] = pack[6 * cols + width :, :]

    hidden_mask = masked[...] > 0.0
    start = jnp.where(hidden_mask, token[...], nt(enc[...], w_embed[...]))
    n_one, r_one = norm(start)
    a = (n_one * gain_one[...]).astype(BF)
    qkv[...] = nt(w_qkv[...], a).astype(BF)
    attend(qkv, probs, mixed, seg_col[...] == seg_row[...], per, P_HEAD_DIM)
    middle = start + tn(mixed[...], w_out[...])
    n_two, r_two = norm(middle)
    b = (n_two * gain_two[...]).astype(BF)
    act, slope = gelu_parts(nn(b, w_up[...]))
    act = act.astype(BF)
    predicted = middle + nn(act, w_down[...])
    for at, block in enumerate(units(predicted)):
        pred_out[at * length : (at + 1) * length, :] = block.astype(BF)
    stats[...] = jnp.zeros_like(stats)
    stats[0:1, :] = jnp.sum(predicted, 0, keepdims=True)
    stats[1:2, :] = jnp.sum(predicted * predicted, 0, keepdims=True)

    homes = (((g_mine,), 0), ((g_theirs,), 0), ((g_mine,), 1), ((g_theirs,), 1))
    grad_low = cot[...]
    d_pre = (nt(grad_low, w_down[...]) * slope).astype(BF)
    source = rows_at[...]
    grad_turned, b_turned = turned(source, grad_low), turned(source, b)
    for shard, (home, at) in enumerate(homes):
        cut = slice(shard * hid, (shard + 1) * hid)
        blocks = units(nn(b_turned, d_pre[:, cut])) + units(nn(grad_turned, act[:, cut]))
        for block, value in enumerate(blocks):
            segments.put(home, at, 4 * cols // 128 + block, value)
    d_middle, d_gain_two = norm_back(n_two, r_two, gain_two[...], nt(d_pre, w_up[...]))
    grad_mid = grad_low.astype(F32) + d_middle
    mid_low = grad_mid.astype(BF)
    d_mixed[...] = nt(w_out[...], mid_low).astype(BF)
    attend_back(qkv, probs, d_mixed, d_qkv, per, P_HEAD_DIM)
    a_turned, mid_turned = turned(source, a), turned(source, mid_low)
    for shard, (home, at) in enumerate(homes):
        g_qkv = nt(a_turned, d_qkv[shard * 3 * cols : (shard + 1) * 3 * cols, :])
        g_out = nt(mid_turned, mixed[shard * cols : (shard + 1) * cols, :])
        for block, value in enumerate(units(jnp.concatenate([g_qkv, g_out], 1))):
            segments.put(home, at, block, value)
    d_value, d_gain_one = norm_back(n_one, r_one, gain_one[...], tn(d_qkv[...], w_qkv[...]))
    d_start = grad_mid + d_value
    d_gains[...] = jnp.zeros_like(d_gains)
    d_gains[0:1, :] = d_gain_one
    d_gains[1:2, :] = d_gain_two
    d_gains[2:3, :] = jnp.sum(jnp.where(hidden_mask, d_start, 0.0), 0, keepdims=True)
    d_low = jnp.where(hidden_mask, 0.0, d_start).astype(BF)
    d_embedded[...] = d_low
    d_enc[...] = nn(d_low, w_embed[...])


def enc_down_kernel(first, pos, rows_at, grad, hidden, *homes):
    width = hidden.shape[1] // SHARDS
    segments = Segments(grad.shape[1], width)
    grad_turned = turned(rows_at[...], grad[...].astype(BF))
    for at in range(2):
        shard = first + 2 * at
        for block, value in enumerate(units(nn(grad_turned, hidden[:, shard * width : (shard + 1) * width]))):
            segments.put(homes, at, block, value)


def enc_up_kernel(pos, rows_at, grad, middle, gain, slope, *refs):
    ups, downs, (grad_mid, d_gain, mine), theirs = refs[:6], refs[6:12], refs[12:15], refs[15:]
    side = pos[1]
    width = ups[0].shape[1]
    value = middle[...]
    segments = Segments(value.shape[1], width)
    n_two, r_two = norm(value)
    b_turned = turned(rows_at[...], (n_two * gain[...]).astype(BF))
    homes = (((mine,), 0), (theirs, 0), ((mine,), 1), (theirs, 1))
    low = grad[...].astype(BF)
    d_b = jnp.zeros_like(value)
    pieces = hidden_pieces(side, ups, width)
    for piece in (1, 4, 5, 0, 2, 3):
        up, first, size = pieces[piece]
        home, at = homes[(0, 1, 2, 2, 3, 3)[piece]]
        d_pre = (nt(low, downs[piece][...]) * slope[:, columns(first, size)].astype(F32)).astype(BF)
        d_b = d_b + nt(d_pre, up[...])
        blocks = units(nn(b_turned, d_pre))

        def put(first_block, home=home, at=at, blocks=blocks):
            for block, part in enumerate(blocks):
                segments.put(home, at, first_block + block, part)

        if piece < 2:
            put(0)
        else:
            second_half = side if piece in (2, 4) else 1 - side
            pl.when(second_half == 0)(lambda put=put: put(0))
            pl.when(second_half == 1)(lambda put=put, blocks=blocks: put(len(blocks)))
    d_middle, d_gain_two = norm_back(n_two, r_two, gain[...], d_b)
    grad_mid[...] = grad[...] + d_middle
    d_gain[...] = d_gain_two


def enc_attn_back_kernel(
    pos, x, gain, grad, qkv, probs, own, core, d_x, e_x, d_c, e_c, d_qkv, d_input, d_gain, far, d_mixed
):
    side = pos[1]
    half = d_x.shape[0]
    per = own.shape[0] // 4 // HEAD_DIM
    cols = per * HEAD_DIM
    for at, (first, second) in enumerate(((d_x, e_x), (d_c, e_c))):
        far[at, pl.ds(pl.multiple_of(side * half, half), half), :] = first[...]
        far[at, pl.ds(pl.multiple_of((1 - side) * half, half), half), :] = second[...]
    packs = (own, core, far.at[0], far.at[1])
    low = grad[...].astype(BF)
    for shard, pack in enumerate(packs):
        d_mixed[shard * cols : (shard + 1) * cols, :] = nt(pack[3 * cols :, :], low).astype(BF)
    attend_back(qkv, probs, d_mixed, d_qkv, per, HEAD_DIM)
    value = x[...].astype(F32)
    length = value.shape[0]
    normed, inverse = norm(value)
    d_a = jnp.zeros_like(value)
    for shard in range(SHARDS):
        d_a = d_a + tn(d_qkv[shard * 3 * cols : (shard + 1) * 3 * cols, :], packs[shard][: 3 * cols, :])
    d_value, d_gain_one = norm_back(normed, inverse, gain[...], d_a)
    d_gain[...] = d_gain_one
    for at, block in enumerate(units(grad[...] + d_value)):
        d_input[at * length : (at + 1) * length, :] = block.astype(BF)


def enc_attn_weights_kernel(
    pos, rows_at, x, gain, grad, mixed, d_qkv, d_embedded, enc, d_gain_one, d_gain_two, p_d_gains, mine, *theirs
):
    me = pos[0]
    value = x[...].astype(F32)
    width = value.shape[1]
    cols = width // SHARDS
    normed, _ = norm(value)
    source = rows_at[...]
    a_turned = turned(source, (normed * gain[...]).astype(BF))
    mid_turned = turned(source, grad[...].astype(BF))
    channels = d_embedded.shape[1]
    e_cols = channels // SHARDS
    row = lax.broadcasted_iota(jnp.int32, (channels, SHARDS * 128), 0)
    column = lax.broadcasted_iota(jnp.int32, (channels, SHARDS * 128), 1)
    within = column & 127
    one_hot = ((((column >> 7) ^ me) * e_cols + within == row) & (within < e_cols)).astype(BF)
    g_embed = nn(turned(source, enc[...]), nn(d_embedded[...], one_hot).astype(BF))
    line = lax.broadcasted_iota(jnp.int32, (8, width), 0)
    lines = jnp.where(line == 0, d_gain_one[...], jnp.where(line == 1, d_gain_two[...], 0.0)).astype(BF)
    lane = lax.broadcasted_iota(jnp.int32, (8, 128), 1) - lax.broadcasted_iota(jnp.int32, (8, 128), 0)
    n_rows, n_small = pos[2], pos[3]
    device = ((source.astype(F32) + 0.5) / n_rows.astype(F32)).astype(jnp.int32)
    within_device = source - device * n_rows
    p_source = device * n_small + jnp.where(within_device >= n_small, within_device - n_small, within_device)
    p_one_hot = (lax.broadcasted_iota(jnp.int32, (width, channels), 1) == p_source).astype(BF)
    g_small = nn(turned(source, lines), (lane == e_cols).astype(BF)) + nn(
        nt(p_one_hot, p_d_gains[...].astype(BF)).astype(BF), (lane == e_cols + 2).astype(BF)
    )

    segments = Segments(width, 4 * cols + 128)
    homes = (((mine,), 0), (theirs, 0), ((mine,), 1), (theirs, 1))
    for shard in (1, 3, 0, 2):
        home, at = homes[shard]
        g_qkv = nt(a_turned, d_qkv[shard * 3 * cols : (shard + 1) * 3 * cols, :])
        g_out = nt(mid_turned, mixed[shard * cols : (shard + 1) * cols, :])
        blocks = units(jnp.concatenate([g_qkv, g_out], 1)) + [g_embed[:, shard * 128 : (shard + 1) * 128] + g_small]
        for block, part in enumerate(blocks):
            segments.put(home, at, block, part)


def in_order_kernel(pos, own, core, x, xc, out):
    length = out.shape[1]
    for shard, ref in enumerate((own, core, x, xc)):
        for at in range(out.shape[2] // 128):
            out[pos[0] ^ shard, :, at * 128 : (at + 1) * 128] = ref[at * length : (at + 1) * length, :]


def swap(value, axis, bit):
    size = lax.axis_size(axis)
    return lax.ppermute(value, axis, [(i, i ^ bit) for i in range(size)])


def pick(value, index, axis=0):
    return lax.dynamic_index_in_dim(value, index, axis, keepdims=False)


def finals(total, cuts):
    results = []
    for first, size, count, is_turned in cuts:
        parts = [total[:, first + at * size : first + (at + 1) * size] for at in range(count)]
        results.append(jnp.stack(parts) if count > 1 else parts[0].T if is_turned else parts[0])
    return results


def source_rows(width):
    size = lax.axis_size("dp")
    number = jnp.arange(8, dtype=jnp.int32)
    owner = (lax.axis_index("dp") & 7) ^ (number >> 2 | number & 2 | (number & 1) << 2)
    inner = jnp.arange(width // 8, dtype=jnp.int32).reshape(1, size // 8, width // size)
    high = jnp.arange(size // 8, dtype=jnp.int32)[None, :, None]
    rows = (high * 8 + owner[:, None, None]) * (width // size) + inner % (width // size)
    return rows.reshape(width, 1)


def body(
    patches, segment_ids, mask_slots, gain_attn, qkv_weight, out_weight, gain_mlp, up_weight, down_weight,
    embed_weight, mask_token, pred_gain_attn, pred_qkv, pred_out, pred_gain_mlp, pred_up, pred_down, cotangent,
):
    me = lax.axis_index("mp")
    side = lax.axis_index("dp") % 2
    dp_size = lax.axis_size("dp")
    length, width = patches.shape[1:]
    channels = cotangent.shape[2]
    cols, hid = qkv_weight.shape[2], up_weight.shape[1]
    p_cols, p_hid = pred_qkv.shape[2], pred_up.shape[1]
    heads = SHARDS * cols // HEAD_DIM
    p_heads = SHARDS * p_cols // P_HEAD_DIM
    pos = jnp.stack([me, side, width // dp_size, channels // dp_size]).astype(jnp.int32)

    attn_own, attn_direct = call(
        pack_attn_kernel, [((4 * cols, width), BF), ((2 * cols, width), BF)],
        (pos, jnp.swapaxes(qkv_weight, 1, 2), out_weight), 1,
    )
    up_direct, down_direct, p_own = call(
        pack_rest_kernel,
        [((width, hid // 2), BF), ((hid // 2, width), BF), ((6 * p_cols + channels + p_hid, channels), BF)],
        (pos, up_weight, down_weight, jnp.swapaxes(pred_qkv, 1, 2), pred_out, embed_weight.T, pred_up, pred_down), 3,
        tokens=(attn_direct,),
    )

    attn_core, up_core, down_core = swap(attn_own, "mp", 1), swap(up_weight, "mp", 1), swap(down_weight, "mp", 1)
    p_core = swap(p_own, "mp", 1)
    attn_x = swap(attn_direct, "mp", 2)
    attn_x, up_direct = gate([attn_x, up_direct], [p_own])
    up_x = swap(up_direct, "mp", 2)
    attn_y = swap(attn_x, "dp", 1)
    (down_direct,) = gate([down_direct], [up_x])
    down_x = swap(down_direct, "mp", 2)
    up_y = swap(up_x, "dp", 1)
    (p_send,) = gate([p_own], [down_x])
    p_x = swap(p_send, "mp", 2)
    attn = (attn_own, attn_core, attn_x, attn_y, swap(attn_x, "mp", 1), swap(attn_y, "mp", 1))

    x = pick(patches, me)
    segments = pick(segment_ids, me)
    seg_row, seg_col = segments[None, :], segments[:, None]
    slots = pick(mask_slots, me)
    masked = jnp.any(jnp.arange(length, dtype=jnp.int32)[:, None] == slots[None, :], -1, keepdims=True).astype(F32)
    cot = pick(cotangent, me)
    row = lambda gain: gain.astype(F32)[None, :]
    rows_at, p_rows_at = source_rows(width), source_rows(channels)
    n_rows, n_small = width // dp_size, channels // dp_size

    middle, qkv, probs, mixed = call(
        enc_attn_kernel,
        [((length, width), F32), ((3 * width, length), BF), ((heads, length, length), BF), ((width, length), BF)],
        (pos, x, seg_row, seg_col, row(gain_attn)) + attn, 9,
        [((2, 4 * cols, width), BF)],
    )
    (up_y,) = gate([up_y], [middle])
    up = (up_weight, up_core, up_x, up_y, swap(up_x, "mp", 1), swap(up_y, "mp", 1))
    down_y = swap(down_x, "dp", 1)
    hidden, slope = call(
        enc_up_forward_kernel, [((length, SHARDS * hid), BF), ((length, SHARDS * hid), BF)],
        (pos, middle, row(gain_mlp)) + up, 6,
    )
    (down_y,) = gate([down_y], [hidden])
    down = (down_weight, down_core, down_x, down_y, swap(down_x, "mp", 1), swap(down_y, "mp", 1))
    (enc,) = call(enc_down_forward_kernel, [((length, width), BF)], (pos, middle, hidden) + down, 4)
    (p_x,) = gate([p_x], [enc])
    p_packs = (p_send, p_core, p_x, swap(p_x, "mp", 1))
    p_seg, d_seg = Segments(channels, 4 * p_cols + 2 * p_hid), Segments(width, hid)
    u_seg, a_seg = Segments(width, hid), Segments(width, 4 * cols + 128)
    p_blocks, x_blocks = channels // 128, width // 128
    predicted, stats, p_mine, p_theirs, d_embedded, d_enc, p_d_gains = call(
        pred_kernel,
        [((p_blocks * length, 128), BF), ((8, channels), F32), (p_seg.shape, BF), (p_seg.shape, BF), ((length, channels), BF),
         ((length, width), F32), ((8, channels), F32)],
        (pos, enc, seg_row, seg_col, masked, row(mask_token), row(pred_gain_attn), row(pred_gain_mlp), cot, p_rows_at)
        + p_packs, 30,
        [((3 * channels, channels), BF), ((channels, channels), BF), ((channels, width), BF),
         ((channels, SHARDS * p_hid), BF), ((SHARDS * p_hid, channels), BF), ((3 * channels, length), BF),
         ((p_heads, length, length), BF), ((channels, length), BF), ((channels, length), BF),
         ((3 * channels, length), BF)],
    )

    p_cuts = [(0, p_cols, 3, False), (3 * p_cols, p_cols, 1, False), (4 * p_cols, p_hid, 1, False), (4 * p_cols + p_hid, p_hid, 1, False)]
    d_cuts, u_cuts = [(0, hid, 1, False)], [(0, hid, 1, False)]
    a_cuts = [(0, cols, 3, False), (3 * cols, cols, 1, True), (4 * cols, p_cols, 1, False), (4 * cols + p_cols, 128 - p_cols, 1, True)]
    small = dp_size == 8

    def sums_of(pieces, tokens, micros, sums=()):
        outs = [segments for segments, _, _ in pieces]
        if small:
            cuts = [(seg.eighth, cut) for _, seg, cut in pieces]
            return combine(outs, tokens, micros, sums, kind=F32, cuts=cuts)
        totals = combine(outs, tokens, micros, sums, kind=F32)
        groups = [[high * 8 + low for high in range(dp_size // 8)] for low in range(8)]
        results = []
        for total, (_, seg, cut) in zip(totals, pieces):
            total = total.reshape(seg.left + seg.right, -1, 128)
            total = lax.psum_scatter(total, "dp", scatter_dimension=1, axis_index_groups=groups, tiled=True)
            results += finals(jnp.swapaxes(total, 0, 1).reshape(total.shape[1], -1), cut)
        return results + list(totals[len(pieces) :])

    def from_core(theirs):
        return [swap(part, "mp", 1) for part in theirs]

    def both(own, at, size):
        mine, away = own
        segments, start = [], 0
        for part in away:
            low, high = max(at, start), min(at + size, start + part.shape[0])
            if low < high:
                segments.append([(mine, low, high - low), (part, low - start, high - low)])
            start += part.shape[0]
        return segments

    def with_term(segments, array, at):
        result = []
        for parts in segments:
            result.append(parts + [(array, at, parts[0][2])])
            at += parts[0][2]
        return result

    def first(own, seg):
        return both(own, *seg.over_x), both(own, *seg.over_y)

    def second(own, seg, got):
        (x, x_at), (y, y_at) = got
        return with_term(both(own, *seg.then_x), y, y_at + seg.b), with_term(both(own, *seg.then_y), x, x_at + seg.a)

    def kept(own, seg, got, then, low, high, extra=()):
        segments = []
        for (start, size), over, after, right in (
            (seg.keep_left, got[0], then[1], 0), (seg.keep_right, got[1], then[0], 1)
        ):
            at, rows = low * size // 4, (high - low) * size // 4
            part = both(own, start + at, rows)
            for array, array_at in (over, after):
                part = with_term(part, array, array_at + at)
            for array, array_at in extra:
                part = with_term(part, array, array_at + right * seg.a * (high - low) // 4)
            segments += part
        return segments

    def stage(parts, tokens, micros, sums=(), z=()):
        outs = [sum((x for x, _ in parts), []), sum((y for _, y in parts), [])] if parts else []
        send = combine(outs + list(z), tokens, micros, sums)
        got, at = ((swap(send[0], "mp", 2), swap(send[1], "dp", 1)) if parts else ()), [0, 0]
        places = []
        for x, y in parts:
            places.append(((got[0], at[0]), (got[1], at[1])))
            at = [at[0] + sum(p[0][2] for p in x), at[1] + sum(p[0][2] for p in y)]
        return send, got, places

    p_away = swap(p_theirs, "mp", 1)
    d_theirs = call(partial(enc_down_kernel, 1), d_seg.parts(), (pos, rows_at, d_enc, hidden), 30)
    (d_mine,) = call(partial(enc_down_kernel, 0), [(d_seg.shape, BF)], (pos, rows_at, d_enc, hidden), 30, tokens=d_theirs[:1])
    p_own, d_own = (p_mine, [p_away]), (d_mine, from_core(d_theirs))
    send, p_arrived, (p_got, d_got, at_predicted) = stage(
        [first(p_own, p_seg), first(d_own, d_seg), ([[(predicted, 0, predicted.shape[0])]], [])], [], 30
    )
    grad_mid, d_gain_two, u_mine, *u_theirs = call(
        enc_up_kernel,
        [((length, width), F32), ((1, width), F32), (u_seg.shape, BF)] + u_seg.parts(),
        (pos, rows_at, d_enc, middle, row(gain_mlp), slope) + up + down, 100, tokens=send,
    )
    u_away = from_core(u_theirs)
    d_qkv, d_input, d_gain_one = call(
        enc_attn_back_kernel,
        [((3 * width, length), BF), ((x_blocks * length, 128), BF), ((1, width), F32)],
        (pos, x, row(gain_attn), grad_mid, qkv, probs) + attn, 1,
        [((2, 4 * cols, width), BF), ((width, length), BF)],
    )
    got_x, got_y, *u_away[:2] = gate([*p_arrived, *u_away[:2]], [d_gain_one])
    moved = lambda places: ((got_x, places[0][1]), (got_y, places[1][1]))
    p_got, d_got, u_own = moved(p_got), moved(d_got), (u_mine, u_away)
    predicted_x = lax.slice_in_dim(got_x, at_predicted[0][1], got_x.shape[0])
    filler = [[(d_input, 0, p_seg.b - p_seg.a)]]
    send, _, (u_got, d_then, p_then, _) = stage(
        [first(u_own, u_seg), second(d_own, d_seg, d_got), second(p_own, p_seg, p_got), ([], filler)], [], 30
    )
    predicted, predicted_x, d_input = gate([predicted, predicted_x, d_input], send)
    a_mine, *a_theirs = call(
        enc_attn_weights_kernel, [(a_seg.shape, BF)] + a_seg.parts(),
        (pos, rows_at, x, row(gain_attn), grad_mid, mixed, d_qkv, d_embedded, enc, d_gain_one, d_gain_two, p_d_gains), 100, tokens=send,
    )
    a_own = (a_mine, from_core(a_theirs))
    a_send, _, (a_got,) = stage([first(a_own, a_seg)], [], 0)
    p_z = (p_own, p_seg, p_got, p_then)
    d_z = (d_own, d_seg, d_got, d_then)
    (*u_send, z_send), _, (u_then,) = stage(
        [second(u_own, u_seg, u_got)], a_send, 3, (), [kept(*p_z, 2, 4) + kept(*d_z, 2, 4)]
    )
    (stats,) = gate([stats], u_send)
    u_z = (u_own, u_seg, u_got, u_then)
    stats_got, z_got = swap(stats, "mp", 1), swap(z_send, "dp", 2)
    p_rows, d_rows, u_rows = ((seg.a + seg.b) // 4 for seg in (p_seg, d_seg, u_seg))
    p_one, d_one = (z_got, 0), (z_got, 2 * p_rows)

    def later(one, seg, quarter):
        array, at = one
        return [(array, at + quarter * seg.a // 4), (array, at + seg.a // 2 + quarter * seg.b // 4)]

    def last(z, one, quarter, two=None):
        own, seg, got, then = z
        segments = []
        lefts_rights = later(one, seg, quarter)
        for part, (start, size), over, after, (array, at), shift in (
            (0, seg.keep_left, got[0], then[1], lefts_rights[0], 0), (1, seg.keep_right, got[1], then[0], lefts_rights[1], seg.a // 4)
        ):
            begin, rows = quarter * size // 4, size // 4
            terms = both(own, start + begin, rows)
            for more, more_at in (over, after):
                terms = with_term(terms, more, more_at + begin)
            terms = with_term(terms, array, at)
            if two is not None:
                terms = with_term(terms, two[0], two[1] + shift)
            segments += terms
        return segments

    filler = [[(a_got[0][0], 0, a_seg.b - a_seg.a)]]
    (*a_send, z_send, stats), _, (a_then, _) = stage(
        [second(a_own, a_seg, a_got), ([], filler)], u_send, 3, (stats, stats_got), [last(p_z, p_one, 1) + last(d_z, d_one, 1)]
    )
    a_z = (a_own, a_seg, a_got, a_then)
    z_got = swap(z_send, "dp", 4)
    (z_send,) = combine([kept(*u_z, 2, 4)], a_send, 3)
    u_one, stats_got = (swap(z_send, "dp", 2), 0), swap(stats, "dp", 2)
    predicted, predicted_x = gate([predicted, predicted_x], [z_send])
    predicted_c, predicted_xc = swap(predicted, "mp", 1), swap(predicted_x, "mp", 1)
    z_send, z_send_u = combine([kept(*a_z, 2, 4), last(u_z, u_one, 1)], [z_send], 3)
    a_one, u_two = (swap(z_send, "dp", 2), 0), (swap(z_send_u, "dp", 4), 0)
    d_input, p_two_array = gate([d_input, z_got], [z_send])
    p_two, d_two = (p_two_array, 0), (p_two_array, p_rows)
    input_x, input_c = swap(d_input, "mp", 2), swap(d_input, "mp", 1)
    *p_results, r_down, stats = sums_of(
        [(last(p_z, p_one, 0, p_two), p_seg, p_cuts), (last(d_z, d_one, 0, d_two), d_seg, d_cuts)], [z_send], 3,
        (stats, stats_got),
    )
    stats_got = swap(stats, "dp", 4)
    z_send, stats = combine([last(a_z, a_one, 1)], [p_results[1]], 3, (stats, stats_got))
    a_two = (swap(z_send, "dp", 4), 0)
    (input_x,) = gate([input_x], [z_send])
    r_up, stats = sums_of([(last(u_z, u_one, 0, u_two), u_seg, u_cuts)], [z_send], 3, (stats, swap(stats, "mp", 2)))
    stats_got = swap(stats, "dp", 1)
    (predictions,) = call(
        in_order_kernel, [((SHARDS, length, channels), BF)], (pos, predicted, predicted_c, predicted_x, predicted_xc), 3,
        tokens=(r_up,),
    )
    (patches_grad,) = call(
        in_order_kernel, [((SHARDS, length, width), BF)], (pos, d_input, input_c, input_x, swap(input_x, "mp", 1)), 2,
        tokens=(predictions,),
    )
    *a_results, stats = sums_of([(last(a_z, a_one, 0, a_two), a_seg, a_cuts)], [patches_grad], 3, (stats, stats_got))
    for at in range(3, dp_size.bit_length() - 1):
        stats = stats + swap(stats, "dp", 1 << at)

    count = dp_size * patches.shape[0] * length
    mean, square = stats[0] / count, stats[1] / count
    n_var = channels // SHARDS
    variance = lax.dynamic_slice_in_dim(square - mean * mean, me * n_var, n_var)
    tail = a_results[3]

    return (
        predictions,
        patches_grad,
        variance,
        tail[0],
        a_results[0],
        a_results[1],
        tail[1],
        r_up,
        r_down.T,
        a_results[2],
        tail[4, :n_small],
        tail[2, :n_small],
        p_results[0],
        p_results[1].T,
        tail[3, :n_small],
        p_results[2],
        p_results[3].T,
    )


def solution(mesh):
    placed = (
        P("dp", None, None), P("dp", None), P("dp", None), P(), P(None, None, "mp"), P("mp", None), P(),
        P(None, "mp"), P("mp", None), P(None, "mp"), P(), P(), P(None, None, "mp"), P("mp", None), P(),
        P(None, "mp"), P("mp", None), P("dp", None, None),
    )
    return jax.shard_map(
        body,
        mesh=mesh,
        in_specs=placed,
        out_specs=(
            P("dp", None, None), P("dp", None, None), P("mp"), P("dp"), P(None, "dp", "mp"), P("mp", "dp"),
            P("dp"), P("dp", "mp"), P("mp", "dp"), P("dp", "mp"), P("dp"), P("dp"), P(None, "dp", "mp"),
            P("mp", "dp"), P("dp"), P("dp", "mp"), P("mp", "dp"),
        ),
        check_vma=False,
    )
```

```python
import math
from functools import partial

import jax
import jax.numpy as jnp
from jax import lax
from jax.experimental import pallas as pl
from jax.experimental.pallas import tpu as pltpu
from jax.sharding import PartitionSpec as P

HEAD_DIM = 64
P_HEAD_DIM = 32
SHARDS = 4
EPS = 1e-06
BF = jnp.bfloat16
F32 = jnp.float32
COST = 1.15e9
VMEM_BYTES = 48 * 1024 * 1024


def contract(left, right, at_left, at_right):
    return lax.dot_general(left, right, (((at_left,), (at_right,)), ((), ())), preferred_element_type=F32)


def nn(left, right):
    return contract(left, right, 1, 0)


def nt(left, right):
    return contract(left, right, 1, 1)


def tn(left, right):
    return contract(left, right, 0, 0)


def norm(value):
    centred = value - jnp.mean(value, -1, keepdims=True)
    inverse = lax.rsqrt(jnp.mean(centred * centred, -1, keepdims=True) + EPS)
    return centred * inverse, inverse


def norm_back(normed, inverse, gain, grad):
    scaled = grad * gain
    along = jnp.mean(scaled * normed, -1, keepdims=True)
    d_value = (scaled - jnp.mean(scaled, -1, keepdims=True) - normed * along) * inverse
    return d_value, jnp.sum(grad * normed, 0, keepdims=True)


def gelu_parts(pre):
    cdf = 0.5 * (1.0 + lax.erf(pre * 0.7071067811865476))
    density = 0.3989422804014327 * jnp.exp(-0.5 * pre * pre)
    return pre * cdf, cdf + pre * density


def turned(source_rows, value):
    width = value.shape[1]
    one_hot = (lax.broadcasted_iota(jnp.int32, (width, width), 1) == source_rows).astype(BF)
    return nt(one_hot, value).astype(BF)


def head_rows(head, per, head_dim):
    shard = head // per
    first = shard * (3 * per * head_dim) + (head - shard * per) * head_dim
    return [pl.ds(pl.multiple_of(first + part * per * head_dim, head_dim), head_dim) for part in range(3)]


def attend(qkv_ref, probs_ref, mixed_ref, same, per, head_dim):
    factor = head_dim ** (-0.5) * math.log2(math.e)

    def one_head(head, carry):
        q_at, k_at, u_at = head_rows(head, per, head_dim)
        scores = jnp.where(same, tn(qkv_ref[k_at, :], qkv_ref[q_at, :]), -1e9)
        top = jnp.max(scores, 0, keepdims=True)
        expd = jnp.exp2((scores - top) * factor)
        probs = (expd * (1.0 / jnp.sum(expd, 0, keepdims=True))).astype(BF)
        probs_ref[head] = probs
        at = pl.ds(pl.multiple_of(head * head_dim, head_dim), head_dim)
        mixed_ref[at, :] = nn(qkv_ref[u_at, :], probs).astype(BF)
        return carry

    lax.fori_loop(0, SHARDS * per, one_head, 0, unroll=6)


def attend_back(qkv_ref, probs_ref, d_mixed_ref, d_qkv_ref, per, head_dim):
    scale = head_dim ** (-0.5)

    def one_head(head, carry):
        q_at, k_at, u_at = head_rows(head, per, head_dim)
        at = pl.ds(pl.multiple_of(head * head_dim, head_dim), head_dim)
        d_mixed = d_mixed_ref[at, :]
        low = probs_ref[head]
        probs = low.astype(F32)
        d_probs = tn(qkv_ref[u_at, :], d_mixed)
        along = jnp.sum(d_probs * probs, 0, keepdims=True)
        d_scores = (probs * (d_probs - along)).astype(BF)
        d_qkv_ref[q_at, :] = (nn(qkv_ref[k_at, :], d_scores) * scale).astype(BF)
        d_qkv_ref[k_at, :] = (nt(qkv_ref[q_at, :], d_scores) * scale).astype(BF)
        d_qkv_ref[u_at, :] = nt(d_mixed, low).astype(BF)
        return carry

    lax.fori_loop(0, SHARDS * per, one_head, 0, unroll=6)


ANYWHERE = pl.BlockSpec(memory_space=pl.ANY)


def in_hbm(arrays, least=256 * 1700):
    return [pltpu.with_memory_space_constraint(a, pltpu.HBM) if n_bytes(a) >= least else a for a in arrays]


def n_bytes(array):
    return math.prod(array.shape) * array.dtype.itemsize


ANYWHERE = pl.BlockSpec(memory_space=pl.ANY)


def in_hbm(arrays, least=256 * 1700):
    return [pltpu.with_memory_space_constraint(a, pltpu.HBM) if n_bytes(a) >= least else a for a in arrays]


def n_bytes(array):
    return math.prod(array.shape) * array.dtype.itemsize


def call(kernel, outs, args, micros, scratch=(), tokens=()):
    shapes = [jax.ShapeDtypeStruct(shape, kind) for shape, kind in outs]
    moved = sum(math.prod(a.shape) * a.dtype.itemsize for a in list(args) + shapes)
    n_args, n_all = len(args), len(args) + len(tokens)
    return pl.pallas_call(
        lambda *refs: kernel(*refs[:n_args], *refs[n_all:]),
        out_shape=shapes,
        in_specs=[pl.BlockSpec(memory_space=pltpu.SMEM)]
        + [pl.BlockSpec(memory_space=pltpu.VMEM)] * (n_args - 1)
        + [ANYWHERE] * len(tokens),
        out_specs=[pl.BlockSpec(memory_space=pltpu.VMEM)] * len(shapes),
        scratch_shapes=[pltpu.VMEM(shape, kind) for shape, kind in scratch],
        compiler_params=pltpu.CompilerParams(vmem_limit_bytes=VMEM_BYTES),
        cost_estimate=pl.CostEstimate(flops=int(micros * COST), bytes_accessed=moved if micros else 0, transcendentals=0),
    )(*args, *in_hbm(tokens, 0))


def gate(values, tokens):
    return pl.pallas_call(
        lambda *refs: None,
        out_shape=[jax.ShapeDtypeStruct(v.shape, v.dtype) for v in values],
        in_specs=[ANYWHERE] * (len(values) + len(tokens)),
        out_specs=[ANYWHERE] * len(values),
        input_output_aliases={at: at for at in range(len(values))},
    )(*in_hbm(values), *in_hbm(tokens, 0))


def units(value):
    return [value[:, at * 128 : (at + 1) * 128] for at in range(value.shape[1] // 128)]


class Segments:
    def __init__(self, rows, cols):
        self.eighth, blocks = rows // 8, cols // 128
        self.left, self.right = blocks // 2, blocks - blocks // 2
        a, b = 4 * self.eighth * self.left, 4 * self.eighth * self.right
        self.over_x, self.over_y = (0, 2 * a), (2 * a, 2 * b)
        self.then_y, self.then_x = (2 * a + 2 * b, a), (3 * a + 2 * b, b)
        self.keep_left, self.keep_right = (3 * a + 3 * b, a), (4 * a + 3 * b, b)
        self.shape = (4 * (a + b), 128)
        self.a, self.b = a, b

    def put(self, refs, shard, block, value):
        a, b, size = self.a, self.b, self.eighth
        if shard:
            starts_left = (self.over_x[0], self.over_x[0] + a)
            starts_right = (self.then_x[0], self.over_y[0] + b)
        else:
            starts_left = (self.keep_left[0], self.then_y[0])
            starts_right = (self.keep_right[0], self.over_y[0])
        is_left = block < self.left
        count, index = (self.left, block) if is_left else (self.right, block - self.left)
        for number in range(8):
            start = (starts_left if is_left else starts_right)[number // 4]
            at = start + (number % 4 * count + index) * size
            for ref in refs:
                if at < ref.shape[0]:
                    ref[at : at + size, :] = value[number * size : (number + 1) * size].astype(BF)
                    break
                at -= ref.shape[0]

    def parts(self):
        return [((size, 128), BF) for size in (self.over_x[1], self.over_y[1], 2 * (self.a + self.b))]


def combine(outs, tokens, micros, sums=(), kind=BF, cuts=None):
    arrays, terms = [], []
    for segments in outs:
        for parts in segments:
            for array, first, size in parts:
                if not any(array is known for known in arrays):
                    arrays.append(array)
                terms.append((next(i for i, known in enumerate(arrays) if known is array), first, size))
    n_sums, n_arrays, n_out, n_terms = len(sums), len(arrays), len(outs), len(terms)
    n_in = n_sums + n_arrays + len(tokens)
    sizes = [sum(parts[0][2] for parts in segments) for segments in outs]
    shapes = [jax.ShapeDtypeStruct((size, 128), kind) for size in sizes]
    n_results = n_out
    if cuts:
        shapes = []
        for (rows, cut) in cuts:
            for first, size, count, is_turned in cut:
                shape = (count, rows, size) if count > 1 else (size, rows) if is_turned else (rows, size)
                shapes.append(jax.ShapeDtypeStruct(shape, F32))
        n_results = len(shapes)

    def kernel(*refs):
        held, sem = refs[-1 - n_terms : -1], refs[-1]
        totals = refs[n_in : n_in + n_out] if not cuts else refs[n_in + n_results + bool(sums) : -1 - n_terms]
        copies = [
            pltpu.make_async_copy(refs[n_sums + which].at[pl.ds(first, size), :], held[at], sem.at[at])
            for at, (which, first, size) in enumerate(terms)
        ]
        for copy in copies:
            copy.start()
        if sums:
            refs[n_in + n_results][...] = refs[0][...] + refs[1][...]
        at = 0
        for out, segments in zip(totals, outs):
            row = 0
            for parts in segments:
                size = parts[0][2]
                mine = list(range(at, at + len(parts)))
                for term in mine:
                    copies[term].wait()

                def add(step, carry, row=row, mine=mine, out=out):
                    here = pl.ds(pl.multiple_of(step * 48, 48), 48)
                    total = held[mine[0]][here, :].astype(F32)
                    for term in mine[1:]:
                        total = total + held[term][here, :].astype(F32)
                    out[pl.ds(pl.multiple_of(row + step * 48, 16), 48), :] = total.astype(kind)
                    return carry

                lax.fori_loop(0, size // 48, add, 0, unroll=2)
                at += len(parts)
                row += size
        if cuts:
            results = iter(refs[n_in : n_in + n_results])
            for out, (rows, cut) in zip(totals, cuts):
                whole = jnp.concatenate([out[u * rows : (u + 1) * rows, :] for u in range(out.shape[0] // rows)], 1)
                for value in finals(whole, cut):
                    next(results)[...] = value

    moved = 256 * (sum(t[2] for t in terms) + sum(sizes))
    in_vmem = pl.BlockSpec(memory_space=pltpu.VMEM)
    return pl.pallas_call(
        kernel,
        out_shape=shapes + ([jax.ShapeDtypeStruct(sums[0].shape, F32)] if sums else []),
        in_specs=[in_vmem] * n_sums + [ANYWHERE] * (n_in - n_sums),
        out_specs=[in_vmem] * (n_results + (1 if sums else 0)),
        scratch_shapes=[pltpu.VMEM((size, 128), F32) for size in sizes if cuts]
        + [pltpu.VMEM((size, 128), BF) for _, _, size in terms]
        + [pltpu.SemaphoreType.DMA((n_terms,))],
        compiler_params=pltpu.CompilerParams(vmem_limit_bytes=VMEM_BYTES),
        cost_estimate=pl.CostEstimate(flops=int(micros * COST), bytes_accessed=moved if micros else 0, transcendentals=0),
    )(*sums, *in_hbm(arrays), *in_hbm(tokens, 0))


def pack_attn_kernel(pos, qkv, out, own, direct):
    cols = qkv.shape[1]
    for part in range(3):
        own[part * cols : (part + 1) * cols, :] = qkv[part]
    own[3 * cols :, :] = out[...]
    half = direct.shape[0]
    direct[...] = own[pl.ds(pl.multiple_of(pos[1] * half, half), half), :]


def pack_rest_kernel(pos, up, down, qkv, out, embed, p_up, p_down, up_direct, down_direct, pred):
    half = up_direct.shape[1]
    at = pl.ds(pl.multiple_of(pos[1] * half, half), half)
    up_direct[...] = up[:, at]
    down_direct[...] = down[at, :]
    width = pred.shape[1]
    row = 0
    for part in (qkv[0], qkv[1], qkv[2], out[...], embed[:, :width], embed[:, width:], p_up[...], p_down[...]):
        pred[row : row + part.shape[0], :] = part
        row += part.shape[0]


def enc_attn_kernel(pos, x, seg_row, seg_col, gain, own, core, d_x, e_x, d_c, e_c, middle, qkv, probs, mixed, far):
    side = pos[1]
    half = d_x.shape[0]
    per = own.shape[0] // 4 // HEAD_DIM
    rows = 3 * per * HEAD_DIM
    for at, (first, second) in enumerate(((d_x, e_x), (d_c, e_c))):
        far[at, pl.ds(pl.multiple_of(side * half, half), half), :] = first[...]
        far[at, pl.ds(pl.multiple_of((1 - side) * half, half), half), :] = second[...]
    value = x[...].astype(F32)
    normed, _ = norm(value)
    low = (normed * gain[...]).astype(BF)
    packs = (own, core, far.at[0], far.at[1])
    for shard, pack in enumerate(packs):
        qkv[shard * rows : (shard + 1) * rows, :] = nt(pack[:rows, :], low).astype(BF)
    attend(qkv, probs, mixed, seg_col[...] == seg_row[...], per, HEAD_DIM)
    total = value
    for shard, pack in enumerate(packs):
        total = total + tn(mixed[shard * rows // 3 : (shard + 1) * rows // 3, :], pack[rows:, :])
    middle[...] = total


def hidden_pieces(side, mats, width):
    half = width // 2
    own, core, d_x, e_x, d_c, e_c = mats
    first, second = side * half, (1 - side) * half
    return (
        (own, 0, width), (core, width, width),
        (d_x, 2 * width + first, half), (e_x, 2 * width + second, half),
        (d_c, 3 * width + first, half), (e_c, 3 * width + second, half),
    )


def columns(first, size):
    return pl.ds(first if isinstance(first, int) else pl.multiple_of(first, 128), size)


def enc_up_forward_kernel(pos, middle, gain, *refs):
    ups, (hidden, slope) = refs[:6], refs[6:]
    width = ups[0].shape[1]
    normed, _ = norm(middle[...])
    low = (normed * gain[...]).astype(BF)
    for up, first, size in hidden_pieces(pos[1], ups, width):
        act, back = gelu_parts(nn(low, up[...]))
        hidden[:, columns(first, size)] = act.astype(BF)
        slope[:, columns(first, size)] = back.astype(BF)


def enc_down_forward_kernel(pos, middle, hidden, *refs):
    downs, out = refs[:6], refs[6]
    total = middle[...]
    for down, first, size in hidden_pieces(pos[1], downs, downs[0].shape[0]):
        total = total + nn(hidden[:, columns(first, size)], down[...])
    out[...] = total.astype(BF)


def pred_kernel(
    pos, enc, seg_row, seg_col, masked, token, gain_one, gain_two, cot, rows_at,
    p_own, p_core, p_x, p_xc,
    pred_out, stats, g_mine, g_theirs, d_embedded, d_enc, d_gains,
    w_qkv, w_out, w_embed, w_up, w_down, qkv, probs, mixed, d_mixed, d_qkv,
):
    me = pos[0]
    length = cot.shape[0]
    cols = w_out.shape[0] // SHARDS
    hid = w_down.shape[0] // SHARDS
    segments = Segments(w_out.shape[0], 4 * cols + 2 * hid)
    per = cols // P_HEAD_DIM
    width = w_out.shape[1]
    for shard, pack in enumerate((p_own, p_core, p_x, p_xc)):
        w_qkv[shard * 3 * cols : (shard + 1) * 3 * cols, :] = pack[: 3 * cols, :]
        w_out[shard * cols : (shard + 1) * cols, :] = pack[3 * cols : 4 * cols, :]
        at = pl.ds(pl.multiple_of((me ^ shard) * cols, 16), cols)
        w_embed[at, :width] = pack[4 * cols : 5 * cols, :]
        w_embed[at, width:] = pack[5 * cols : 6 * cols, :]
        w_up[:, shard * hid : (shard + 1) * hid] = pack[6 * cols : 6 * cols + width, :]
        w_down[shard * hid : (shard + 1) * hid, :] = pack[6 * cols + width :, :]

    hidden_mask = masked[...] > 0.0
    start = jnp.where(hidden_mask, token[...], nt(enc[...], w_embed[...]))
    n_one, r_one = norm(start)
    a = (n_one * gain_one[...]).astype(BF)
    qkv[...] = nt(w_qkv[...], a).astype(BF)
    attend(qkv, probs, mixed, seg_col[...] == seg_row[...], per, P_HEAD_DIM)
    middle = start + tn(mixed[...], w_out[...])
    n_two, r_two = norm(middle)
    b = (n_two * gain_two[...]).astype(BF)
    act, slope = gelu_parts(nn(b, w_up[...]))
    act = act.astype(BF)
    predicted = middle + nn(act, w_down[...])
    for at, block in enumerate(units(predicted)):
        pred_out[at * length : (at + 1) * length, :] = block.astype(BF)
    stats[...] = jnp.zeros_like(stats)
    stats[0:1, :] = jnp.sum(predicted, 0, keepdims=True)
    stats[1:2, :] = jnp.sum(predicted * predicted, 0, keepdims=True)

    homes = (((g_mine,), 0), ((g_theirs,), 0), ((g_mine,), 1), ((g_theirs,), 1))
    grad_low = cot[...]
    d_pre = (nt(grad_low, w_down[...]) * slope).astype(BF)
    source = rows_at[...]
    grad_turned, b_turned = turned(source, grad_low), turned(source, b)
    for shard, (home, at) in enumerate(homes):
        cut = slice(shard * hid, (shard + 1) * hid)
        blocks = units(nn(b_turned, d_pre[:, cut])) + units(nn(grad_turned, act[:, cut]))
        for block, value in enumerate(blocks):
            segments.put(home, at, 4 * cols // 128 + block, value)
    d_middle, d_gain_two = norm_back(n_two, r_two, gain_two[...], nt(d_pre, w_up[...]))
    grad_mid = grad_low.astype(F32) + d_middle
    mid_low = grad_mid.astype(BF)
    d_mixed[...] = nt(w_out[...], mid_low).astype(BF)
    attend_back(qkv, probs, d_mixed, d_qkv, per, P_HEAD_DIM)
    a_turned, mid_turned = turned(source, a), turned(source, mid_low)
    for shard, (home, at) in enumerate(homes):
        g_qkv = nt(a_turned, d_qkv[shard * 3 * cols : (shard + 1) * 3 * cols, :])
        g_out = nt(mid_turned, mixed[shard * cols : (shard + 1) * cols, :])
        for block, value in enumerate(units(jnp.concatenate([g_qkv, g_out], 1))):
            segments.put(home, at, block, value)
    d_value, d_gain_one = norm_back(n_one, r_one, gain_one[...], tn(d_qkv[...], w_qkv[...]))
    d_start = grad_mid + d_value
    d_gains[...] = jnp.zeros_like(d_gains)
    d_gains[0:1, :] = d_gain_one
    d_gains[1:2, :] = d_gain_two
    d_gains[2:3, :] = jnp.sum(jnp.where(hidden_mask, d_start, 0.0), 0, keepdims=True)
    d_low = jnp.where(hidden_mask, 0.0, d_start).astype(BF)
    d_embedded[...] = d_low
    d_enc[...] = nn(d_low, w_embed[...])


def enc_down_kernel(first, pos, rows_at, grad, hidden, *homes):
    width = hidden.shape[1] // SHARDS
    segments = Segments(grad.shape[1], width)
    grad_turned = turned(rows_at[...], grad[...].astype(BF))
    for at in range(2):
        shard = first + 2 * at
        for block, value in enumerate(units(nn(grad_turned, hidden[:, shard * width : (shard + 1) * width]))):
            segments.put(homes, at, block, value)


def enc_up_kernel(pos, rows_at, grad, middle, gain, slope, *refs):
    ups, downs, (grad_mid, d_gain, mine), theirs = refs[:6], refs[6:12], refs[12:15], refs[15:]
    side = pos[1]
    width = ups[0].shape[1]
    value = middle[...]
    segments = Segments(value.shape[1], width)
    n_two, r_two = norm(value)
    b_turned = turned(rows_at[...], (n_two * gain[...]).astype(BF))
    homes = (((mine,), 0), (theirs, 0), ((mine,), 1), (theirs, 1))
    low = grad[...].astype(BF)
    d_b = jnp.zeros_like(value)
    pieces = hidden_pieces(side, ups, width)
    for piece in (1, 4, 5, 0, 2, 3):
        up, first, size = pieces[piece]
        home, at = homes[(0, 1, 2, 2, 3, 3)[piece]]
        d_pre = (nt(low, downs[piece][...]) * slope[:, columns(first, size)].astype(F32)).astype(BF)
        d_b = d_b + nt(d_pre, up[...])
        blocks = units(nn(b_turned, d_pre))

        def put(first_block, home=home, at=at, blocks=blocks):
            for block, part in enumerate(blocks):
                segments.put(home, at, first_block + block, part)

        if piece < 2:
            put(0)
        else:
            second_half = side if piece in (2, 4) else 1 - side
            pl.when(second_half == 0)(lambda put=put: put(0))
            pl.when(second_half == 1)(lambda put=put, blocks=blocks: put(len(blocks)))
    d_middle, d_gain_two = norm_back(n_two, r_two, gain[...], d_b)
    grad_mid[...] = grad[...] + d_middle
    d_gain[...] = d_gain_two


def enc_attn_back_kernel(
    pos, x, gain, grad, qkv, probs, own, core, d_x, e_x, d_c, e_c, d_qkv, d_input, d_gain, far, d_mixed
):
    side = pos[1]
    half = d_x.shape[0]
    per = own.shape[0] // 4 // HEAD_DIM
    cols = per * HEAD_DIM
    for at, (first, second) in enumerate(((d_x, e_x), (d_c, e_c))):
        far[at, pl.ds(pl.multiple_of(side * half, half), half), :] = first[...]
        far[at, pl.ds(pl.multiple_of((1 - side) * half, half), half), :] = second[...]
    packs = (own, core, far.at[0], far.at[1])
    low = grad[...].astype(BF)
    for shard, pack in enumerate(packs):
        d_mixed[shard * cols : (shard + 1) * cols, :] = nt(pack[3 * cols :, :], low).astype(BF)
    attend_back(qkv, probs, d_mixed, d_qkv, per, HEAD_DIM)
    value = x[...].astype(F32)
    length = value.shape[0]
    normed, inverse = norm(value)
    d_a = jnp.zeros_like(value)
    for shard in range(SHARDS):
        d_a = d_a + tn(d_qkv[shard * 3 * cols : (shard + 1) * 3 * cols, :], packs[shard][: 3 * cols, :])
    d_value, d_gain_one = norm_back(normed, inverse, gain[...], d_a)
    d_gain[...] = d_gain_one
    for at, block in enumerate(units(grad[...] + d_value)):
        d_input[at * length : (at + 1) * length, :] = block.astype(BF)


def enc_attn_weights_kernel(
    pos, rows_at, x, gain, grad, mixed, d_qkv, d_embedded, enc, d_gain_one, d_gain_two, p_d_gains, mine, *theirs
):
    me = pos[0]
    value = x[...].astype(F32)
    width = value.shape[1]
    cols = width // SHARDS
    normed, _ = norm(value)
    source = rows_at[...]
    a_turned = turned(source, (normed * gain[...]).astype(BF))
    mid_turned = turned(source, grad[...].astype(BF))
    channels = d_embedded.shape[1]
    e_cols = channels // SHARDS
    row = lax.broadcasted_iota(jnp.int32, (channels, SHARDS * 128), 0)
    column = lax.broadcasted_iota(jnp.int32, (channels, SHARDS * 128), 1)
    within = column & 127
    one_hot = ((((column >> 7) ^ me) * e_cols + within == row) & (within < e_cols)).astype(BF)
    g_embed = nn(turned(source, enc[...]), nn(d_embedded[...], one_hot).astype(BF))
    line = lax.broadcasted_iota(jnp.int32, (8, width), 0)
    lines = jnp.where(line == 0, d_gain_one[...], jnp.where(line == 1, d_gain_two[...], 0.0)).astype(BF)
    lane = lax.broadcasted_iota(jnp.int32, (8, 128), 1) - lax.broadcasted_iota(jnp.int32, (8, 128), 0)
    n_rows, n_small = pos[2], pos[3]
    device = ((source.astype(F32) + 0.5) / n_rows.astype(F32)).astype(jnp.int32)
    within_device = source - device * n_rows
    p_source = device * n_small + jnp.where(within_device >= n_small, within_device - n_small, within_device)
    p_one_hot = (lax.broadcasted_iota(jnp.int32, (width, channels), 1) == p_source).astype(BF)
    g_small = nn(turned(source, lines), (lane == e_cols).astype(BF)) + nn(
        nt(p_one_hot, p_d_gains[...].astype(BF)).astype(BF), (lane == e_cols + 2).astype(BF)
    )

    segments = Segments(width, 4 * cols + 128)
    homes = (((mine,), 0), (theirs, 0), ((mine,), 1), (theirs, 1))
    for shard in (1, 3, 0, 2):
        home, at = homes[shard]
        g_qkv = nt(a_turned, d_qkv[shard * 3 * cols : (shard + 1) * 3 * cols, :])
        g_out = nt(mid_turned, mixed[shard * cols : (shard + 1) * cols, :])
        blocks = units(jnp.concatenate([g_qkv, g_out], 1)) + [g_embed[:, shard * 128 : (shard + 1) * 128] + g_small]
        for block, part in enumerate(blocks):
            segments.put(home, at, block, part)


def in_order_kernel(pos, own, core, x, xc, out):
    length = out.shape[1]
    for shard, ref in enumerate((own, core, x, xc)):
        for at in range(out.shape[2] // 128):
            out[pos[0] ^ shard, :, at * 128 : (at + 1) * 128] = ref[at * length : (at + 1) * length, :]


def swap(value, axis, bit):
    size = lax.axis_size(axis)
    return lax.ppermute(value, axis, [(i, i ^ bit) for i in range(size)])


def pick(value, index, axis=0):
    return lax.dynamic_index_in_dim(value, index, axis, keepdims=False)


def finals(total, cuts):
    results = []
    for first, size, count, is_turned in cuts:
        parts = [total[:, first + at * size : first + (at + 1) * size] for at in range(count)]
        results.append(jnp.stack(parts) if count > 1 else parts[0].T if is_turned else parts[0])
    return results


def source_rows(width):
    size = lax.axis_size("dp")
    number = jnp.arange(8, dtype=jnp.int32)
    owner = (lax.axis_index("dp") & 7) ^ (number >> 2 | number & 2 | (number & 1) << 2)
    inner = jnp.arange(width // 8, dtype=jnp.int32).reshape(1, size // 8, width // size)
    high = jnp.arange(size // 8, dtype=jnp.int32)[None, :, None]
    rows = (high * 8 + owner[:, None, None]) * (width // size) + inner % (width // size)
    return rows.reshape(width, 1)


def body(
    patches, segment_ids, mask_slots, gain_attn, qkv_weight, out_weight, gain_mlp, up_weight, down_weight,
    embed_weight, mask_token, pred_gain_attn, pred_qkv, pred_out, pred_gain_mlp, pred_up, pred_down, cotangent,
):
    me = lax.axis_index("mp")
    side = lax.axis_index("dp") % 2
    dp_size = lax.axis_size("dp")
    length, width = patches.shape[1:]
    channels = cotangent.shape[2]
    cols, hid = qkv_weight.shape[2], up_weight.shape[1]
    p_cols, p_hid = pred_qkv.shape[2], pred_up.shape[1]
    heads = SHARDS * cols // HEAD_DIM
    p_heads = SHARDS * p_cols // P_HEAD_DIM
    pos = jnp.stack([me, side, width // dp_size, channels // dp_size]).astype(jnp.int32)

    attn_own, attn_direct = call(
        pack_attn_kernel, [((4 * cols, width), BF), ((2 * cols, width), BF)],
        (pos, jnp.swapaxes(qkv_weight, 1, 2), out_weight), 1,
    )
    up_direct, down_direct, p_own = call(
        pack_rest_kernel,
        [((width, hid // 2), BF), ((hid // 2, width), BF), ((6 * p_cols + channels + p_hid, channels), BF)],
        (pos, up_weight, down_weight, jnp.swapaxes(pred_qkv, 1, 2), pred_out, embed_weight.T, pred_up, pred_down), 3,
        tokens=(attn_direct,),
    )

    attn_core, up_core, down_core = swap(attn_own, "mp", 1), swap(up_weight, "mp", 1), swap(down_weight, "mp", 1)
    p_core = swap(p_own, "mp", 1)
    attn_x = swap(attn_direct, "mp", 2)
    attn_x, up_direct = gate([attn_x, up_direct], [p_own])
    up_x = swap(up_direct, "mp", 2)
    attn_y = swap(attn_x, "dp", 1)
    (down_direct,) = gate([down_direct], [up_x])
    down_x = swap(down_direct, "mp", 2)
    up_y = swap(up_x, "dp", 1)
    (p_send,) = gate([p_own], [down_x])
    p_x = swap(p_send, "mp", 2)
    attn = (attn_own, attn_core, attn_x, attn_y, swap(attn_x, "mp", 1), swap(attn_y, "mp", 1))

    x = pick(patches, me)
    segments = pick(segment_ids, me)
    seg_row, seg_col = segments[None, :], segments[:, None]
    slots = pick(mask_slots, me)
    masked = jnp.any(jnp.arange(length, dtype=jnp.int32)[:, None] == slots[None, :], -1, keepdims=True).astype(F32)
    cot = pick(cotangent, me)
    row = lambda gain: gain.astype(F32)[None, :]
    rows_at, p_rows_at = source_rows(width), source_rows(channels)
    n_rows, n_small = width // dp_size, channels // dp_size

    middle, qkv, probs, mixed = call(
        enc_attn_kernel,
        [((length, width), F32), ((3 * width, length), BF), ((heads, length, length), BF), ((width, length), BF)],
        (pos, x, seg_row, seg_col, row(gain_attn)) + attn, 9,
        [((2, 4 * cols, width), BF)],
    )
    (up_y,) = gate([up_y], [middle])
    up = (up_weight, up_core, up_x, up_y, swap(up_x, "mp", 1), swap(up_y, "mp", 1))
    down_y = swap(down_x, "dp", 1)
    hidden, slope = call(
        enc_up_forward_kernel, [((length, SHARDS * hid), BF), ((length, SHARDS * hid), BF)],
        (pos, middle, row(gain_mlp)) + up, 6,
    )
    (down_y,) = gate([down_y], [hidden])
    down = (down_weight, down_core, down_x, down_y, swap(down_x, "mp", 1), swap(down_y, "mp", 1))
    (enc,) = call(enc_down_forward_kernel, [((length, width), BF)], (pos, middle, hidden) + down, 4)
    (p_x,) = gate([p_x], [enc])
    p_packs = (p_send, p_core, p_x, swap(p_x, "mp", 1))
    p_seg, d_seg = Segments(channels, 4 * p_cols + 2 * p_hid), Segments(width, hid)
    u_seg, a_seg = Segments(width, hid), Segments(width, 4 * cols + 128)
    p_blocks, x_blocks = channels // 128, width // 128
    predicted, stats, p_mine, p_theirs, d_embedded, d_enc, p_d_gains = call(
        pred_kernel,
        [((p_blocks * length, 128), BF), ((8, channels), F32), (p_seg.shape, BF), (p_seg.shape, BF), ((length, channels), BF),
         ((length, width), F32), ((8, channels), F32)],
        (pos, enc, seg_row, seg_col, masked, row(mask_token), row(pred_gain_attn), row(pred_gain_mlp), cot, p_rows_at)
        + p_packs, 30,
        [((3 * channels, channels), BF), ((channels, channels), BF), ((channels, width), BF),
         ((channels, SHARDS * p_hid), BF), ((SHARDS * p_hid, channels), BF), ((3 * channels, length), BF),
         ((p_heads, length, length), BF), ((channels, length), BF), ((channels, length), BF),
         ((3 * channels, length), BF)],
    )

    p_cuts = [(0, p_cols, 3, False), (3 * p_cols, p_cols, 1, False), (4 * p_cols, p_hid, 1, False), (4 * p_cols + p_hid, p_hid, 1, False)]
    d_cuts, u_cuts = [(0, hid, 1, False)], [(0, hid, 1, False)]
    a_cuts = [(0, cols, 3, False), (3 * cols, cols, 1, True), (4 * cols, p_cols, 1, False), (4 * cols + p_cols, 128 - p_cols, 1, True)]
    small = dp_size == 8

    def sums_of(pieces, tokens, micros, sums=()):
        outs = [segments for segments, _, _ in pieces]
        if small:
            cuts = [(seg.eighth, cut) for _, seg, cut in pieces]
            return combine(outs, tokens, micros, sums, kind=F32, cuts=cuts)
        totals = combine(outs, tokens, micros, sums, kind=F32)
        groups = [[high * 8 + low for high in range(dp_size // 8)] for low in range(8)]
        results = []
        for total, (_, seg, cut) in zip(totals, pieces):
            total = total.reshape(seg.left + seg.right, -1, 128)
            total = lax.psum_scatter(total, "dp", scatter_dimension=1, axis_index_groups=groups, tiled=True)
            results += finals(jnp.swapaxes(total, 0, 1).reshape(total.shape[1], -1), cut)
        return results + list(totals[len(pieces) :])

    def from_core(theirs):
        return [swap(part, "mp", 1) for part in theirs]

    def both(own, at, size):
        mine, away = own
        segments, start = [], 0
        for part in away:
            low, high = max(at, start), min(at + size, start + part.shape[0])
            if low < high:
                segments.append([(mine, low, high - low), (part, low - start, high - low)])
            start += part.shape[0]
        return segments

    def with_term(segments, array, at):
        result = []
        for parts in segments:
            result.append(parts + [(array, at, parts[0][2])])
            at += parts[0][2]
        return result

    def first(own, seg):
        return both(own, *seg.over_x), both(own, *seg.over_y)

    def second(own, seg, got):
        (x, x_at), (y, y_at) = got
        return with_term(both(own, *seg.then_x), y, y_at + seg.b), with_term(both(own, *seg.then_y), x, x_at + seg.a)

    def kept(own, seg, got, then, low, high, extra=()):
        segments = []
        for (start, size), over, after, right in (
            (seg.keep_left, got[0], then[1], 0), (seg.keep_right, got[1], then[0], 1)
        ):
            at, rows = low * size // 4, (high - low) * size // 4
            part = both(own, start + at, rows)
            for array, array_at in (over, after):
                part = with_term(part, array, array_at + at)
            for array, array_at in extra:
                part = with_term(part, array, array_at + right * seg.a * (high - low) // 4)
            segments += part
        return segments

    def stage(parts, tokens, micros, sums=(), z=()):
        outs = [sum((x for x, _ in parts), []), sum((y for _, y in parts), [])] if parts else []
        send = combine(outs + list(z), tokens, micros, sums)
        got, at = ((swap(send[0], "mp", 2), swap(send[1], "dp", 1)) if parts else ()), [0, 0]
        places = []
        for x, y in parts:
            places.append(((got[0], at[0]), (got[1], at[1])))
            at = [at[0] + sum(p[0][2] for p in x), at[1] + sum(p[0][2] for p in y)]
        return send, got, places

    p_away = swap(p_theirs, "mp", 1)
    d_theirs = call(partial(enc_down_kernel, 1), d_seg.parts(), (pos, rows_at, d_enc, hidden), 30)
    (d_mine,) = call(partial(enc_down_kernel, 0), [(d_seg.shape, BF)], (pos, rows_at, d_enc, hidden), 30, tokens=d_theirs[:1])
    p_own, d_own = (p_mine, [p_away]), (d_mine, from_core(d_theirs))
    send, p_arrived, (p_got, d_got, at_predicted) = stage(
        [first(p_own, p_seg), first(d_own, d_seg), ([[(predicted, 0, predicted.shape[0])]], [])], [], 30
    )
    grad_mid, d_gain_two, u_mine, *u_theirs = call(
        enc_up_kernel,
        [((length, width), F32), ((1, width), F32), (u_seg.shape, BF)] + u_seg.parts(),
        (pos, rows_at, d_enc, middle, row(gain_mlp), slope) + up + down, 100, tokens=send,
    )
    u_away = from_core(u_theirs)
    d_qkv, d_input, d_gain_one = call(
        enc_attn_back_kernel,
        [((3 * width, length), BF), ((x_blocks * length, 128), BF), ((1, width), F32)],
        (pos, x, row(gain_attn), grad_mid, qkv, probs) + attn, 1,
        [((2, 4 * cols, width), BF), ((width, length), BF)],
    )
    got_x, got_y, *u_away[:2] = gate([*p_arrived, *u_away[:2]], [d_gain_one])
    moved = lambda places: ((got_x, places[0][1]), (got_y, places[1][1]))
    p_got, d_got, u_own = moved(p_got), moved(d_got), (u_mine, u_away)
    predicted_x = lax.slice_in_dim(got_x, at_predicted[0][1], got_x.shape[0])
    filler = [[(d_input, 0, p_seg.b - p_seg.a)]]
    send, _, (u_got, d_then, p_then, _) = stage(
        [first(u_own, u_seg), second(d_own, d_seg, d_got), second(p_own, p_seg, p_got), ([], filler)], [], 30
    )
    predicted, predicted_x, d_input = gate([predicted, predicted_x, d_input], send)
    a_mine, *a_theirs = call(
        enc_attn_weights_kernel, [(a_seg.shape, BF)] + a_seg.parts(),
        (pos, rows_at, x, row(gain_attn), grad_mid, mixed, d_qkv, d_embedded, enc, d_gain_one, d_gain_two, p_d_gains), 100, tokens=send,
    )
    a_own = (a_mine, from_core(a_theirs))
    a_send, _, (a_got,) = stage([first(a_own, a_seg)], [], 0)
    p_z = (p_own, p_seg, p_got, p_then)
    d_z = (d_own, d_seg, d_got, d_then)
    (*u_send, z_send), _, (u_then,) = stage(
        [second(u_own, u_seg, u_got)], a_send, 12, (), [kept(*p_z, 2, 4) + kept(*d_z, 2, 4)]
    )
    (stats,) = gate([stats], u_send)
    u_z = (u_own, u_seg, u_got, u_then)
    stats_got, z_got = swap(stats, "mp", 1), swap(z_send, "dp", 2)
    p_rows, d_rows, u_rows = ((seg.a + seg.b) // 4 for seg in (p_seg, d_seg, u_seg))
    p_one, d_one = (z_got, 0), (z_got, 2 * p_rows)

    def later(one, seg, quarter):
        array, at = one
        return [(array, at + quarter * seg.a // 4), (array, at + seg.a // 2 + quarter * seg.b // 4)]

    def last(z, one, quarter, two=None):
        own, seg, got, then = z
        segments = []
        lefts_rights = later(one, seg, quarter)
        for part, (start, size), over, after, (array, at), shift in (
            (0, seg.keep_left, got[0], then[1], lefts_rights[0], 0), (1, seg.keep_right, got[1], then[0], lefts_rights[1], seg.a // 4)
        ):
            begin, rows = quarter * size // 4, size // 4
            terms = both(own, start + begin, rows)
            for more, more_at in (over, after):
                terms = with_term(terms, more, more_at + begin)
            terms = with_term(terms, array, at)
            if two is not None:
                terms = with_term(terms, two[0], two[1] + shift)
            segments += terms
        return segments

    filler = [[(a_got[0][0], 0, a_seg.b - a_seg.a)]]
    (*a_send, z_send, stats), _, (a_then, _) = stage(
        [second(a_own, a_seg, a_got), ([], filler)], u_send, 12, (stats, stats_got), [last(p_z, p_one, 1) + last(d_z, d_one, 1)]
    )
    a_z = (a_own, a_seg, a_got, a_then)
    z_got = swap(z_send, "dp", 4)
    (z_send,) = combine([kept(*u_z, 2, 4)], a_send, 3)
    u_one, stats_got = (swap(z_send, "dp", 2), 0), swap(stats, "dp", 2)
    predicted, predicted_x = gate([predicted, predicted_x], [z_send])
    predicted_c, predicted_xc = swap(predicted, "mp", 1), swap(predicted_x, "mp", 1)
    (z_send,) = combine([kept(*a_z, 2, 4)], [z_send], 3)
    (z_send_u,) = combine([last(u_z, u_one, 1)], [z_send], 3)
    a_one, u_two = (swap(z_send, "dp", 2), 0), (swap(z_send_u, "dp", 4), 0)
    d_input, p_two_array = gate([d_input, z_got], [z_send])
    p_two, d_two = (p_two_array, 0), (p_two_array, p_rows)
    input_x, input_c = swap(d_input, "mp", 2), swap(d_input, "mp", 1)
    *p_results, r_down, stats = sums_of(
        [(last(p_z, p_one, 0, p_two), p_seg, p_cuts), (last(d_z, d_one, 0, d_two), d_seg, d_cuts)], [z_send], 3,
        (stats, stats_got),
    )
    stats_got = swap(stats, "dp", 4)
    z_send, stats = combine([last(a_z, a_one, 1)], [p_results[1]], 3, (stats, stats_got))
    a_two = (swap(z_send, "dp", 4), 0)
    (input_x,) = gate([input_x], [z_send])
    r_up, stats = sums_of([(last(u_z, u_one, 0, u_two), u_seg, u_cuts)], [z_send], 3, (stats, swap(stats, "mp", 2)))
    stats_got = swap(stats, "dp", 1)
    (predictions,) = call(
        in_order_kernel, [((SHARDS, length, channels), BF)], (pos, predicted, predicted_c, predicted_x, predicted_xc), 3,
        tokens=(r_up,),
    )
    (patches_grad,) = call(
        in_order_kernel, [((SHARDS, length, width), BF)], (pos, d_input, input_c, input_x, swap(input_x, "mp", 1)), 2,
        tokens=(predictions,),
    )
    *a_results, stats = sums_of([(last(a_z, a_one, 0, a_two), a_seg, a_cuts)], [patches_grad], 3, (stats, stats_got))
    for at in range(3, dp_size.bit_length() - 1):
        stats = stats + swap(stats, "dp", 1 << at)

    count = dp_size * patches.shape[0] * length
    mean, square = stats[0] / count, stats[1] / count
    n_var = channels // SHARDS
    variance = lax.dynamic_slice_in_dim(square - mean * mean, me * n_var, n_var)
    tail = a_results[3]

    return (
        predictions,
        patches_grad,
        variance,
        tail[0],
        a_results[0],
        a_results[1],
        tail[1],
        r_up,
        r_down.T,
        a_results[2],
        tail[4, :n_small],
        tail[2, :n_small],
        p_results[0],
        p_results[1].T,
        tail[3, :n_small],
        p_results[2],
        p_results[3].T,
    )


def solution(mesh):
    placed = (
        P("dp", None, None), P("dp", None), P("dp", None), P(), P(None, None, "mp"), P("mp", None), P(),
        P(None, "mp"), P("mp", None), P(None, "mp"), P(), P(), P(None, None, "mp"), P("mp", None), P(),
        P(None, "mp"), P("mp", None), P("dp", None, None),
    )
    return jax.shard_map(
        body,
        mesh=mesh,
        in_specs=placed,
        out_specs=(
            P("dp", None, None), P("dp", None, None), P("mp"), P("dp"), P(None, "dp", "mp"), P("mp", "dp"),
            P("dp"), P("dp", "mp"), P("mp", "dp"), P("dp", "mp"), P("dp"), P("dp"), P(None, "dp", "mp"),
            P("mp", "dp"), P("dp"), P("dp", "mp"), P("mp", "dp"),
        ),
        check_vma=False,
    )
```
